32 devices in a mesh: facet: 4 (over x, core), sub: 4 (over z), wa: 2 (over y).
Axes of the slice: x: 2, y: 2, z: 4, core: 2. Of those that a mesh axis runs over, the one named last changes fastest.
Arguments:
- facets: float32 [4, 128, 2, 4096], P('facet'), may hold values from -6 to 6
- correction: float32 [4, 4096], P('facet'), may hold values from 0.5 to 2
- window: float32 [128], replicated, may hold values from 0.25 to 1
- offsets: int32 [8], replicated, may hold values from 0 to 4095
- phases: float32 [4, 512], P('wa'), may hold values from -3.140625 to 3.140625
- coverage: int32 [8, 4, 512], P('sub', 'wa'), may hold values from 0 to 3
Outputs:
- facets_out: float32 [4, 128, 2, 4096], P('facet', ('sub', 'wa'))
The draws below stay inside these ranges and needn't reach their ends.
All inputs are finite; a program needn't handle non-finite values.
Results may differ from the reference program's by a relative error of at most 0.0001.
Values sent between devices are 32-bit elements; how exact they have to be, the bound alone decides.
A program may use at most 192 MiB of HBM per device.

```python
import math
import jax
import jax.numpy as jnp

YN = 4096
CM = 128
WPLANES = 4
FACETS = 4
ROWS = 128
SUBS = 8
XM = 512


def with_ends(drawn, own_key, least, high):
    longest = drawn.shape.index(max(drawn.shape))
    spots = []
    for shift in (0, 1):
        where = [jax.random.randint(jax.random.fold_in(own_key, axis), (), 0, length) for axis, length in enumerate(drawn.shape)]
        where[longest] = (where[longest] + shift) % drawn.shape[longest]
        spots.append(tuple(where))
    return drawn.at[spots[0]].set(least).at[spots[1]].set(high)


def shard_levels(stream_key, extent, cuts, least, largest):
    def one(dim, shards_of):
        steps = jax.random.uniform(jax.random.fold_in(jax.random.fold_in(stream_key, 6), dim), (shards_of,), jnp.float32, least / len(cuts), largest / len(cuts))
        return jnp.repeat(jnp.exp(steps), extent[dim] // shards_of).reshape((-1,) + (1,) * (len(extent) - dim - 1))

    factor_of = one(*cuts[0])
    for cut in cuts[1:]:
        factor_of = factor_of * one(*cut)
    return factor_of


def bell_draw(rng, shape, spread, reach, pieces=(), kind=jnp.bfloat16):
    values = jax.random.normal(rng, shape, jnp.float32) * spread
    if len(pieces) > 0:
        values = shard_levels(rng, shape, pieces, -0.22, 0.18) * values
    return jnp.clip(values, min=-reach, max=reach).astype(kind)


def setup_inputs(seed: int = 0) -> dict:
    seeds = jax.random.split(jax.random.key(seed), 7)
    facets = bell_draw(seeds[0], (FACETS, ROWS, 2, YN), 1.0, 6.0, ((0, 4),), jnp.float32)
    correction = jnp.clip(jnp.exp(math.log(2.0) - 1.3862944 * jax.random.uniform(seeds[1], (FACETS, YN), jnp.float32) ** shard_levels(seeds[1], (FACETS, YN), ((0, 4),), -0.2, 0.2)), 0.5, 2.0)
    window = jnp.clip(jnp.exp(jax.random.uniform(seeds[2], (CM,), jnp.float32, math.log(0.25), math.log(1.0))), 0.25, 1.0)
    offsets = with_ends(jax.random.randint(seeds[3], (SUBS,), 0, YN), jax.random.fold_in(seeds[3], 1), 0, YN - 1).astype(jnp.int32)
    phases = jnp.clip(jax.random.uniform(seeds[4], (WPLANES, XM), jnp.float32, -3.140625, 3.140625), -3.140625, 3.140625)
    coverage = with_ends(jax.random.randint(seeds[5], (SUBS, WPLANES, XM), 0, 4), jax.random.fold_in(seeds[5], 1), 0, 3).astype(jnp.int32)
    return dict(facets=facets, correction=correction, window=window, offsets=offsets, phases=phases, coverage=coverage)


def reference(facets, correction, window, offsets, phases, coverage):
    pixels = (facets[:, :, 0, :] + 1j * facets[:, :, 1, :]) * correction[:, None, :]
    spectrum = jnp.fft.fft(pixels, axis=-1, norm="ortho")
    positions = (offsets[:, None] + jnp.arange(CM, dtype=jnp.int32)[None, :]) % YN
    segments = spectrum[:, :, positions] * window
    blocks = jnp.fft.ifft(segments, axis=-1, norm="ortho")
    subgrid = jnp.transpose(blocks, (1, 2, 0, 3)).reshape(ROWS, SUBS, XM)
    adjoint = jnp.zeros_like(subgrid)
    for wplane in range(WPLANES):
        kernel = jnp.exp(1j * phases[wplane])
        grid_values = jnp.fft.fft(kernel * subgrid, axis=-1, norm="ortho")
        weighted = grid_values * coverage[:, wplane, :].astype(jnp.float32)
        adjoint = adjoint + jnp.conj(kernel) * jnp.fft.ifft(weighted, axis=-1, norm="ortho")
    adjoint = adjoint / WPLANES
    returned = jnp.transpose(adjoint.reshape(ROWS, SUBS, FACETS, CM), (2, 0, 1, 3))
    back_segments = jnp.fft.fft(returned, axis=-1, norm="ortho") * window
    accumulated = jnp.zeros((FACETS, ROWS, YN), back_segments.dtype).at[:, :, positions].add(back_segments)
    result = jnp.fft.ifft(accumulated, axis=-1, norm="ortho") * correction[:, None, :]
    return jnp.stack([jnp.real(result), jnp.imag(result)], axis=2).astype(jnp.float32)
```

```python
import functools
import math

import jax
import jax.numpy as jnp
import numpy as np
from jax import lax
from jax.experimental import pallas as pl
from jax.experimental.pallas import tpu as pltpu
from jax.sharding import PartitionSpec as P

MESH = pl.DeviceIdType.MESH
F32 = jnp.float32
BF16 = jnp.bfloat16


def complex_rows(matrix):
    return np.block([[matrix.real, matrix.imag], [-matrix.imag, matrix.real]])


def tables(length, width, facet_count):
    low = length // width
    quads = width // low
    a = np.arange(width)
    b = np.arange(low)
    dft = np.exp(-2j * np.pi * np.outer(a, a) / width)
    order = (a.reshape(width // quads, quads).T).reshape(-1)
    picked = dft[:, order]
    spread = np.zeros((2, width, width, 2))
    spread[0, :, :, 0] = picked.real
    spread[0, :, :, 1] = -picked.imag
    spread[1, :, :, 0] = picked.imag
    spread[1, :, :, 1] = picked.real
    outer = spread.reshape(2 * width, 2 * width)
    turn = np.tile(np.exp(-2j * np.pi * np.outer(a, b) / length), (1, quads))
    turn = np.stack([turn.real, turn.imag]).astype(np.float32)
    fine = np.exp(-2j * np.pi * np.outer(b, b) / low) * length**-0.5
    pick = np.zeros((low, 2, quads, 2, quads, low))
    for quad in range(quads):
        pick[:, 0, quad, 0, quad] = fine.real
        pick[:, 0, quad, 1, quad] = -fine.imag
        pick[:, 1, quad, 0, quad] = fine.imag
        pick[:, 1, quad, 1, quad] = fine.real
    pick = pick.reshape(low, 2 * quads, 2 * width).astype(np.float32)
    unit = complex_rows(np.conj(dft) * width**-0.5)
    twist = np.exp(-2j * np.pi * np.outer(np.arange(facet_count), a) / (facet_count * width))
    twist = np.stack([twist.real, twist.imag]).astype(np.float32)
    outer, unit = outer.astype(np.float32), unit.astype(np.float32)
    return outer, outer.T, turn, pick, unit, unit.T, twist


def split(value):
    high = value.astype(BF16)
    return high, (value - high.astype(F32)).astype(BF16)


def mm(left, right, transposed=False):
    dims = (((1,), (1 if transposed else 0,)), ((), ()))
    dot = functools.partial(lax.dot_general, dimension_numbers=dims, preferred_element_type=F32)
    return dot(left[0], right[0]) + (dot(left[0], right[1]) + dot(left[1], right[0]))


def radix(parts, sign):
    count = len(parts)
    if count == 1:
        return parts
    if count % 2:
        raise ValueError("odd length")
    even = radix(parts[0::2], sign)
    odd = radix(parts[1::2], sign)
    first, second = [], []
    for k in range(count // 2):
        real, imag = odd[k]
        if 4 * k == count:
            real, imag = (-imag, real) if sign > 0 else (imag, -real)
        elif k:
            c = math.cos(2 * math.pi * k / count)
            s = sign * math.sin(2 * math.pi * k / count)
            real, imag = real * c - imag * s, real * s + imag * c
        first.append((even[k][0] + real, even[k][1] + imag))
        second.append((even[k][0] - real, even[k][1] - imag))
    return first + second


def swap_blocks(blocks, low):
    quads = len(blocks)
    group = lax.broadcasted_iota(jnp.int32, blocks[0].shape, 1) // low
    width = quads * low
    out = []
    for i in range(quads):
        total = None
        for j in range(quads):
            shift = ((j - i) * low) % width
            moved = pltpu.roll(blocks[j], shift, 1) if shift else blocks[j]
            total = moved if total is None else jnp.where(group == j, moved, total)
        out.append(total)
    return out


def kernel(
    geometry,
    offsets_ref,
    facets_ref,
    correction_ref,
    window_ref,
    phases_ref,
    coverage_ref,
    outer_ref,
    outer_t_ref,
    turn_ref,
    pick_ref,
    unit_ref,
    unit_t_ref,
    twist_ref,
    out_ref,
    image,
    gain,
    cut,
    sent,
    arrived,
    back,
    returned,
    segments,
    counts,
    expanded,
    screens,
    load_sem,
    fwd_send,
    fwd_recv,
    bwd_send,
    bwd_recv,
    cov_send,
    cov_recv,
    ph_send,
    ph_recv,
):
    facet_count, sub_count, pair_count = geometry
    facet = lax.axis_index("facet")
    sub = lax.axis_index("sub")
    pair = lax.axis_index("wa")
    rows = image.shape[0]
    width = window_ref.shape[1]
    subs = offsets_ref.shape[0]
    low = pick_ref.shape[0]
    quads = width // low
    length = low * width
    span = subs * quads
    per_sub, per_wa = coverage_ref.shape[0], coverage_ref.shape[1]
    planes = per_wa * pair_count
    total = facet_count * width

    unit, unit_t = split(unit_ref[...]), split(unit_t_ref[...])

    facet_mates = [lax.rem(facet + d, facet_count) for d in range(1, facet_count)]
    hops = [(ds, dw) for ds in range(sub_count) for dw in range(pair_count) if ds or dw]
    barrier = pltpu.get_barrier_semaphore()
    for mate in facet_mates:
        pl.semaphore_signal(barrier, inc=1, device_id={"facet": mate}, device_id_type=MESH)
    grid_mates = [(lax.rem(sub + ds, sub_count), lax.rem(pair + dw, pair_count)) for ds, dw in hops]
    for mate_sub, mate_pair in grid_mates:
        pl.semaphore_signal(
            barrier, inc=1, device_id={"sub": mate_sub, "wa": mate_pair}, device_id_type=MESH
        )
    load = pltpu.make_async_copy(
        facets_ref.at[pl.ds((sub * pair_count + pair) * rows, rows)], image, load_sem
    )
    load.start()

    gain[pl.ds(0, low, stride=2), :] = correction_ref[...]
    gain[pl.ds(1, low, stride=2), :] = correction_ref[...]
    lane = lax.broadcasted_iota(jnp.int32, (1, width), 1)
    starts = [offsets_ref[s] for s in range(subs)]
    first_q = [start // width for start in starts]
    rests = [start - q * width for start, q in zip(starts, first_q)]
    rows_of = lax.broadcasted_iota(jnp.int32, (span, width), 0) // quads
    offset_rows = jnp.zeros((span, width), jnp.int32)
    for s in range(subs):
        offset_rows = jnp.where(rows_of == s, rests[s], offset_rows)
    span_lane = lax.broadcasted_iota(jnp.int32, (span, width), 1)
    angle = lax.rem(offset_rows * span_lane, width).astype(F32) * (2.0 * math.pi / width)
    turn_cos, turn_sin = jnp.cos(angle), jnp.sin(angle)
    is_first = span_lane >= offset_rows
    window_full = jnp.broadcast_to(window_ref[...], (8, width))
    window_rows = jnp.zeros((span, width), F32)
    for s in range(subs):
        moved = pltpu.roll(window_full, rests[s], 1)[0:1]
        window_rows = jnp.where(rows_of == s, moved, window_rows)
    picked = []
    for s in range(subs):
        picked.append(pick_ref[first_q[s]])
        picked.append(pick_ref[lax.rem(first_q[s] + 1, low)])
    picked = split(jnp.concatenate(picked, axis=0))

    load.wait()
    gains = gain[...]
    groups = []
    for g in range(facet_count):
        blocks = [image[g * quads + i] * gains for i in range(quads)]
        groups.append(jnp.concatenate(swap_blocks(blocks, low), axis=0))
    spread = jnp.concatenate(groups, axis=1)
    mixed = mm(split(outer_ref[...]), split(spread))
    table_cos, table_sin = turn_ref[0], turn_ref[1]
    turned = []
    for g in range(facet_count):
        real = mixed[:width, g * width : (g + 1) * width]
        imag = mixed[width:, g * width : (g + 1) * width]
        turned.append(
            jnp.concatenate(
                [real * table_cos - imag * table_sin, real * table_sin + imag * table_cos], axis=1
            )
        )
    turned = jnp.concatenate(turned, axis=0)
    spectrum = mm(picked, split(turned), transposed=True)

    pl.semaphore_wait(barrier, len(facet_mates) + len(hops))
    copies = []
    for i, (mate_sub, mate_pair) in enumerate(grid_mates):
        copy = pltpu.make_async_remote_copy(
            src_ref=coverage_ref,
            dst_ref=counts.at[sub, pair],
            send_sem=cov_send.at[i],
            recv_sem=cov_recv.at[i],
            device_id={"sub": mate_sub, "wa": mate_pair},
            device_id_type=MESH,
        )
        copy.start()
        copies.append(copy)
    counts[sub, pair] = coverage_ref[...]
    for d in range(1, pair_count):
        copy = pltpu.make_async_remote_copy(
            src_ref=phases_ref,
            dst_ref=screens.at[pair],
            send_sem=ph_send.at[d - 1],
            recv_sem=ph_recv.at[d - 1],
            device_id={"wa": lax.rem(pair + d, pair_count)},
            device_id_type=MESH,
        )
        copy.start()
        copies.append(copy)
    screens[pair] = phases_ref[...]

    for s in range(subs):
        here = slice(s * quads, (s + 1) * quads)
        base = s * 4 * quads
        keep = is_first[here]
        win = window_rows[here]
        for g in range(facet_count):
            cols = slice(g * width, (g + 1) * width)
            for c in range(2):
                one = spectrum[base + c * quads : base + (c + 1) * quads, cols]
                two = spectrum[base + (2 + c) * quads : base + (3 + c) * quads, cols]
                cut[g, here, c * width : (c + 1) * width] = jnp.where(keep, one, two) * win
    mixed = mm(split(cut[...].reshape(facet_count * span, 2 * width)), unit)
    for g in range(facet_count):
        real = mixed[g * span : (g + 1) * span, :width]
        imag = mixed[g * span : (g + 1) * span, width:]
        sent[g, :, :width] = real * turn_cos + imag * turn_sin
        sent[g, :, width:] = imag * turn_cos - real * turn_sin
    forward = []
    for i, mate in enumerate(facet_mates):
        copy = pltpu.make_async_remote_copy(
            src_ref=sent.at[mate],
            dst_ref=arrived.at[facet],
            send_sem=fwd_send.at[i],
            recv_sem=fwd_recv.at[i],
            device_id={"facet": mate},
            device_id_type=MESH,
        )
        copy.start()
        forward.append(copy)
    arrived[facet] = sent[facet]

    for copy in copies:
        copy.wait()
    for owner in range(sub_count):
        for p in range(pair_count):
            for i in range(per_sub):
                for j in range(per_wa):
                    at = (p * per_wa + j) * span + (owner * per_sub + i) * quads
                    row = counts[owner, p, i, j : j + 1].astype(F32)
                    expanded[at : at + quads, :] = jnp.broadcast_to(row, (quads, total))
    source = lax.broadcasted_iota(jnp.int32, (total, total), 0)
    target = lax.broadcasted_iota(jnp.int32, (total, total), 1)
    wanted = lax.rem(target, width) * facet_count + target // width
    chooser = jnp.where(source == wanted, 1.0, 0.0).astype(BF16)
    weights = jnp.dot(expanded[...].astype(BF16), chooser, preferred_element_type=F32)
    weights = weights * (1.0 / (facet_count * planes))
    kernels = []
    for p in range(pair_count):
        screen = screens[p]
        cos_all, sin_all = jnp.cos(screen), jnp.sin(screen)
        for j in range(per_wa):
            kernels.append((cos_all[j : j + 1], sin_all[j : j + 1]))
    twist = [(twist_ref[0, k : k + 1], twist_ref[1, k : k + 1]) for k in range(facet_count)]

    for copy in forward:
        copy.wait()
    pieces = [[] for _ in range(facet_count)]
    for w in range(planes):
        parts = []
        for f in range(facet_count):
            cols = slice(f * width, (f + 1) * width)
            kc, ks = kernels[w][0][:, cols], kernels[w][1][:, cols]
            real, imag = arrived[f, :, :width], arrived[f, :, width:]
            parts.append((real * kc - imag * ks, real * ks + imag * kc))
        for k, (real, imag) in enumerate(radix(parts, -1)):
            tc, ts = twist[k]
            pieces[k].append(
                jnp.concatenate([real * tc - imag * ts, real * ts + imag * tc], axis=1)
            )
    stacked = jnp.concatenate([piece for group in pieces for piece in group], axis=0)
    grid = mm(split(stacked), unit_t)
    scale = jnp.concatenate(
        [weights[:, k * width : (k + 1) * width] for k in range(facet_count)], axis=0
    )
    weighted = grid * jnp.concatenate([scale, scale], axis=1)
    image_side = mm(split(weighted), unit)
    sums = [None] * facet_count
    for w in range(planes):
        parts = []
        for k in range(facet_count):
            at = (k * planes + w) * span
            real = image_side[at : at + span, :width]
            imag = image_side[at : at + span, width:]
            tc, ts = twist[k]
            parts.append((real * tc + imag * ts, imag * tc - real * ts))
        for f, (real, imag) in enumerate(radix(parts, 1)):
            cols = slice(f * width, (f + 1) * width)
            kc, ks = kernels[w][0][:, cols], kernels[w][1][:, cols]
            term = (real * kc + imag * ks, imag * kc - real * ks)
            sums[f] = term if w == 0 else (sums[f][0] + term[0], sums[f][1] + term[1])
    for f in range(facet_count):
        back[f, :, :width] = sums[f][0]
        back[f, :, width:] = sums[f][1]
    backward = []
    for i, mate in enumerate(facet_mates):
        copy = pltpu.make_async_remote_copy(
            src_ref=back.at[mate],
            dst_ref=returned.at[facet],
            send_sem=bwd_send.at[i],
            recv_sem=bwd_recv.at[i],
            device_id={"facet": mate},
            device_id_type=MESH,
        )
        copy.start()
        backward.append(copy)
    returned[facet] = back[facet]
    for copy in backward:
        copy.wait()

    unturned = []
    for g in range(facet_count):
        real, imag = returned[g, :, :width], returned[g, :, width:]
        unturned.append(
            jnp.concatenate(
                [real * turn_cos - imag * turn_sin, real * turn_sin + imag * turn_cos], axis=1
            )
        )
    unturned = jnp.concatenate(unturned, axis=0)
    mixed = mm(split(unturned), unit_t)
    win_first = jnp.where(is_first, window_rows, 0.0)
    win_second = jnp.where(is_first, 0.0, window_rows)
    for g in range(facet_count):
        cols = slice(g * width, (g + 1) * width)
        for c in range(2):
            part = mixed[g * span : (g + 1) * span, c * width : (c + 1) * width]
            for h, win in enumerate((win_first, win_second)):
                masked = part * win
                for s in range(subs):
                    at = (4 * s + 2 * h + c) * quads
                    segments[at : at + quads, cols] = masked[s * quads : (s + 1) * quads]
    columns = jnp.concatenate(
        [segments[:, g * width : (g + 1) * width].T for g in range(facet_count)], axis=0
    )
    fine = mm(split(columns), picked)
    reals, imags = [], []
    for g in range(facet_count):
        real = fine[g * width : (g + 1) * width, :width]
        imag = fine[g * width : (g + 1) * width, width:]
        reals.append(real * table_cos + imag * table_sin)
        imags.append(imag * table_cos - real * table_sin)
    joined = jnp.concatenate(
        [jnp.concatenate(reals, axis=1), jnp.concatenate(imags, axis=1)], axis=0
    )
    spread = mm(split(outer_t_ref[...]), split(joined))
    part = 2 * width // quads
    for g in range(facet_count):
        cols = slice(g * width, (g + 1) * width)
        blocks = [spread[i * part : (i + 1) * part, cols] for i in range(quads)]
        for i, block in enumerate(swap_blocks(blocks, low)):
            out_ref[g * quads + i] = block * gains


def on_device(facets, correction, window, offsets, phases, coverage):
    facet_count = lax.axis_size("facet")
    sub_count = lax.axis_size("sub")
    pair_count = lax.axis_size("wa")
    row_count, length = facets.shape[1], facets.shape[3]
    width = window.shape[0]
    subs = offsets.shape[0]
    rows = row_count // (sub_count * pair_count)
    low = length // width
    quads = width // low
    if rows != facet_count * quads or low * quads != width:
        raise ValueError("unsupported sizes")
    span = subs * quads
    total = facet_count * width
    lines = length // width
    image = facets.reshape(row_count, 2, lines, width)
    image = jnp.transpose(image, (0, 2, 1, 3)).reshape(row_count, 2 * lines, width)
    constants = tables(length, width, facet_count)
    vmem = pl.BlockSpec(memory_space=pltpu.VMEM)
    others = sub_count * pair_count - 1
    dma = pltpu.SemaphoreType.DMA
    block = (facet_count, span, 2 * width)
    result = pl.pallas_call(
        functools.partial(kernel, (facet_count, sub_count, pair_count)),
        out_shape=jax.ShapeDtypeStruct((rows, 2 * lines, width), F32),
        in_specs=[
            pl.BlockSpec(memory_space=pltpu.SMEM),
            pl.BlockSpec(memory_space=pl.ANY),
        ]
        + [vmem] * (4 + len(constants)),
        out_specs=vmem,
        scratch_shapes=[
            pltpu.VMEM((rows, 2 * lines, width), F32),
            pltpu.VMEM((2 * lines, width), F32),
            pltpu.VMEM(block, F32),
            pltpu.VMEM(block, F32),
            pltpu.VMEM(block, F32),
            pltpu.VMEM(block, F32),
            pltpu.VMEM(block, F32),
            pltpu.VMEM((4 * span, total), F32),
            pltpu.VMEM((sub_count, pair_count) + coverage.shape, jnp.int32),
            pltpu.VMEM((coverage.shape[1] * pair_count * span, total), F32),
            pltpu.VMEM((pair_count,) + phases.shape, F32),
            dma,
            dma((facet_count - 1,)),
            dma((facet_count - 1,)),
            dma((facet_count - 1,)),
            dma((facet_count - 1,)),
            dma((others,)),
            dma((others,)),
            dma((max(pair_count - 1, 1),)),
            dma((max(pair_count - 1, 1),)),
        ],
        compiler_params=pltpu.CompilerParams(
            collective_id=0, has_side_effects=True, vmem_limit_bytes=56 * 1024 * 1024
        ),
    )(
        offsets,
        image,
        correction.reshape(lines, width),
        window.reshape(1, width),
        phases,
        coverage,
        *[jnp.asarray(table) for table in constants],
    )
    result = jnp.transpose(result.reshape(rows, lines, 2, width), (0, 2, 1, 3))
    return result.reshape(1, rows, 2, length)


def solution(mesh):
    return jax.shard_map(
        on_device,
        mesh=mesh,
        in_specs=(
            P("facet", None, None, None),
            P("facet", None),
            P(),
            P(),
            P("wa", None),
            P("sub", "wa", None),
        ),
        out_specs=P("facet", ("sub", "wa"), None, None),
        check_vma=False,
    )
```

```python
import functools
import math

import jax
import jax.numpy as jnp
import numpy as np
from jax import lax
from jax.experimental import pallas as pl
from jax.experimental.pallas import tpu as pltpu
from jax.sharding import PartitionSpec as P

MESH = pl.DeviceIdType.MESH
F32 = jnp.float32
BF16 = jnp.bfloat16


def complex_rows(matrix):
    return np.block([[matrix.real, matrix.imag], [-matrix.imag, matrix.real]])


def tables(length, width, facet_count):
    low = length // width
    quads = width // low
    a = np.arange(width)
    b = np.arange(low)
    dft = np.exp(-2j * np.pi * np.outer(a, a) / width)
    order = (a.reshape(width // quads, quads).T).reshape(-1)
    picked = dft[:, order]
    spread = np.zeros((2, width, width, 2))
    spread[0, :, :, 0] = picked.real
    spread[0, :, :, 1] = -picked.imag
    spread[1, :, :, 0] = picked.imag
    spread[1, :, :, 1] = picked.real
    outer = spread.reshape(2 * width, 2 * width)
    turn = np.tile(np.exp(-2j * np.pi * np.outer(a, b) / length), (1, quads))
    turn = np.stack([turn.real, turn.imag]).astype(np.float32)
    fine = np.exp(-2j * np.pi * np.outer(b, b) / low) * length**-0.5
    pick = np.zeros((low, 2, quads, 2, quads, low))
    for quad in range(quads):
        pick[:, 0, quad, 0, quad] = fine.real
        pick[:, 0, quad, 1, quad] = -fine.imag
        pick[:, 1, quad, 0, quad] = fine.imag
        pick[:, 1, quad, 1, quad] = fine.real
    pick = pick.reshape(low, 2 * quads, 2 * width).astype(np.float32)
    unit = complex_rows(np.conj(dft) * width**-0.5)
    twist = np.exp(-2j * np.pi * np.outer(np.arange(facet_count), a) / (facet_count * width))
    twist = np.stack([twist.real, twist.imag]).astype(np.float32)
    outer, unit = outer.astype(np.float32), unit.astype(np.float32)
    return twist, outer, turn, pick, unit, unit.T, outer.T


def split(value):
    high = value.astype(BF16)
    return high, (value - high.astype(F32)).astype(BF16)


def mm(left, right, transposed=False):
    dims = (((1,), (1 if transposed else 0,)), ((), ()))
    dot = functools.partial(lax.dot_general, dimension_numbers=dims, preferred_element_type=F32)
    return dot(left[0], right[0]) + (dot(left[0], right[1]) + dot(left[1], right[0]))


def cos_sin(value):
    turns = jnp.floor(value * (2.0 / math.pi) + 0.5)
    rest = (value - turns * 1.5703125) - turns * (math.pi / 2 - 1.5703125)
    square = rest * rest
    sine = rest + rest * square * (
        -1.0 / 6 + square * (1.0 / 120 + square * (-1.0 / 5040 + square * (1.0 / 362880)))
    )
    cosine = 1.0 + square * (
        -0.5 + square * (1.0 / 24 + square * (-1.0 / 720 + square * (1.0 / 40320)))
    )
    odd = jnp.abs(turns) == 1.0
    sign_cos = jnp.where(turns == 1.0, -1.0, jnp.where(jnp.abs(turns) == 2.0, -1.0, 1.0))
    sign_sin = jnp.where(turns == -1.0, -1.0, jnp.where(jnp.abs(turns) == 2.0, -1.0, 1.0))
    return jnp.where(odd, sine, cosine) * sign_cos, jnp.where(odd, cosine, sine) * sign_sin


def radix(parts, sign):
    count = len(parts)
    if count == 1:
        return parts
    if count % 2:
        raise ValueError("odd length")
    even = radix(parts[0::2], sign)
    odd = radix(parts[1::2], sign)
    first, second = [], []
    for k in range(count // 2):
        real, imag = odd[k]
        if 4 * k == count:
            real, imag = (-imag, real) if sign > 0 else (imag, -real)
        elif k:
            c = math.cos(2 * math.pi * k / count)
            s = sign * math.sin(2 * math.pi * k / count)
            real, imag = real * c - imag * s, real * s + imag * c
        first.append((even[k][0] + real, even[k][1] + imag))
        second.append((even[k][0] - real, even[k][1] - imag))
    return first + second


def swap_blocks(blocks, low):
    blocks = list(blocks)
    count = len(blocks)
    width = count * low
    lane = lax.broadcasted_iota(jnp.int32, blocks[0].shape, 1)
    step = count // 2
    while step:
        shift = step * low
        upper = (lane & shift) != 0
        for i in range(count):
            if i & step:
                continue
            one, two = blocks[i], blocks[i + step]
            blocks[i] = jnp.where(upper, pltpu.roll(two, shift, 1), one)
            blocks[i + step] = jnp.where(upper, two, pltpu.roll(one, width - shift, 1))
        step //= 2
    return blocks


def kernel(
    geometry,
    offsets_ref,
    facets_ref,
    correction_ref,
    window_ref,
    phases_ref,
    coverage_ref,
    twist_ref,
    outer_far,
    turn_far,
    pick_far,
    unit_far,
    unit_t_far,
    outer_t_far,
    out_ref,
    image,
    gain,
    cut,
    sent,
    arrived,
    back,
    returned,
    segments,
    counts,
    expanded,
    screens,
    load_sem,
    fwd_send,
    fwd_recv,
    bwd_send,
    bwd_recv,
    cov_send,
    cov_recv,
    ph_send,
    ph_recv,
    outer_ref,
    turn_ref,
    pick_ref,
    unit_ref,
    unit_t_ref,
    outer_t_ref,
    table_sem,
):
    facet_count, sub_count, pair_count = geometry
    facet = lax.axis_index("facet")
    sub = lax.axis_index("sub")
    pair = lax.axis_index("wa")
    rows = image.shape[0]
    width = window_ref.shape[1]
    subs = offsets_ref.shape[0]
    low = pick_ref.shape[0]
    quads = width // low
    length = low * width
    span = subs * quads
    per_sub, per_wa = coverage_ref.shape[0], coverage_ref.shape[1]
    planes = per_wa * pair_count
    total = facet_count * width

    facet_mates = [lax.rem(facet + d, facet_count) for d in range(1, facet_count)]
    hops = [(ds, dw) for ds in range(sub_count) for dw in range(pair_count) if ds or dw]
    barrier = pltpu.get_barrier_semaphore()
    for mate in facet_mates:
        pl.semaphore_signal(barrier, inc=1, device_id={"facet": mate}, device_id_type=MESH)
    grid_mates = [(lax.rem(sub + ds, sub_count), lax.rem(pair + dw, pair_count)) for ds, dw in hops]
    for mate_sub, mate_pair in grid_mates:
        pl.semaphore_signal(
            barrier, inc=1, device_id={"sub": mate_sub, "wa": mate_pair}, device_id_type=MESH
        )
    load = pltpu.make_async_copy(
        facets_ref.at[pl.ds((sub * pair_count + pair) * rows, rows)], image, load_sem
    )
    load.start()
    fetches = {}
    for i, (name, far, near) in enumerate(
        (
            ("outer", outer_far, outer_ref),
            ("turn", turn_far, turn_ref),
            ("pick", pick_far, pick_ref),
            ("unit", unit_far, unit_ref),
            ("unit_t", unit_t_far, unit_t_ref),
            ("outer_t", outer_t_far, outer_t_ref),
        )
    ):
        fetches[name] = pltpu.make_async_copy(far, near, table_sem.at[i])
        fetches[name].start()

    gain[pl.ds(0, low, stride=2), :] = correction_ref[...]
    gain[pl.ds(1, low, stride=2), :] = correction_ref[...]
    starts = [offsets_ref[s] for s in range(subs)]
    first_q = [start // width for start in starts]
    rests = [start & (width - 1) for start in starts]
    row = lax.broadcasted_iota(jnp.int32, (span, width), 0)
    offset_rows = jnp.zeros((span, width), jnp.int32)
    for s in range(subs):
        offset_rows = jnp.where(row >= s * quads, rests[s], offset_rows)
    span_lane = lax.broadcasted_iota(jnp.int32, (span, width), 1)
    steps = ((offset_rows * span_lane + width // 2) & (width - 1)) - width // 2
    turn_cos, turn_sin = cos_sin(steps.astype(F32) * (2.0 * math.pi / width))
    is_first = span_lane >= offset_rows
    window_full = jnp.broadcast_to(window_ref[...], (8, width))
    window_rows = jnp.zeros((span, width), F32)
    for s in range(subs):
        moved = pltpu.roll(window_full, rests[s], 1)[0:1]
        window_rows = jnp.where(row >= s * quads, moved, window_rows)
    fetches["pick"].wait()
    picked = []
    for s in range(subs):
        picked.append(pick_ref[first_q[s]])
        picked.append(pick_ref[lax.rem(first_q[s] + 1, low)])
    picked = split(jnp.concatenate(picked, axis=0))

    load.wait()
    gains = gain[...]
    groups = []
    for g in range(facet_count):
        blocks = [image[g * quads + i] * gains for i in range(quads)]
        groups.append(jnp.concatenate(swap_blocks(blocks, low), axis=0))
    spread = jnp.concatenate(groups, axis=1)
    fetches["outer"].wait()
    mixed = mm(split(outer_ref[...]), split(spread))
    fetches["turn"].wait()
    table_cos, table_sin = turn_ref[0], turn_ref[1]
    turned = []
    for g in range(facet_count):
        real = mixed[:width, g * width : (g + 1) * width]
        imag = mixed[width:, g * width : (g + 1) * width]
        turned.append(
            jnp.concatenate(
                [real * table_cos - imag * table_sin, real * table_sin + imag * table_cos], axis=1
            )
        )
    turned = jnp.concatenate(turned, axis=0)
    spectrum = mm(picked, split(turned), transposed=True)

    pl.semaphore_wait(barrier, len(facet_mates) + len(hops))
    copies = []
    for i, (mate_sub, mate_pair) in enumerate(grid_mates):
        copy = pltpu.make_async_remote_copy(
            src_ref=coverage_ref,
            dst_ref=counts.at[sub, pair],
            send_sem=cov_send.at[i],
            recv_sem=cov_recv.at[i],
            device_id={"sub": mate_sub, "wa": mate_pair},
            device_id_type=MESH,
        )
        copy.start()
        copies.append(copy)
    counts[sub, pair] = coverage_ref[...]
    for d in range(1, pair_count):
        copy = pltpu.make_async_remote_copy(
            src_ref=phases_ref,
            dst_ref=screens.at[pair],
            send_sem=ph_send.at[d - 1],
            recv_sem=ph_recv.at[d - 1],
            device_id={"wa": lax.rem(pair + d, pair_count)},
            device_id_type=MESH,
        )
        copy.start()
        copies.append(copy)
    screens[pair] = phases_ref[...]

    for s in range(subs):
        here = slice(s * quads, (s + 1) * quads)
        base = s * 4 * quads
        keep = is_first[here]
        win = window_rows[here]
        for g in range(facet_count):
            cols = slice(g * width, (g + 1) * width)
            for c in range(2):
                one = spectrum[base + c * quads : base + (c + 1) * quads, cols]
                two = spectrum[base + (2 + c) * quads : base + (3 + c) * quads, cols]
                cut[g, here, c * width : (c + 1) * width] = jnp.where(keep, one, two) * win
    fetches["unit"].wait()
    unit = split(unit_ref[...])
    mixed = mm(split(cut[...].reshape(facet_count * span, 2 * width)), unit)
    for g in range(facet_count):
        real = mixed[g * span : (g + 1) * span, :width]
        imag = mixed[g * span : (g + 1) * span, width:]
        sent[g, :, :width] = real * turn_cos + imag * turn_sin
        sent[g, :, width:] = imag * turn_cos - real * turn_sin
    forward = []
    for i, mate in enumerate(facet_mates):
        copy = pltpu.make_async_remote_copy(
            src_ref=sent.at[mate],
            dst_ref=arrived.at[facet],
            send_sem=fwd_send.at[i],
            recv_sem=fwd_recv.at[i],
            device_id={"facet": mate},
            device_id_type=MESH,
        )
        copy.start()
        forward.append(copy)
    arrived[facet] = sent[facet]

    fetches["unit_t"].wait()
    unit_t = split(unit_t_ref[...])
    fetches["outer_t"].wait()

    for copy in copies:
        copy.wait()
    for owner in range(sub_count):
        for p in range(pair_count):
            for i in range(per_sub):
                for j in range(per_wa):
                    at = (p * per_wa + j) * span + (owner * per_sub + i) * quads
                    row = counts[owner, p, i, j : j + 1].astype(F32)
                    expanded[at : at + quads, :] = jnp.broadcast_to(row, (quads, total))
    source = lax.broadcasted_iota(jnp.int32, (total, total), 0)
    inner = lax.broadcasted_iota(jnp.int32, (1, width), 1) * facet_count
    wanted = jnp.concatenate([inner + k for k in range(facet_count)], axis=1)
    chooser = jnp.where(source == wanted, 1.0, 0.0).astype(BF16)
    weights = jnp.dot(expanded[...].astype(BF16), chooser, preferred_element_type=F32)
    weights = weights * (1.0 / (facet_count * planes))
    kernels = []
    for p in range(pair_count):
        screen = screens[p]
        cos_all, sin_all = cos_sin(screen)
        for j in range(per_wa):
            kernels.append((cos_all[j : j + 1], sin_all[j : j + 1]))
    twist = [(twist_ref[0, k : k + 1], twist_ref[1, k : k + 1]) for k in range(facet_count)]

    for copy in forward:
        copy.wait()
    pieces = [[] for _ in range(facet_count)]
    for w in range(planes):
        parts = []
        for f in range(facet_count):
            cols = slice(f * width, (f + 1) * width)
            kc, ks = kernels[w][0][:, cols], kernels[w][1][:, cols]
            real, imag = arrived[f, :, :width], arrived[f, :, width:]
            parts.append((real * kc - imag * ks, real * ks + imag * kc))
        for k, (real, imag) in enumerate(radix(parts, -1)):
            tc, ts = twist[k]
            pieces[k].append(
                jnp.concatenate([real * tc - imag * ts, real * ts + imag * tc], axis=1)
            )
    stacked = jnp.concatenate([piece for group in pieces for piece in group], axis=0)
    grid = mm(split(stacked), unit_t)
    scale = jnp.concatenate(
        [weights[:, k * width : (k + 1) * width] for k in range(facet_count)], axis=0
    )
    weighted = grid * jnp.concatenate([scale, scale], axis=1)
    image_side = mm(split(weighted), unit)
    sums = [None] * facet_count
    for w in range(planes):
        parts = []
        for k in range(facet_count):
            at = (k * planes + w) * span
            real = image_side[at : at + span, :width]
            imag = image_side[at : at + span, width:]
            tc, ts = twist[k]
            parts.append((real * tc + imag * ts, imag * tc - real * ts))
        for f, (real, imag) in enumerate(radix(parts, 1)):
            cols = slice(f * width, (f + 1) * width)
            kc, ks = kernels[w][0][:, cols], kernels[w][1][:, cols]
            term = (real * kc + imag * ks, imag * kc - real * ks)
            sums[f] = term if w == 0 else (sums[f][0] + term[0], sums[f][1] + term[1])
    for f in range(facet_count):
        back[f, :, :width] = sums[f][0]
        back[f, :, width:] = sums[f][1]
    backward = []
    for i, mate in enumerate(facet_mates):
        copy = pltpu.make_async_remote_copy(
            src_ref=back.at[mate],
            dst_ref=returned.at[facet],
            send_sem=bwd_send.at[i],
            recv_sem=bwd_recv.at[i],
            device_id={"facet": mate},
            device_id_type=MESH,
        )
        copy.start()
        backward.append(copy)
    returned[facet] = back[facet]
    for copy in backward:
        copy.wait()

    unturned = []
    for g in range(facet_count):
        real, imag = returned[g, :, :width], returned[g, :, width:]
        unturned.append(
            jnp.concatenate(
                [real * turn_cos - imag * turn_sin, real * turn_sin + imag * turn_cos], axis=1
            )
        )
    unturned = jnp.concatenate(unturned, axis=0)
    mixed = mm(split(unturned), unit_t)
    win_first = jnp.where(is_first, window_rows, 0.0)
    win_second = jnp.where(is_first, 0.0, window_rows)
    for g in range(facet_count):
        cols = slice(g * width, (g + 1) * width)
        for c in range(2):
            part = mixed[g * span : (g + 1) * span, c * width : (c + 1) * width]
            for h, win in enumerate((win_first, win_second)):
                masked = part * win
                for s in range(subs):
                    at = (4 * s + 2 * h + c) * quads
                    segments[at : at + quads, cols] = masked[s * quads : (s + 1) * quads]
    columns = jnp.concatenate(
        [segments[:, g * width : (g + 1) * width].T for g in range(facet_count)], axis=0
    )
    fine = mm(split(columns), picked)
    reals, imags = [], []
    for g in range(facet_count):
        real = fine[g * width : (g + 1) * width, :width]
        imag = fine[g * width : (g + 1) * width, width:]
        reals.append(real * table_cos + imag * table_sin)
        imags.append(imag * table_cos - real * table_sin)
    joined = jnp.concatenate(
        [jnp.concatenate(reals, axis=1), jnp.concatenate(imags, axis=1)], axis=0
    )
    spread = mm(split(outer_t_ref[...]), split(joined))
    part = 2 * width // quads
    for g in range(facet_count):
        cols = slice(g * width, (g + 1) * width)
        blocks = [spread[i * part : (i + 1) * part, cols] for i in range(quads)]
        for i, block in enumerate(swap_blocks(blocks, low)):
            out_ref[g * quads + i] = block * gains


def on_device(facets, correction, window, offsets, phases, coverage):
    facet_count = lax.axis_size("facet")
    sub_count = lax.axis_size("sub")
    pair_count = lax.axis_size("wa")
    row_count, length = facets.shape[1], facets.shape[3]
    width = window.shape[0]
    subs = offsets.shape[0]
    rows = row_count // (sub_count * pair_count)
    low = length // width
    quads = width // low
    if rows != facet_count * quads or low * quads != width:
        raise ValueError("unsupported sizes")
    span = subs * quads
    total = facet_count * width
    lines = length // width
    image = facets.reshape(row_count, 2, lines, width)
    image = jnp.transpose(image, (0, 2, 1, 3)).reshape(row_count, 2 * lines, width)
    constants = tables(length, width, facet_count)
    vmem = pl.BlockSpec(memory_space=pltpu.VMEM)
    others = sub_count * pair_count - 1
    dma = pltpu.SemaphoreType.DMA
    block = (facet_count, span, 2 * width)
    result = pl.pallas_call(
        functools.partial(kernel, (facet_count, sub_count, pair_count)),
        out_shape=jax.ShapeDtypeStruct((rows, 2 * lines, width), F32),
        in_specs=[
            pl.BlockSpec(memory_space=pltpu.SMEM),
            pl.BlockSpec(memory_space=pl.ANY),
        ]
        + [vmem] * 5
        + [pl.BlockSpec(memory_space=pl.ANY)] * (len(constants) - 1),
        out_specs=vmem,
        scratch_shapes=[
            pltpu.VMEM((rows, 2 * lines, width), F32),
            pltpu.VMEM((2 * lines, width), F32),
            pltpu.VMEM(block, F32),
            pltpu.VMEM(block, F32),
            pltpu.VMEM(block, F32),
            pltpu.VMEM(block, F32),
            pltpu.VMEM(block, F32),
            pltpu.VMEM((4 * span, total), F32),
            pltpu.VMEM((sub_count, pair_count) + coverage.shape, jnp.int32),
            pltpu.VMEM((coverage.shape[1] * pair_count * span, total), F32),
            pltpu.VMEM((pair_count,) + phases.shape, F32),
            dma,
            dma((facet_count - 1,)),
            dma((facet_count - 1,)),
            dma((facet_count - 1,)),
            dma((facet_count - 1,)),
            dma((others,)),
            dma((others,)),
            dma((max(pair_count - 1, 1),)),
            dma((max(pair_count - 1, 1),)),
        ]
        + [pltpu.VMEM(table.shape, F32) for table in constants[1:]]
        + [dma((len(constants) - 1,))],
        compiler_params=pltpu.CompilerParams(
            collective_id=0, has_side_effects=True, vmem_limit_bytes=56 * 1024 * 1024
        ),
    )(
        offsets,
        image,
        correction.reshape(lines, width),
        window.reshape(1, width),
        phases,
        coverage,
        *[jnp.asarray(table) for table in constants],
    )
    result = jnp.transpose(result.reshape(rows, lines, 2, width), (0, 2, 1, 3))
    return result.reshape(1, rows, 2, length)


def solution(mesh):
    return jax.shard_map(
        on_device,
        mesh=mesh,
        in_specs=(
            P("facet", None, None, None),
            P("facet", None),
            P(),
            P(),
            P("wa", None),
            P("sub", "wa", None),
        ),
        out_specs=P("facet", ("sub", "wa"), None, None),
        check_vma=False,
    )
```

```python
import functools
import math

import jax
import jax.numpy as jnp
import numpy as np
from jax import lax
from jax.experimental import pallas as pl
from jax.experimental.pallas import tpu as pltpu
from jax.sharding import PartitionSpec as P

MESH = pl.DeviceIdType.MESH
F32 = jnp.float32
BF16 = jnp.bfloat16


def complex_rows(matrix):
    return np.block([[matrix.real, matrix.imag], [-matrix.imag, matrix.real]])


def tables(length, width, facet_count):
    low = length // width
    quads = width // low
    a = np.arange(width)
    b = np.arange(low)
    dft = np.exp(-2j * np.pi * np.outer(a, a) / width)
    order = (a.reshape(width // quads, quads).T).reshape(-1)
    picked = dft[:, order]
    spread = np.zeros((2, width, width, 2))
    spread[0, :, :, 0] = picked.real
    spread[0, :, :, 1] = -picked.imag
    spread[1, :, :, 0] = picked.imag
    spread[1, :, :, 1] = picked.real
    outer = spread.reshape(2 * width, 2 * width)
    turn = np.tile(np.exp(-2j * np.pi * np.outer(a, b) / length), (1, quads))
    turn = np.stack([turn.real, turn.imag]).astype(np.float32)
    fine = np.exp(-2j * np.pi * np.outer(b, b) / low) * length**-0.5
    pick = np.zeros((low, 2, quads, 2, quads, low))
    for quad in range(quads):
        pick[:, 0, quad, 0, quad] = fine.real
        pick[:, 0, quad, 1, quad] = -fine.imag
        pick[:, 1, quad, 0, quad] = fine.imag
        pick[:, 1, quad, 1, quad] = fine.real
    pick = pick.reshape(low, 2 * quads, 2 * width).astype(np.float32)
    unit = complex_rows(np.conj(dft) * width**-0.5)
    twist = np.exp(-2j * np.pi * np.outer(np.arange(facet_count), a) / (facet_count * width))
    twist = np.stack([twist.real, twist.imag]).astype(np.float32)
    outer, unit = outer.astype(np.float32), unit.astype(np.float32)
    return twist, outer, turn, pick, unit, unit.T, outer.T


def split(value):
    high = value.astype(BF16)
    return high, (value - high.astype(F32)).astype(BF16)


def mm(left, right, transposed=False):
    dims = (((1,), (1 if transposed else 0,)), ((), ()))
    dot = functools.partial(lax.dot_general, dimension_numbers=dims, preferred_element_type=F32)
    return dot(left[0], right[0]) + (dot(left[0], right[1]) + dot(left[1], right[0]))


def cos_sin(value):
    turns = jnp.floor(value * (2.0 / math.pi) + 0.5)
    rest = (value - turns * 1.5703125) - turns * (math.pi / 2 - 1.5703125)
    square = rest * rest
    sine = rest + rest * square * (
        -1.0 / 6 + square * (1.0 / 120 + square * (-1.0 / 5040 + square * (1.0 / 362880)))
    )
    cosine = 1.0 + square * (
        -0.5 + square * (1.0 / 24 + square * (-1.0 / 720 + square * (1.0 / 40320)))
    )
    odd = jnp.abs(turns) == 1.0
    sign_cos = jnp.where(turns == 1.0, -1.0, jnp.where(jnp.abs(turns) == 2.0, -1.0, 1.0))
    sign_sin = jnp.where(turns == -1.0, -1.0, jnp.where(jnp.abs(turns) == 2.0, -1.0, 1.0))
    return jnp.where(odd, sine, cosine) * sign_cos, jnp.where(odd, cosine, sine) * sign_sin


def radix(parts, sign):
    count = len(parts)
    if count == 1:
        return parts
    if count % 2:
        raise ValueError("odd length")
    even = radix(parts[0::2], sign)
    odd = radix(parts[1::2], sign)
    first, second = [], []
    for k in range(count // 2):
        real, imag = odd[k]
        if 4 * k == count:
            real, imag = (-imag, real) if sign > 0 else (imag, -real)
        elif k:
            c = math.cos(2 * math.pi * k / count)
            s = sign * math.sin(2 * math.pi * k / count)
            real, imag = real * c - imag * s, real * s + imag * c
        first.append((even[k][0] + real, even[k][1] + imag))
        second.append((even[k][0] - real, even[k][1] - imag))
    return first + second


def swap_blocks(blocks, low):
    blocks = list(blocks)
    count = len(blocks)
    width = count * low
    lane = lax.broadcasted_iota(jnp.int32, blocks[0].shape, 1)
    step = count // 2
    while step:
        shift = step * low
        upper = (lane & shift) != 0
        for i in range(count):
            if i & step:
                continue
            one, two = blocks[i], blocks[i + step]
            blocks[i] = jnp.where(upper, pltpu.roll(two, shift, 1), one)
            blocks[i + step] = jnp.where(upper, two, pltpu.roll(one, width - shift, 1))
        step //= 2
    return blocks


def offset_tables(offsets_ref, window_ref, quads):
    width = window_ref.shape[1]
    subs = offsets_ref.shape[0]
    span = subs * quads
    starts = [offsets_ref[s] for s in range(subs)]
    first_q = [start // width for start in starts]
    rests = [start & (width - 1) for start in starts]
    row = lax.broadcasted_iota(jnp.int32, (span, width), 0)
    offset_rows = jnp.zeros((span, width), jnp.int32)
    window_full = jnp.broadcast_to(window_ref[...], (8, width))
    window_rows = jnp.zeros((span, width), F32)
    for s in range(subs):
        offset_rows = jnp.where(row >= s * quads, rests[s], offset_rows)
        moved = pltpu.roll(window_full, rests[s], 1)[0:1]
        window_rows = jnp.where(row >= s * quads, moved, window_rows)
    span_lane = lax.broadcasted_iota(jnp.int32, (span, width), 1)
    steps = ((offset_rows * span_lane + width // 2) & (width - 1)) - width // 2
    turn_cos, turn_sin = cos_sin(steps.astype(F32) * (2.0 * math.pi / width))
    return first_q, turn_cos, turn_sin, span_lane >= offset_rows, window_rows


def gather_pick(first_q, pick_ref):
    low = pick_ref.shape[0]
    picked = []
    for q in first_q:
        picked.append(pick_ref[q])
        picked.append(pick_ref[lax.rem(q + 1, low)])
    return split(jnp.concatenate(picked, axis=0))


def kernel(
    geometry,
    offsets_ref,
    facets_ref,
    correction_ref,
    window_ref,
    phases_ref,
    coverage_ref,
    twist_ref,
    outer_far,
    turn_far,
    pick_far,
    unit_far,
    unit_t_far,
    returned,
    image,
    gain,
    cut,
    sent,
    arrived,
    back,
    counts,
    expanded,
    screens,
    load_sem,
    fwd_send,
    fwd_recv,
    bwd_send,
    bwd_recv,
    cov_send,
    cov_recv,
    ph_send,
    ph_recv,
    outer_ref,
    turn_ref,
    pick_ref,
    unit_ref,
    unit_t_ref,
    table_sem,
):
    facet_count, sub_count, pair_count = geometry
    facet = lax.axis_index("facet")
    sub = lax.axis_index("sub")
    pair = lax.axis_index("wa")
    rows = image.shape[0]
    width = window_ref.shape[1]
    subs = offsets_ref.shape[0]
    low = pick_ref.shape[0]
    quads = width // low
    length = low * width
    span = subs * quads
    per_sub, per_wa = coverage_ref.shape[0], coverage_ref.shape[1]
    planes = per_wa * pair_count
    total = facet_count * width

    facet_mates = [lax.rem(facet + d, facet_count) for d in range(1, facet_count)]
    hops = [(ds, dw) for ds in range(sub_count) for dw in range(pair_count) if ds or dw]
    barrier = pltpu.get_barrier_semaphore()
    for mate in facet_mates:
        pl.semaphore_signal(barrier, inc=1, device_id={"facet": mate}, device_id_type=MESH)
    grid_mates = [(lax.rem(sub + ds, sub_count), lax.rem(pair + dw, pair_count)) for ds, dw in hops]
    for mate_sub, mate_pair in grid_mates:
        pl.semaphore_signal(
            barrier, inc=1, device_id={"sub": mate_sub, "wa": mate_pair}, device_id_type=MESH
        )
    load = pltpu.make_async_copy(
        facets_ref.at[pl.ds((sub * pair_count + pair) * rows, rows)], image, load_sem
    )
    load.start()
    fetches = {}
    for i, (name, far, near) in enumerate(
        (
            ("outer", outer_far, outer_ref),
            ("turn", turn_far, turn_ref),
            ("pick", pick_far, pick_ref),
            ("unit", unit_far, unit_ref),
            ("unit_t", unit_t_far, unit_t_ref),
        )
    ):
        fetches[name] = pltpu.make_async_copy(far, near, table_sem.at[i])
        fetches[name].start()

    gain[pl.ds(0, low, stride=2), :] = correction_ref[...]
    gain[pl.ds(1, low, stride=2), :] = correction_ref[...]
    first_q, turn_cos, turn_sin, is_first, window_rows = offset_tables(
        offsets_ref, window_ref, quads
    )
    fetches["pick"].wait()
    picked = gather_pick(first_q, pick_ref)

    load.wait()
    gains = gain[...]
    groups = []
    for g in range(facet_count):
        blocks = [image[g * quads + i] * gains for i in range(quads)]
        groups.append(jnp.concatenate(swap_blocks(blocks, low), axis=0))
    spread = jnp.concatenate(groups, axis=1)
    fetches["outer"].wait()
    mixed = mm(split(outer_ref[...]), split(spread))
    fetches["turn"].wait()
    table_cos, table_sin = turn_ref[0], turn_ref[1]
    turned = []
    for g in range(facet_count):
        real = mixed[:width, g * width : (g + 1) * width]
        imag = mixed[width:, g * width : (g + 1) * width]
        turned.append(
            jnp.concatenate(
                [real * table_cos - imag * table_sin, real * table_sin + imag * table_cos], axis=1
            )
        )
    turned = jnp.concatenate(turned, axis=0)
    spectrum = mm(picked, split(turned), transposed=True)

    pl.semaphore_wait(barrier, len(facet_mates) + len(hops))
    copies = []
    for i, (mate_sub, mate_pair) in enumerate(grid_mates):
        copy = pltpu.make_async_remote_copy(
            src_ref=coverage_ref,
            dst_ref=counts.at[sub, pair],
            send_sem=cov_send.at[i],
            recv_sem=cov_recv.at[i],
            device_id={"sub": mate_sub, "wa": mate_pair},
            device_id_type=MESH,
        )
        copy.start()
        copies.append(copy)
    counts[sub, pair] = coverage_ref[...]
    for d in range(1, pair_count):
        copy = pltpu.make_async_remote_copy(
            src_ref=phases_ref,
            dst_ref=screens.at[pair],
            send_sem=ph_send.at[d - 1],
            recv_sem=ph_recv.at[d - 1],
            device_id={"wa": lax.rem(pair + d, pair_count)},
            device_id_type=MESH,
        )
        copy.start()
        copies.append(copy)
    screens[pair] = phases_ref[...]

    for s in range(subs):
        here = slice(s * quads, (s + 1) * quads)
        base = s * 4 * quads
        keep = is_first[here]
        win = window_rows[here]
        for g in range(facet_count):
            cols = slice(g * width, (g + 1) * width)
            for c in range(2):
                one = spectrum[base + c * quads : base + (c + 1) * quads, cols]
                two = spectrum[base + (2 + c) * quads : base + (3 + c) * quads, cols]
                cut[g, here, c * width : (c + 1) * width] = jnp.where(keep, one, two) * win
    fetches["unit"].wait()
    unit = split(unit_ref[...])
    mixed = mm(split(cut[...].reshape(facet_count * span, 2 * width)), unit)
    for g in range(facet_count):
        real = mixed[g * span : (g + 1) * span, :width]
        imag = mixed[g * span : (g + 1) * span, width:]
        sent[g, :, :width] = real * turn_cos + imag * turn_sin
        sent[g, :, width:] = imag * turn_cos - real * turn_sin
    forward = []
    for i, mate in enumerate(facet_mates):
        copy = pltpu.make_async_remote_copy(
            src_ref=sent.at[mate],
            dst_ref=arrived.at[facet],
            send_sem=fwd_send.at[i],
            recv_sem=fwd_recv.at[i],
            device_id={"facet": mate},
            device_id_type=MESH,
        )
        copy.start()
        forward.append(copy)
    arrived[facet] = sent[facet]

    fetches["unit_t"].wait()
    unit_t = split(unit_t_ref[...])

    for copy in copies:
        copy.wait()
    for owner in range(sub_count):
        for p in range(pair_count):
            for i in range(per_sub):
                for j in range(per_wa):
                    at = (p * per_wa + j) * span + (owner * per_sub + i) * quads
                    row = counts[owner, p, i, j : j + 1].astype(F32)
                    expanded[at : at + quads, :] = jnp.broadcast_to(row, (quads, total))
    source = lax.broadcasted_iota(jnp.int32, (total, total), 0)
    inner = lax.broadcasted_iota(jnp.int32, (1, width), 1) * facet_count
    wanted = jnp.concatenate([inner + k for k in range(facet_count)], axis=1)
    chooser = jnp.where(source == wanted, 1.0, 0.0).astype(BF16)
    weights = jnp.dot(expanded[...].astype(BF16), chooser, preferred_element_type=F32)
    weights = weights * (1.0 / (facet_count * planes))
    kernels = []
    for p in range(pair_count):
        screen = screens[p]
        cos_all, sin_all = cos_sin(screen)
        for j in range(per_wa):
            kernels.append((cos_all[j : j + 1], sin_all[j : j + 1]))
    twist = [(twist_ref[0, k : k + 1], twist_ref[1, k : k + 1]) for k in range(facet_count)]

    for copy in forward:
        copy.wait()
    pieces = [[] for _ in range(facet_count)]
    for w in range(planes):
        parts = []
        for f in range(facet_count):
            cols = slice(f * width, (f + 1) * width)
            kc, ks = kernels[w][0][:, cols], kernels[w][1][:, cols]
            real, imag = arrived[f, :, :width], arrived[f, :, width:]
            parts.append((real * kc - imag * ks, real * ks + imag * kc))
        for k, (real, imag) in enumerate(radix(parts, -1)):
            tc, ts = twist[k]
            pieces[k].append(
                jnp.concatenate([real * tc - imag * ts, real * ts + imag * tc], axis=1)
            )
    stacked = jnp.concatenate([piece for group in pieces for piece in group], axis=0)
    grid = mm(split(stacked), unit_t)
    scale = jnp.concatenate(
        [weights[:, k * width : (k + 1) * width] for k in range(facet_count)], axis=0
    )
    weighted = grid * jnp.concatenate([scale, scale], axis=1)
    image_side = mm(split(weighted), unit)
    sums = [None] * facet_count
    for w in range(planes):
        parts = []
        for k in range(facet_count):
            at = (k * planes + w) * span
            real = image_side[at : at + span, :width]
            imag = image_side[at : at + span, width:]
            tc, ts = twist[k]
            parts.append((real * tc + imag * ts, imag * tc - real * ts))
        for f, (real, imag) in enumerate(radix(parts, 1)):
            cols = slice(f * width, (f + 1) * width)
            kc, ks = kernels[w][0][:, cols], kernels[w][1][:, cols]
            term = (real * kc + imag * ks, imag * kc - real * ks)
            sums[f] = term if w == 0 else (sums[f][0] + term[0], sums[f][1] + term[1])
    for f in range(facet_count):
        back[f, :, :width] = sums[f][0]
        back[f, :, width:] = sums[f][1]
    backward = []
    for i, mate in enumerate(facet_mates):
        copy = pltpu.make_async_remote_copy(
            src_ref=back.at[mate],
            dst_ref=returned.at[facet],
            send_sem=bwd_send.at[i],
            recv_sem=bwd_recv.at[i],
            device_id={"facet": mate},
            device_id_type=MESH,
        )
        copy.start()
        backward.append(copy)
    returned[facet] = back[facet]
    for copy in backward:
        copy.wait()


def inverse_kernel(
    offsets_ref,
    returned,
    correction_ref,
    window_ref,
    unit_t_far,
    pick_far,
    turn_far,
    outer_t_far,
    out_ref,
    gain,
    segments,
    image,
    unit_t_ref,
    pick_ref,
    turn_ref,
    outer_t_ref,
    table_sem,
    out_sem,
):
    facet_count, span, double = returned.shape
    width = double // 2
    subs = offsets_ref.shape[0]
    low = pick_ref.shape[0]
    quads = width // low
    fetches = {}
    for i, (name, far, near) in enumerate(
        (
            ("unit_t", unit_t_far, unit_t_ref),
            ("pick", pick_far, pick_ref),
            ("turn", turn_far, turn_ref),
            ("outer_t", outer_t_far, outer_t_ref),
        )
    ):
        fetches[name] = pltpu.make_async_copy(far, near, table_sem.at[i])
        fetches[name].start()
    gain[pl.ds(0, low, stride=2), :] = correction_ref[...]
    gain[pl.ds(1, low, stride=2), :] = correction_ref[...]
    gains = gain[...]
    first_q, turn_cos, turn_sin, is_first, window_rows = offset_tables(
        offsets_ref, window_ref, quads
    )
    unturned = []
    for g in range(facet_count):
        real, imag = returned[g, :, :width], returned[g, :, width:]
        unturned.append(
            jnp.concatenate(
                [real * turn_cos - imag * turn_sin, real * turn_sin + imag * turn_cos], axis=1
            )
        )
    unturned = jnp.concatenate(unturned, axis=0)
    fetches["unit_t"].wait()
    mixed = mm(split(unturned), split(unit_t_ref[...]))
    win_first = jnp.where(is_first, window_rows, 0.0)
    win_second = jnp.where(is_first, 0.0, window_rows)
    for g in range(facet_count):
        cols = slice(g * width, (g + 1) * width)
        for c in range(2):
            part = mixed[g * span : (g + 1) * span, c * width : (c + 1) * width]
            for h, win in enumerate((win_first, win_second)):
                masked = part * win
                for s in range(subs):
                    at = (4 * s + 2 * h + c) * quads
                    segments[at : at + quads, cols] = masked[s * quads : (s + 1) * quads]
    columns = jnp.concatenate(
        [segments[:, g * width : (g + 1) * width].T for g in range(facet_count)], axis=0
    )
    fetches["pick"].wait()
    fine = mm(split(columns), gather_pick(first_q, pick_ref))
    fetches["turn"].wait()
    table_cos, table_sin = turn_ref[0], turn_ref[1]
    reals, imags = [], []
    for g in range(facet_count):
        real = fine[g * width : (g + 1) * width, :width]
        imag = fine[g * width : (g + 1) * width, width:]
        reals.append(real * table_cos + imag * table_sin)
        imags.append(imag * table_cos - real * table_sin)
    joined = jnp.concatenate(
        [jnp.concatenate(reals, axis=1), jnp.concatenate(imags, axis=1)], axis=0
    )
    fetches["outer_t"].wait()
    spread = mm(split(outer_t_ref[...]), split(joined))
    part = 2 * width // quads
    stores = []
    for g in range(facet_count):
        cols = slice(g * width, (g + 1) * width)
        blocks = [spread[i * part : (i + 1) * part, cols] for i in range(quads)]
        for i, block in enumerate(swap_blocks(blocks, low)):
            image[g * quads + i] = block * gains
        store = pltpu.make_async_copy(
            image.at[pl.ds(g * quads, quads)], out_ref.at[pl.ds(g * quads, quads)], out_sem.at[g]
        )
        store.start()
        stores.append(store)
    for store in stores:
        store.wait()


def on_device(facets, correction, window, offsets, phases, coverage):
    facet_count = lax.axis_size("facet")
    sub_count = lax.axis_size("sub")
    pair_count = lax.axis_size("wa")
    row_count, length = facets.shape[1], facets.shape[3]
    width = window.shape[0]
    subs = offsets.shape[0]
    rows = row_count // (sub_count * pair_count)
    low = length // width
    quads = width // low
    if rows != facet_count * quads or low * quads != width:
        raise ValueError("unsupported sizes")
    span = subs * quads
    total = facet_count * width
    lines = length // width
    image = facets.reshape(row_count, 2, lines, width)
    image = jnp.transpose(image, (0, 2, 1, 3)).reshape(row_count, 2 * lines, width)
    twist, outer, turn, pick, unit, unit_t, outer_t = tables(length, width, facet_count)
    vmem = pl.BlockSpec(memory_space=pltpu.VMEM)
    smem = pl.BlockSpec(memory_space=pltpu.SMEM)
    far = pl.BlockSpec(memory_space=pltpu.HBM)
    others = sub_count * pair_count - 1
    dma = pltpu.SemaphoreType.DMA
    block = (facet_count, span, 2 * width)
    gains = correction.reshape(lines, width)
    window = window.reshape(1, width)
    first_tables = [outer, turn, pick, unit, unit_t]
    returned = pl.pallas_call(
        functools.partial(kernel, (facet_count, sub_count, pair_count)),
        out_shape=pltpu.VMEM(block, F32),
        in_specs=[smem, far] + [vmem] * 5 + [far] * len(first_tables),
        out_specs=vmem,
        scratch_shapes=[
            pltpu.VMEM((rows, 2 * lines, width), F32),
            pltpu.VMEM((2 * lines, width), F32),
            pltpu.VMEM(block, F32),
            pltpu.VMEM(block, F32),
            pltpu.VMEM(block, F32),
            pltpu.VMEM(block, F32),
            pltpu.VMEM((sub_count, pair_count) + coverage.shape, jnp.int32),
            pltpu.VMEM((coverage.shape[1] * pair_count * span, total), F32),
            pltpu.VMEM((pair_count,) + phases.shape, F32),
            dma,
            dma((facet_count - 1,)),
            dma((facet_count - 1,)),
            dma((facet_count - 1,)),
            dma((facet_count - 1,)),
            dma((others,)),
            dma((others,)),
            dma((max(pair_count - 1, 1),)),
            dma((max(pair_count - 1, 1),)),
        ]
        + [pltpu.VMEM(table.shape, F32) for table in first_tables]
        + [dma((len(first_tables),))],
        compiler_params=pltpu.CompilerParams(
            collective_id=0, has_side_effects=True, vmem_limit_bytes=55 * 1024 * 1024
        ),
    )(offsets, image, gains, window, phases, coverage, jnp.asarray(twist), *map(jnp.asarray, first_tables))
    second_tables = [unit_t, pick, turn, outer_t]
    result = pl.pallas_call(
        inverse_kernel,
        out_shape=jax.ShapeDtypeStruct((rows, 2 * lines, width), F32),
        in_specs=[smem] + [vmem] * 3 + [pl.BlockSpec(memory_space=pl.ANY)] * len(second_tables),
        out_specs=far,
        scratch_shapes=[
            pltpu.VMEM((2 * lines, width), F32),
            pltpu.VMEM((4 * span, total), F32),
            pltpu.VMEM((rows, 2 * lines, width), F32),
        ]
        + [pltpu.VMEM(table.shape, F32) for table in second_tables]
        + [dma((len(second_tables),)), dma((facet_count,))],
        compiler_params=pltpu.CompilerParams(vmem_limit_bytes=48 * 1024 * 1024),
    )(offsets, returned, gains, window, *map(jnp.asarray, second_tables))
    result = jnp.transpose(result.reshape(rows, lines, 2, width), (0, 2, 1, 3))
    return result.reshape(1, rows, 2, length)


def solution(mesh):
    return jax.shard_map(
        on_device,
        mesh=mesh,
        in_specs=(
            P("facet", None, None, None),
            P("facet", None),
            P(),
            P(),
            P("wa", None),
            P("sub", "wa", None),
        ),
        out_specs=P("facet", ("sub", "wa"), None, None),
        check_vma=False,
    )
```

```python
import functools
import math

import jax
import jax.numpy as jnp
import numpy as np
from jax import lax
from jax.experimental import pallas as pl
from jax.experimental.pallas import tpu as pltpu
from jax.sharding import PartitionSpec as P

MESH = pl.DeviceIdType.MESH
F32 = jnp.float32
BF16 = jnp.bfloat16


def complex_rows(matrix):
    return np.block([[matrix.real, matrix.imag], [-matrix.imag, matrix.real]])


def tables(length, width, facet_count):
    low = length // width
    quads = width // low
    a = np.arange(width)
    b = np.arange(low)
    dft = np.exp(-2j * np.pi * np.outer(a, a) / width)
    order = (a.reshape(width // quads, quads).T).reshape(-1)
    picked = dft[:, order]
    spread = np.zeros((2, width, width, 2))
    spread[0, :, :, 0] = picked.real
    spread[0, :, :, 1] = -picked.imag
    spread[1, :, :, 0] = picked.imag
    spread[1, :, :, 1] = picked.real
    outer = spread.reshape(2 * width, 2 * width)
    turn = np.tile(np.exp(-2j * np.pi * np.outer(a, b) / length), (1, quads))
    turn = np.stack([turn.real, turn.imag]).astype(np.float32)
    fine = np.exp(-2j * np.pi * np.outer(b, b) / low) * length**-0.5
    pick = np.zeros((low, 2, quads, 2, quads, low))
    for quad in range(quads):
        pick[:, 0, quad, 0, quad] = fine.real
        pick[:, 0, quad, 1, quad] = -fine.imag
        pick[:, 1, quad, 0, quad] = fine.imag
        pick[:, 1, quad, 1, quad] = fine.real
    pick = pick.reshape(low, 2 * quads, 2 * width).astype(np.float32)
    unit = complex_rows(np.conj(dft) * width**-0.5)
    twist = np.exp(-2j * np.pi * np.outer(np.arange(facet_count), a) / (facet_count * width))
    twist = np.stack([twist.real, twist.imag]).astype(np.float32)
    outer, unit = outer.astype(np.float32), unit.astype(np.float32)
    return twist, outer, turn, pick, unit, unit.T, outer.T


def split(value):
    high = value.astype(BF16)
    return high, (value - high.astype(F32)).astype(BF16)


def mm(left, right, transposed=False):
    axis = 1 if transposed else 0
    one = jnp.concatenate([left[0], left[0], left[1]], axis=1)
    two = jnp.concatenate([right[0], right[1], right[0]], axis=axis)
    return lax.dot_general(one, two, (((1,), (axis,)), ((), ())), preferred_element_type=F32)


def cos_sin(value):
    turns = jnp.floor(value * (2.0 / math.pi) + 0.5)
    rest = (value - turns * 1.5703125) - turns * (math.pi / 2 - 1.5703125)
    square = rest * rest
    sine = rest + rest * square * (
        -1.0 / 6 + square * (1.0 / 120 + square * (-1.0 / 5040 + square * (1.0 / 362880)))
    )
    cosine = 1.0 + square * (
        -0.5 + square * (1.0 / 24 + square * (-1.0 / 720 + square * (1.0 / 40320)))
    )
    odd = jnp.abs(turns) == 1.0
    sign_cos = jnp.where(turns == 1.0, -1.0, jnp.where(jnp.abs(turns) == 2.0, -1.0, 1.0))
    sign_sin = jnp.where(turns == -1.0, -1.0, jnp.where(jnp.abs(turns) == 2.0, -1.0, 1.0))
    return jnp.where(odd, sine, cosine) * sign_cos, jnp.where(odd, cosine, sine) * sign_sin


def radix(parts, sign):
    count = len(parts)
    if count == 1:
        return parts
    if count % 2:
        raise ValueError("odd length")
    even = radix(parts[0::2], sign)
    odd = radix(parts[1::2], sign)
    first, second = [], []
    for k in range(count // 2):
        real, imag = odd[k]
        if 4 * k == count:
            real, imag = (-imag, real) if sign > 0 else (imag, -real)
        elif k:
            c = math.cos(2 * math.pi * k / count)
            s = sign * math.sin(2 * math.pi * k / count)
            real, imag = real * c - imag * s, real * s + imag * c
        first.append((even[k][0] + real, even[k][1] + imag))
        second.append((even[k][0] - real, even[k][1] - imag))
    return first + second


def swap_blocks(blocks, low):
    blocks = list(blocks)
    count = len(blocks)
    width = count * low
    lane = lax.broadcasted_iota(jnp.int32, blocks[0].shape, 1)
    step = count // 2
    while step:
        shift = step * low
        upper = (lane & shift) != 0
        for i in range(count):
            if i & step:
                continue
            one, two = blocks[i], blocks[i + step]
            blocks[i] = jnp.where(upper, pltpu.roll(two, shift, 1), one)
            blocks[i + step] = jnp.where(upper, two, pltpu.roll(one, width - shift, 1))
        step //= 2
    return blocks


def offset_tables(offsets_ref, window_ref, quads):
    width = window_ref.shape[1]
    subs = offsets_ref.shape[0]
    span = subs * quads
    starts = [offsets_ref[s] for s in range(subs)]
    first_q = [start // width for start in starts]
    rests = [start & (width - 1) for start in starts]
    row = lax.broadcasted_iota(jnp.int32, (span, width), 0)
    offset_rows = jnp.zeros((span, width), jnp.int32)
    window_full = jnp.broadcast_to(window_ref[...], (8, width))
    window_rows = jnp.zeros((span, width), F32)
    for s in range(subs):
        offset_rows = jnp.where(row >= s * quads, rests[s], offset_rows)
        moved = pltpu.roll(window_full, rests[s], 1)[0:1]
        window_rows = jnp.where(row >= s * quads, moved, window_rows)
    span_lane = lax.broadcasted_iota(jnp.int32, (span, width), 1)
    steps = ((offset_rows * span_lane + width // 2) & (width - 1)) - width // 2
    turn_cos, turn_sin = cos_sin(steps.astype(F32) * (2.0 * math.pi / width))
    return first_q, turn_cos, turn_sin, span_lane >= offset_rows, window_rows


def gather_pick(first_q, pick_ref):
    low = pick_ref.shape[0]
    picked = []
    for q in first_q:
        picked.append(pick_ref[q])
        picked.append(pick_ref[lax.rem(q + 1, low)])
    return split(jnp.concatenate(picked, axis=0))


def kernel(
    geometry,
    offsets_ref,
    facets_ref,
    correction_ref,
    window_ref,
    phases_ref,
    coverage_ref,
    twist_ref,
    outer_far,
    turn_far,
    pick_far,
    unit_far,
    unit_t_far,
    returned,
    image,
    gain,
    cut,
    sent,
    arrived,
    back,
    counts,
    expanded,
    screens,
    load_sem,
    fwd_send,
    fwd_recv,
    bwd_send,
    bwd_recv,
    cov_send,
    cov_recv,
    ph_send,
    ph_recv,
    outer_ref,
    turn_ref,
    pick_ref,
    unit_ref,
    unit_t_ref,
    table_sem,
):
    facet_count, sub_count, pair_count = geometry
    facet = lax.axis_index("facet")
    sub = lax.axis_index("sub")
    pair = lax.axis_index("wa")
    rows = image.shape[0]
    width = window_ref.shape[1]
    subs = offsets_ref.shape[0]
    low = pick_ref.shape[0]
    quads = width // low
    length = low * width
    span = subs * quads
    per_sub, per_wa = coverage_ref.shape[0], coverage_ref.shape[1]
    planes = per_wa * pair_count
    total = facet_count * width

    facet_mates = [lax.rem(facet + d, facet_count) for d in range(1, facet_count)]
    hops = [(ds, dw) for ds in range(sub_count) for dw in range(pair_count) if ds or dw]
    barrier = pltpu.get_barrier_semaphore()
    for mate in facet_mates:
        pl.semaphore_signal(barrier, inc=1, device_id={"facet": mate}, device_id_type=MESH)
    grid_mates = [(lax.rem(sub + ds, sub_count), lax.rem(pair + dw, pair_count)) for ds, dw in hops]
    for mate_sub, mate_pair in grid_mates:
        pl.semaphore_signal(
            barrier, inc=1, device_id={"sub": mate_sub, "wa": mate_pair}, device_id_type=MESH
        )
    load = pltpu.make_async_copy(
        facets_ref.at[pl.ds((sub * pair_count + pair) * rows, rows)], image, load_sem
    )
    load.start()
    fetches = {}
    for i, (name, far, near) in enumerate(
        (
            ("outer", outer_far, outer_ref),
            ("turn", turn_far, turn_ref),
            ("pick", pick_far, pick_ref),
            ("unit", unit_far, unit_ref),
            ("unit_t", unit_t_far, unit_t_ref),
        )
    ):
        fetches[name] = pltpu.make_async_copy(far, near, table_sem.at[i])
        fetches[name].start()

    def gathers():
        copies = []
        for i, (mate_sub, mate_pair) in enumerate(grid_mates):
            copies.append(
                pltpu.make_async_remote_copy(
                    src_ref=coverage_ref,
                    dst_ref=counts.at[sub, pair],
                    send_sem=cov_send.at[i],
                    recv_sem=cov_recv.at[i],
                    device_id={"sub": mate_sub, "wa": mate_pair},
                    device_id_type=MESH,
                )
            )
        for d in range(1, pair_count):
            copies.append(
                pltpu.make_async_remote_copy(
                    src_ref=phases_ref,
                    dst_ref=screens.at[pair],
                    send_sem=ph_send.at[d - 1],
                    recv_sem=ph_recv.at[d - 1],
                    device_id={"wa": lax.rem(pair + d, pair_count)},
                    device_id_type=MESH,
                )
            )
        return copies

    def greet():
        pl.semaphore_wait(barrier, len(facet_mates) + len(hops))
        for copy in gathers():
            copy.start()

    counts[sub, pair] = coverage_ref[...]
    screens[pair] = phases_ref[...]

    gain[pl.ds(0, low, stride=2), :] = correction_ref[...]
    gain[pl.ds(1, low, stride=2), :] = correction_ref[...]
    first_q, turn_cos, turn_sin, is_first, window_rows = offset_tables(
        offsets_ref, window_ref, quads
    )
    fetches["pick"].wait()
    picked = gather_pick(first_q, pick_ref)

    load.wait()
    gains = gain[...]
    groups = []
    for g in range(facet_count):
        blocks = [image[g * quads + i] * gains for i in range(quads)]
        groups.append(jnp.concatenate(swap_blocks(blocks, low), axis=0))
    spread = jnp.concatenate(groups, axis=1)
    fetches["outer"].wait()
    mixed = mm(split(outer_ref[...]), split(spread))
    pl.when(sub != 0)(greet)
    fetches["turn"].wait()
    table_cos, table_sin = turn_ref[0], turn_ref[1]
    turned = []
    for g in range(facet_count):
        real = mixed[:width, g * width : (g + 1) * width]
        imag = mixed[width:, g * width : (g + 1) * width]
        turned.append(
            jnp.concatenate(
                [real * table_cos - imag * table_sin, real * table_sin + imag * table_cos], axis=1
            )
        )
    turned = jnp.concatenate(turned, axis=0)
    spectrum = mm(picked, split(turned), transposed=True)

    pl.when(sub == 0)(greet)
    for s in range(subs):
        here = slice(s * quads, (s + 1) * quads)
        base = s * 4 * quads
        keep = is_first[here]
        win = window_rows[here]
        for g in range(facet_count):
            cols = slice(g * width, (g + 1) * width)
            for c in range(2):
                one = spectrum[base + c * quads : base + (c + 1) * quads, cols]
                two = spectrum[base + (2 + c) * quads : base + (3 + c) * quads, cols]
                cut[g, here, c * width : (c + 1) * width] = jnp.where(keep, one, two) * win
    fetches["unit"].wait()
    unit = split(unit_ref[...])
    mixed = mm(split(cut[...].reshape(facet_count * span, 2 * width)), unit)
    for g in range(facet_count):
        real = mixed[g * span : (g + 1) * span, :width]
        imag = mixed[g * span : (g + 1) * span, width:]
        sent[g, :, :width] = real * turn_cos + imag * turn_sin
        sent[g, :, width:] = imag * turn_cos - real * turn_sin
    forward = []
    for i, mate in enumerate(facet_mates):
        copy = pltpu.make_async_remote_copy(
            src_ref=sent.at[mate],
            dst_ref=arrived.at[facet],
            send_sem=fwd_send.at[i],
            recv_sem=fwd_recv.at[i],
            device_id={"facet": mate},
            device_id_type=MESH,
        )
        copy.start()
        forward.append(copy)
    arrived[facet] = sent[facet]

    fetches["unit_t"].wait()
    unit_t = split(unit_t_ref[...])

    for copy in gathers():
        copy.wait()
    for owner in range(sub_count):
        for p in range(pair_count):
            for i in range(per_sub):
                for j in range(per_wa):
                    at = (p * per_wa + j) * span + (owner * per_sub + i) * quads
                    row = counts[owner, p, i, j : j + 1].astype(F32)
                    expanded[at : at + quads, :] = jnp.broadcast_to(row, (quads, total))
    source = lax.broadcasted_iota(jnp.int32, (total, total), 0)
    inner = lax.broadcasted_iota(jnp.int32, (1, width), 1) * facet_count
    wanted = jnp.concatenate([inner + k for k in range(facet_count)], axis=1)
    chooser = jnp.where(source == wanted, 1.0, 0.0).astype(BF16)
    weights = jnp.dot(expanded[...].astype(BF16), chooser, preferred_element_type=F32)
    weights = weights * (1.0 / (facet_count * planes))
    kernels = []
    for p in range(pair_count):
        screen = screens[p]
        cos_all, sin_all = cos_sin(screen)
        for j in range(per_wa):
            kernels.append((cos_all[j : j + 1], sin_all[j : j + 1]))
    twist = [(twist_ref[0, k : k + 1], twist_ref[1, k : k + 1]) for k in range(facet_count)]

    for copy in forward:
        copy.wait()
    pieces = [[] for _ in range(facet_count)]
    for w in range(planes):
        parts = []
        for f in range(facet_count):
            cols = slice(f * width, (f + 1) * width)
            kc, ks = kernels[w][0][:, cols], kernels[w][1][:, cols]
            real, imag = arrived[f, :, :width], arrived[f, :, width:]
            parts.append((real * kc - imag * ks, real * ks + imag * kc))
        for k, (real, imag) in enumerate(radix(parts, -1)):
            tc, ts = twist[k]
            pieces[k].append(
                jnp.concatenate([real * tc - imag * ts, real * ts + imag * tc], axis=1)
            )
    stacked = jnp.concatenate([piece for group in pieces for piece in group], axis=0)
    grid = mm(split(stacked), unit_t)
    scale = jnp.concatenate(
        [weights[:, k * width : (k + 1) * width] for k in range(facet_count)], axis=0
    )
    weighted = grid * jnp.concatenate([scale, scale], axis=1)
    image_side = mm(split(weighted), unit)
    sums = [None] * facet_count
    for w in range(planes):
        parts = []
        for k in range(facet_count):
            at = (k * planes + w) * span
            real = image_side[at : at + span, :width]
            imag = image_side[at : at + span, width:]
            tc, ts = twist[k]
            parts.append((real * tc + imag * ts, imag * tc - real * ts))
        for f, (real, imag) in enumerate(radix(parts, 1)):
            cols = slice(f * width, (f + 1) * width)
            kc, ks = kernels[w][0][:, cols], kernels[w][1][:, cols]
            term = (real * kc + imag * ks, imag * kc - real * ks)
            sums[f] = term if w == 0 else (sums[f][0] + term[0], sums[f][1] + term[1])
    for f in range(facet_count):
        back[f, :, :width] = sums[f][0]
        back[f, :, width:] = sums[f][1]
    backward = []
    for i, mate in enumerate(facet_mates):
        copy = pltpu.make_async_remote_copy(
            src_ref=back.at[mate],
            dst_ref=returned.at[facet],
            send_sem=bwd_send.at[i],
            recv_sem=bwd_recv.at[i],
            device_id={"facet": mate},
            device_id_type=MESH,
        )
        copy.start()
        backward.append(copy)
    returned[facet] = back[facet]
    for copy in backward:
        copy.wait()


def inverse_kernel(
    offsets_ref,
    returned,
    correction_ref,
    window_ref,
    unit_t_far,
    pick_far,
    turn_far,
    outer_t_far,
    out_ref,
    gain,
    segments,
    image,
    unit_t_ref,
    pick_ref,
    turn_ref,
    outer_t_ref,
    table_sem,
    out_sem,
):
    facet_count, span, double = returned.shape
    width = double // 2
    subs = offsets_ref.shape[0]
    low = pick_ref.shape[0]
    quads = width // low
    fetches = {}
    for i, (name, far, near) in enumerate(
        (
            ("unit_t", unit_t_far, unit_t_ref),
            ("pick", pick_far, pick_ref),
            ("turn", turn_far, turn_ref),
            ("outer_t", outer_t_far, outer_t_ref),
        )
    ):
        fetches[name] = pltpu.make_async_copy(far, near, table_sem.at[i])
        fetches[name].start()
    gain[pl.ds(0, low, stride=2), :] = correction_ref[...]
    gain[pl.ds(1, low, stride=2), :] = correction_ref[...]
    gains = gain[...]
    first_q, turn_cos, turn_sin, is_first, window_rows = offset_tables(
        offsets_ref, window_ref, quads
    )
    unturned = []
    for g in range(facet_count):
        real, imag = returned[g, :, :width], returned[g, :, width:]
        unturned.append(
            jnp.concatenate(
                [real * turn_cos - imag * turn_sin, real * turn_sin + imag * turn_cos], axis=1
            )
        )
    unturned = jnp.concatenate(unturned, axis=0)
    fetches["unit_t"].wait()
    mixed = mm(split(unturned), split(unit_t_ref[...]))
    win_first = jnp.where(is_first, window_rows, 0.0)
    win_second = jnp.where(is_first, 0.0, window_rows)
    for g in range(facet_count):
        cols = slice(g * width, (g + 1) * width)
        for c in range(2):
            part = mixed[g * span : (g + 1) * span, c * width : (c + 1) * width]
            for h, win in enumerate((win_first, win_second)):
                masked = part * win
                for s in range(subs):
                    at = (4 * s + 2 * h + c) * quads
                    segments[at : at + quads, cols] = masked[s * quads : (s + 1) * quads]
    columns = jnp.concatenate(
        [segments[:, g * width : (g + 1) * width].T for g in range(facet_count)], axis=0
    )
    fetches["pick"].wait()
    fine = mm(split(columns), gather_pick(first_q, pick_ref))
    fetches["turn"].wait()
    table_cos, table_sin = turn_ref[0], turn_ref[1]
    reals, imags = [], []
    for g in range(facet_count):
        real = fine[g * width : (g + 1) * width, :width]
        imag = fine[g * width : (g + 1) * width, width:]
        reals.append(real * table_cos + imag * table_sin)
        imags.append(imag * table_cos - real * table_sin)
    joined = jnp.concatenate(
        [jnp.concatenate(reals, axis=1), jnp.concatenate(imags, axis=1)], axis=0
    )
    fetches["outer_t"].wait()
    spread = mm(split(outer_t_ref[...]), split(joined))
    part = 2 * width // quads
    stores = []
    for g in range(facet_count):
        cols = slice(g * width, (g + 1) * width)
        blocks = [spread[i * part : (i + 1) * part, cols] for i in range(quads)]
        for i, block in enumerate(swap_blocks(blocks, low)):
            image[g * quads + i] = block * gains
        store = pltpu.make_async_copy(
            image.at[pl.ds(g * quads, quads)], out_ref.at[pl.ds(g * quads, quads)], out_sem.at[g]
        )
        store.start()
        stores.append(store)
    for store in stores:
        store.wait()


def on_device(facets, correction, window, offsets, phases, coverage):
    facet_count = lax.axis_size("facet")
    sub_count = lax.axis_size("sub")
    pair_count = lax.axis_size("wa")
    row_count, length = facets.shape[1], facets.shape[3]
    width = window.shape[0]
    subs = offsets.shape[0]
    rows = row_count // (sub_count * pair_count)
    low = length // width
    quads = width // low
    if rows != facet_count * quads or low * quads != width:
        raise ValueError("unsupported sizes")
    span = subs * quads
    total = facet_count * width
    lines = length // width
    image = facets.reshape(row_count, 2, lines, width)
    image = jnp.transpose(image, (0, 2, 1, 3)).reshape(row_count, 2 * lines, width)
    twist, outer, turn, pick, unit, unit_t, outer_t = tables(length, width, facet_count)
    vmem = pl.BlockSpec(memory_space=pltpu.VMEM)
    smem = pl.BlockSpec(memory_space=pltpu.SMEM)
    far = pl.BlockSpec(memory_space=pltpu.HBM)
    others = sub_count * pair_count - 1
    dma = pltpu.SemaphoreType.DMA
    block = (facet_count, span, 2 * width)
    gains = correction.reshape(lines, width)
    window = window.reshape(1, width)
    first_tables = [outer, turn, pick, unit, unit_t]
    returned = pl.pallas_call(
        functools.partial(kernel, (facet_count, sub_count, pair_count)),
        out_shape=pltpu.VMEM(block, F32),
        in_specs=[smem, far] + [vmem] * 5 + [far] * len(first_tables),
        out_specs=vmem,
        scratch_shapes=[
            pltpu.VMEM((rows, 2 * lines, width), F32),
            pltpu.VMEM((2 * lines, width), F32),
            pltpu.VMEM(block, F32),
            pltpu.VMEM(block, F32),
            pltpu.VMEM(block, F32),
            pltpu.VMEM(block, F32),
            pltpu.VMEM((sub_count, pair_count) + coverage.shape, jnp.int32),
            pltpu.VMEM((coverage.shape[1] * pair_count * span, total), F32),
            pltpu.VMEM((pair_count,) + phases.shape, F32),
            dma,
            dma((facet_count - 1,)),
            dma((facet_count - 1,)),
            dma((facet_count - 1,)),
            dma((facet_count - 1,)),
            dma((others,)),
            dma((others,)),
            dma((max(pair_count - 1, 1),)),
            dma((max(pair_count - 1, 1),)),
        ]
        + [pltpu.VMEM(table.shape, F32) for table in first_tables]
        + [dma((len(first_tables),))],
        compiler_params=pltpu.CompilerParams(
            collective_id=0, has_side_effects=True, vmem_limit_bytes=55 * 1024 * 1024
        ),
    )(offsets, image, gains, window, phases, coverage, jnp.asarray(twist), *map(jnp.asarray, first_tables))
    second_tables = [unit_t, pick, turn, outer_t]
    result = pl.pallas_call(
        inverse_kernel,
        out_shape=jax.ShapeDtypeStruct((rows, 2 * lines, width), F32),
        in_specs=[smem] + [vmem] * 3 + [pl.BlockSpec(memory_space=pl.ANY)] * len(second_tables),
        out_specs=far,
        scratch_shapes=[
            pltpu.VMEM((2 * lines, width), F32),
            pltpu.VMEM((4 * span, total), F32),
            pltpu.VMEM((rows, 2 * lines, width), F32),
        ]
        + [pltpu.VMEM(table.shape, F32) for table in second_tables]
        + [dma((len(second_tables),)), dma((facet_count,))],
        compiler_params=pltpu.CompilerParams(vmem_limit_bytes=48 * 1024 * 1024),
    )(offsets, returned, gains, window, *map(jnp.asarray, second_tables))
    result = jnp.transpose(result.reshape(rows, lines, 2, width), (0, 2, 1, 3))
    return result.reshape(1, rows, 2, length)


def solution(mesh):
    return jax.shard_map(
        on_device,
        mesh=mesh,
        in_specs=(
            P("facet", None, None, None),
            P("facet", None),
            P(),
            P(),
            P("wa", None),
            P("sub", "wa", None),
        ),
        out_specs=P("facet", ("sub", "wa"), None, None),
        check_vma=False,
    )
```

```python
import functools
import math

import jax
import jax.numpy as jnp
import numpy as np
from jax import lax
from jax.experimental import pallas as pl
from jax.experimental.pallas import tpu as pltpu
from jax.sharding import PartitionSpec as P

MESH = pl.DeviceIdType.MESH
F32 = jnp.float32
BF16 = jnp.bfloat16


def complex_rows(matrix):
    return np.block([[matrix.real, matrix.imag], [-matrix.imag, matrix.real]])


def tables(length, width, facet_count):
    low = length // width
    quads = width // low
    a = np.arange(width)
    b = np.arange(low)
    dft = np.exp(-2j * np.pi * np.outer(a, a) / width)
    order = (a.reshape(width // quads, quads).T).reshape(-1)
    picked = dft[:, order]
    spread = np.zeros((2, width, width, 2))
    spread[0, :, :, 0] = picked.real
    spread[0, :, :, 1] = -picked.imag
    spread[1, :, :, 0] = picked.imag
    spread[1, :, :, 1] = picked.real
    outer = spread.reshape(2 * width, 2 * width)
    turn = np.tile(np.exp(-2j * np.pi * np.outer(a, b) / length), (1, quads))
    turn = np.stack([turn.real, turn.imag]).astype(np.float32)
    fine = np.exp(-2j * np.pi * np.outer(b, b) / low) * length**-0.5
    pick = np.zeros((low, 2, quads, 2, quads, low))
    for quad in range(quads):
        pick[:, 0, quad, 0, quad] = fine.real
        pick[:, 0, quad, 1, quad] = -fine.imag
        pick[:, 1, quad, 0, quad] = fine.imag
        pick[:, 1, quad, 1, quad] = fine.real
    pick = pick.reshape(low, 2 * quads, 2 * width).astype(np.float32)
    unit = complex_rows(np.conj(dft) * width**-0.5)
    twist = np.exp(-2j * np.pi * np.outer(np.arange(facet_count), a) / (facet_count * width))
    twist = np.stack([twist.real, twist.imag]).astype(np.float32)
    outer, unit = outer.astype(np.float32), unit.astype(np.float32)
    return twist, outer, turn, pick, unit, unit.T, outer.T


def split(value):
    high = value.astype(BF16)
    return high, (value - high.astype(F32)).astype(BF16)


def mm(left, right, transposed=False):
    axis = 1 if transposed else 0
    one = jnp.concatenate([left[0], left[0], left[1]], axis=1)
    two = jnp.concatenate([right[0], right[1], right[0]], axis=axis)
    return lax.dot_general(one, two, (((1,), (axis,)), ((), ())), preferred_element_type=F32)


def cos_sin(value):
    turns = jnp.floor(value * (2.0 / math.pi) + 0.5)
    rest = (value - turns * 1.5703125) - turns * (math.pi / 2 - 1.5703125)
    square = rest * rest
    sine = rest + rest * square * (
        -1.0 / 6 + square * (1.0 / 120 + square * (-1.0 / 5040 + square * (1.0 / 362880)))
    )
    cosine = 1.0 + square * (
        -0.5 + square * (1.0 / 24 + square * (-1.0 / 720 + square * (1.0 / 40320)))
    )
    odd = jnp.abs(turns) == 1.0
    sign_cos = jnp.where(turns == 1.0, -1.0, jnp.where(jnp.abs(turns) == 2.0, -1.0, 1.0))
    sign_sin = jnp.where(turns == -1.0, -1.0, jnp.where(jnp.abs(turns) == 2.0, -1.0, 1.0))
    return jnp.where(odd, sine, cosine) * sign_cos, jnp.where(odd, cosine, sine) * sign_sin


def radix(parts, sign):
    count = len(parts)
    if count == 1:
        return parts
    if count % 2:
        raise ValueError("odd length")
    even = radix(parts[0::2], sign)
    odd = radix(parts[1::2], sign)
    first, second = [], []
    for k in range(count // 2):
        real, imag = odd[k]
        if 4 * k == count:
            real, imag = (-imag, real) if sign > 0 else (imag, -real)
        elif k:
            c = math.cos(2 * math.pi * k / count)
            s = sign * math.sin(2 * math.pi * k / count)
            real, imag = real * c - imag * s, real * s + imag * c
        first.append((even[k][0] + real, even[k][1] + imag))
        second.append((even[k][0] - real, even[k][1] - imag))
    return first + second


def swap_blocks(blocks, low):
    blocks = list(blocks)
    count = len(blocks)
    width = count * low
    lane = lax.broadcasted_iota(jnp.int32, blocks[0].shape, 1)
    step = count // 2
    while step:
        shift = step * low
        upper = (lane & shift) != 0
        for i in range(count):
            if i & step:
                continue
            one, two = blocks[i], blocks[i + step]
            blocks[i] = jnp.where(upper, pltpu.roll(two, shift, 1), one)
            blocks[i + step] = jnp.where(upper, two, pltpu.roll(one, width - shift, 1))
        step //= 2
    return blocks


def offset_tables(offsets_ref, window_ref, quads):
    width = window_ref.shape[1]
    subs = offsets_ref.shape[0]
    span = subs * quads
    starts = [offsets_ref[s] for s in range(subs)]
    first_q = [start // width for start in starts]
    rests = [start & (width - 1) for start in starts]
    row = lax.broadcasted_iota(jnp.int32, (span, width), 0)
    offset_rows = jnp.zeros((span, width), jnp.int32)
    window_full = jnp.broadcast_to(window_ref[...], (8, width))
    window_rows = jnp.zeros((span, width), F32)
    for s in range(subs):
        offset_rows = jnp.where(row >= s * quads, rests[s], offset_rows)
        moved = pltpu.roll(window_full, rests[s], 1)[0:1]
        window_rows = jnp.where(row >= s * quads, moved, window_rows)
    span_lane = lax.broadcasted_iota(jnp.int32, (span, width), 1)
    steps = ((offset_rows * span_lane + width // 2) & (width - 1)) - width // 2
    turn_cos, turn_sin = cos_sin(steps.astype(F32) * (2.0 * math.pi / width))
    return first_q, turn_cos, turn_sin, span_lane >= offset_rows, window_rows


def gather_pick(first_q, pick_ref):
    low = pick_ref.shape[0]
    picked = []
    for q in first_q:
        picked.append(pick_ref[q])
        picked.append(pick_ref[lax.rem(q + 1, low)])
    return split(jnp.concatenate(picked, axis=0))


def kernel(
    geometry,
    offsets_ref,
    facets_ref,
    correction_ref,
    window_ref,
    phases_ref,
    coverage_ref,
    twist_ref,
    outer_far,
    turn_far,
    pick_far,
    unit_far,
    unit_t_far,
    returned,
    image,
    gain,
    cut,
    sent,
    arrived,
    back,
    ordered,
    counts,
    expanded,
    screens,
    load_sem,
    fwd_send,
    fwd_recv,
    bwd_send,
    bwd_recv,
    cov_send,
    cov_recv,
    ph_send,
    ph_recv,
    outer_ref,
    turn_ref,
    pick_ref,
    unit_ref,
    unit_t_ref,
    table_sem,
):
    facet_count, sub_count, pair_count = geometry
    facet = lax.axis_index("facet")
    sub = lax.axis_index("sub")
    pair = lax.axis_index("wa")
    rows = image.shape[0]
    width = window_ref.shape[1]
    subs = offsets_ref.shape[0]
    low = pick_ref.shape[0]
    quads = width // low
    length = low * width
    span = subs * quads
    per_sub, per_wa = coverage_ref.shape[0], coverage_ref.shape[1]
    planes = per_wa * pair_count
    total = facet_count * width

    facet_mates = [lax.rem(facet + d, facet_count) for d in range(1, facet_count)]
    hops = [(ds, dw) for ds in range(sub_count) for dw in range(pair_count) if ds or dw]
    barrier = pltpu.get_barrier_semaphore()
    for mate in facet_mates:
        pl.semaphore_signal(barrier, inc=1, device_id={"facet": mate}, device_id_type=MESH)
    grid_mates = [(lax.rem(sub + ds, sub_count), lax.rem(pair + dw, pair_count)) for ds, dw in hops]
    for mate_sub, mate_pair in grid_mates:
        pl.semaphore_signal(
            barrier, inc=1, device_id={"sub": mate_sub, "wa": mate_pair}, device_id_type=MESH
        )
    load = pltpu.make_async_copy(
        facets_ref.at[pl.ds((sub * pair_count + pair) * rows, rows)], image, load_sem
    )
    load.start()
    fetches = {}
    for i, (name, far, near) in enumerate(
        (
            ("outer", outer_far, outer_ref),
            ("turn", turn_far, turn_ref),
            ("pick", pick_far, pick_ref),
            ("unit", unit_far, unit_ref),
            ("unit_t", unit_t_far, unit_t_ref),
        )
    ):
        fetches[name] = pltpu.make_async_copy(far, near, table_sem.at[i])
        fetches[name].start()

    def gathers():
        copies = []
        for i, (mate_sub, mate_pair) in enumerate(grid_mates):
            copies.append(
                pltpu.make_async_remote_copy(
                    src_ref=ordered,
                    dst_ref=counts.at[sub, pair],
                    send_sem=cov_send.at[i],
                    recv_sem=cov_recv.at[i],
                    device_id={"sub": mate_sub, "wa": mate_pair},
                    device_id_type=MESH,
                )
            )
        for d in range(1, pair_count):
            copies.append(
                pltpu.make_async_remote_copy(
                    src_ref=phases_ref,
                    dst_ref=screens.at[pair],
                    send_sem=ph_send.at[d - 1],
                    recv_sem=ph_recv.at[d - 1],
                    device_id={"wa": lax.rem(pair + d, pair_count)},
                    device_id_type=MESH,
                )
            )
        return copies

    def greet():
        pl.semaphore_wait(barrier, len(facet_mates) + len(hops))
        for copy in gathers():
            copy.start()

    source = lax.broadcasted_iota(jnp.int32, (total, total), 0)
    inner = lax.broadcasted_iota(jnp.int32, (1, width), 1) * facet_count
    wanted = jnp.concatenate([inner + k for k in range(facet_count)], axis=1)
    chooser = jnp.where(source == wanted, 1.0, 0.0).astype(BF16)
    own = [coverage_ref[i].astype(F32) for i in range(per_sub)]
    own = jnp.dot(
        jnp.concatenate(own, axis=0).astype(BF16), chooser, preferred_element_type=F32
    )
    ordered[...] = own * (1.0 / (facet_count * planes))
    counts[sub, pair] = ordered[...]
    screens[pair] = phases_ref[...]

    gain[pl.ds(0, low, stride=2), :] = correction_ref[...]
    gain[pl.ds(1, low, stride=2), :] = correction_ref[...]
    first_q, turn_cos, turn_sin, is_first, window_rows = offset_tables(
        offsets_ref, window_ref, quads
    )
    fetches["pick"].wait()
    picked = gather_pick(first_q, pick_ref)

    pl.when((sub != 0) & (sub == sub_count - 1))(greet)
    load.wait()
    gains = gain[...]
    groups = []
    for g in range(facet_count):
        blocks = [image[g * quads + i] * gains for i in range(quads)]
        groups.append(jnp.concatenate(swap_blocks(blocks, low), axis=0))
    spread = jnp.concatenate(groups, axis=1)
    fetches["outer"].wait()
    mixed = mm(split(outer_ref[...]), split(spread))
    pl.when((sub != 0) & (sub != sub_count - 1))(greet)
    fetches["turn"].wait()
    table_cos, table_sin = turn_ref[0], turn_ref[1]
    turned = []
    for g in range(facet_count):
        real = mixed[:width, g * width : (g + 1) * width]
        imag = mixed[width:, g * width : (g + 1) * width]
        turned.append(
            jnp.concatenate(
                [real * table_cos - imag * table_sin, real * table_sin + imag * table_cos], axis=1
            )
        )
    turned = jnp.concatenate(turned, axis=0)
    spectrum = mm(picked, split(turned), transposed=True)

    pl.when(sub == 0)(greet)
    for s in range(subs):
        here = slice(s * quads, (s + 1) * quads)
        base = s * 4 * quads
        keep = is_first[here]
        win = window_rows[here]
        for g in range(facet_count):
            cols = slice(g * width, (g + 1) * width)
            for c in range(2):
                one = spectrum[base + c * quads : base + (c + 1) * quads, cols]
                two = spectrum[base + (2 + c) * quads : base + (3 + c) * quads, cols]
                cut[g, here, c * width : (c + 1) * width] = jnp.where(keep, one, two) * win
    fetches["unit"].wait()
    unit = split(unit_ref[...])
    halves, part = sent.shape[0], sent.shape[2]
    forward = []
    for h in range(halves):
        rows_h = slice(h * part, (h + 1) * part)
        mixed = mm(split(cut[:, rows_h].reshape(facet_count * part, 2 * width)), unit)
        tc, ts = turn_cos[rows_h], turn_sin[rows_h]
        for g in range(facet_count):
            real = mixed[g * part : (g + 1) * part, :width]
            imag = mixed[g * part : (g + 1) * part, width:]
            sent[h, g, :, :width] = real * tc + imag * ts
            sent[h, g, :, width:] = imag * tc - real * ts
        copies = []
        for i, mate in enumerate(facet_mates):
            copy = pltpu.make_async_remote_copy(
                src_ref=sent.at[h, mate],
                dst_ref=arrived.at[h, facet],
                send_sem=fwd_send.at[h, i],
                recv_sem=fwd_recv.at[h, i],
                device_id={"facet": mate},
                device_id_type=MESH,
            )
            copy.start()
            copies.append(copy)
        forward.append(copies)
        arrived[h, facet] = sent[h, facet]
    fetches["unit_t"].wait()
    unit_t = split(unit_t_ref[...])

    for copy in gathers():
        copy.wait()
    for owner in range(sub_count):
        for p in range(pair_count):
            for i in range(per_sub):
                for j in range(per_wa):
                    at = (p * per_wa + j) * span + (owner * per_sub + i) * quads
                    row = counts[owner, p, i * per_wa + j : i * per_wa + j + 1]
                    expanded[at : at + quads, :] = jnp.broadcast_to(row, (quads, total))
    kernels = []
    for p in range(pair_count):
        screen = screens[p]
        cos_all, sin_all = cos_sin(screen)
        for j in range(per_wa):
            kernels.append((cos_all[j : j + 1], sin_all[j : j + 1]))
    twist = [(twist_ref[0, k : k + 1], twist_ref[1, k : k + 1]) for k in range(facet_count)]

    backward = []
    for h in range(halves):
        for copy in forward[h]:
            copy.wait()
        pieces = [[] for _ in range(facet_count)]
        for w in range(planes):
            parts = []
            for f in range(facet_count):
                cols = slice(f * width, (f + 1) * width)
                kc, ks = kernels[w][0][:, cols], kernels[w][1][:, cols]
                real, imag = arrived[h, f, :, :width], arrived[h, f, :, width:]
                parts.append((real * kc - imag * ks, real * ks + imag * kc))
            for k, (real, imag) in enumerate(radix(parts, -1)):
                tc, ts = twist[k]
                pieces[k].append(
                    jnp.concatenate([real * tc - imag * ts, real * ts + imag * tc], axis=1)
                )
        stacked = jnp.concatenate([piece for group in pieces for piece in group], axis=0)
        grid = mm(split(stacked), unit_t)
        scale = jnp.concatenate(
            [
                expanded[w * span + h * part : w * span + (h + 1) * part, k * width : (k + 1) * width]
                for k in range(facet_count)
                for w in range(planes)
            ],
            axis=0,
        )
        weighted = grid * jnp.concatenate([scale, scale], axis=1)
        image_side = mm(split(weighted), unit)
        sums = [None] * facet_count
        for w in range(planes):
            parts = []
            for k in range(facet_count):
                at = (k * planes + w) * part
                real = image_side[at : at + part, :width]
                imag = image_side[at : at + part, width:]
                tc, ts = twist[k]
                parts.append((real * tc + imag * ts, imag * tc - real * ts))
            for f, (real, imag) in enumerate(radix(parts, 1)):
                cols = slice(f * width, (f + 1) * width)
                kc, ks = kernels[w][0][:, cols], kernels[w][1][:, cols]
                term = (real * kc + imag * ks, imag * kc - real * ks)
                sums[f] = term if w == 0 else (sums[f][0] + term[0], sums[f][1] + term[1])
        for f in range(facet_count):
            back[h, f, :, :width] = sums[f][0]
            back[h, f, :, width:] = sums[f][1]
        for i, mate in enumerate(facet_mates):
            copy = pltpu.make_async_remote_copy(
                src_ref=back.at[h, mate],
                dst_ref=returned.at[h, facet],
                send_sem=bwd_send.at[h, i],
                recv_sem=bwd_recv.at[h, i],
                device_id={"facet": mate},
                device_id_type=MESH,
            )
            copy.start()
            backward.append(copy)
        returned[h, facet] = back[h, facet]
    for copy in backward:
        copy.wait()


def inverse_kernel(
    offsets_ref,
    returned,
    correction_ref,
    window_ref,
    unit_t_far,
    pick_far,
    turn_far,
    outer_t_far,
    out_ref,
    gain,
    segments,
    image,
    unit_t_ref,
    pick_ref,
    turn_ref,
    outer_t_ref,
    table_sem,
    out_sem,
):
    halves, facet_count, part, double = returned.shape
    span = halves * part
    width = double // 2
    subs = offsets_ref.shape[0]
    low = pick_ref.shape[0]
    quads = width // low
    fetches = {}
    for i, (name, far, near) in enumerate(
        (
            ("unit_t", unit_t_far, unit_t_ref),
            ("pick", pick_far, pick_ref),
            ("turn", turn_far, turn_ref),
            ("outer_t", outer_t_far, outer_t_ref),
        )
    ):
        fetches[name] = pltpu.make_async_copy(far, near, table_sem.at[i])
        fetches[name].start()
    gain[pl.ds(0, low, stride=2), :] = correction_ref[...]
    gain[pl.ds(1, low, stride=2), :] = correction_ref[...]
    gains = gain[...]
    first_q, turn_cos, turn_sin, is_first, window_rows = offset_tables(
        offsets_ref, window_ref, quads
    )
    unturned = []
    for g in range(facet_count):
        whole = jnp.concatenate([returned[h, g] for h in range(halves)], axis=0)
        real, imag = whole[:, :width], whole[:, width:]
        unturned.append(
            jnp.concatenate(
                [real * turn_cos - imag * turn_sin, real * turn_sin + imag * turn_cos], axis=1
            )
        )
    unturned = jnp.concatenate(unturned, axis=0)
    fetches["unit_t"].wait()
    mixed = mm(split(unturned), split(unit_t_ref[...]))
    win_first = jnp.where(is_first, window_rows, 0.0)
    win_second = jnp.where(is_first, 0.0, window_rows)
    for g in range(facet_count):
        cols = slice(g * width, (g + 1) * width)
        for c in range(2):
            part = mixed[g * span : (g + 1) * span, c * width : (c + 1) * width]
            for h, win in enumerate((win_first, win_second)):
                masked = part * win
                for s in range(subs):
                    at = (4 * s + 2 * h + c) * quads
                    segments[at : at + quads, cols] = masked[s * quads : (s + 1) * quads]
    columns = jnp.concatenate(
        [segments[:, g * width : (g + 1) * width].T for g in range(facet_count)], axis=0
    )
    fetches["pick"].wait()
    fine = mm(split(columns), gather_pick(first_q, pick_ref))
    fetches["turn"].wait()
    table_cos, table_sin = turn_ref[0], turn_ref[1]
    reals, imags = [], []
    for g in range(facet_count):
        real = fine[g * width : (g + 1) * width, :width]
        imag = fine[g * width : (g + 1) * width, width:]
        reals.append(real * table_cos + imag * table_sin)
        imags.append(imag * table_cos - real * table_sin)
    joined = jnp.concatenate(
        [jnp.concatenate(reals, axis=1), jnp.concatenate(imags, axis=1)], axis=0
    )
    fetches["outer_t"].wait()
    spread = mm(split(outer_t_ref[...]), split(joined))
    part = 2 * width // quads
    stores = []
    for g in range(facet_count):
        cols = slice(g * width, (g + 1) * width)
        blocks = [spread[i * part : (i + 1) * part, cols] for i in range(quads)]
        for i, block in enumerate(swap_blocks(blocks, low)):
            image[g * quads + i] = block * gains
        store = pltpu.make_async_copy(
            image.at[pl.ds(g * quads, quads)], out_ref.at[pl.ds(g * quads, quads)], out_sem.at[g]
        )
        store.start()
        stores.append(store)
    for store in stores:
        store.wait()


def on_device(facets, correction, window, offsets, phases, coverage):
    facet_count = lax.axis_size("facet")
    sub_count = lax.axis_size("sub")
    pair_count = lax.axis_size("wa")
    row_count, length = facets.shape[1], facets.shape[3]
    width = window.shape[0]
    subs = offsets.shape[0]
    rows = row_count // (sub_count * pair_count)
    low = length // width
    quads = width // low
    if rows != facet_count * quads or low * quads != width:
        raise ValueError("unsupported sizes")
    span = subs * quads
    total = facet_count * width
    lines = length // width
    image = facets.reshape(row_count, 2, lines, width)
    image = jnp.transpose(image, (0, 2, 1, 3)).reshape(row_count, 2 * lines, width)
    twist, outer, turn, pick, unit, unit_t, outer_t = tables(length, width, facet_count)
    vmem = pl.BlockSpec(memory_space=pltpu.VMEM)
    smem = pl.BlockSpec(memory_space=pltpu.SMEM)
    far = pl.BlockSpec(memory_space=pltpu.HBM)
    others = sub_count * pair_count - 1
    dma = pltpu.SemaphoreType.DMA
    halves = 2 if subs % 2 == 0 and (span // 2) % 8 == 0 else 1
    block = (halves, facet_count, span // halves, 2 * width)
    gains = correction.reshape(lines, width)
    held = coverage.shape[0] * coverage.shape[1]
    window = window.reshape(1, width)
    first_tables = [outer, turn, pick, unit, unit_t]
    returned = pl.pallas_call(
        functools.partial(kernel, (facet_count, sub_count, pair_count)),
        out_shape=pltpu.VMEM(block, F32),
        in_specs=[smem, far] + [vmem] * 5 + [far] * len(first_tables),
        out_specs=vmem,
        scratch_shapes=[
            pltpu.VMEM((rows, 2 * lines, width), F32),
            pltpu.VMEM((2 * lines, width), F32),
            pltpu.VMEM((facet_count, span, 2 * width), F32),
            pltpu.VMEM(block, F32),
            pltpu.VMEM(block, F32),
            pltpu.VMEM(block, F32),
            pltpu.VMEM((held, total), F32),
            pltpu.VMEM((sub_count, pair_count, held, total), F32),
            pltpu.VMEM((coverage.shape[1] * pair_count * span, total), F32),
            pltpu.VMEM((pair_count,) + phases.shape, F32),
            dma,
            dma((halves, facet_count - 1)),
            dma((halves, facet_count - 1)),
            dma((halves, facet_count - 1)),
            dma((halves, facet_count - 1)),
            dma((others,)),
            dma((others,)),
            dma((max(pair_count - 1, 1),)),
            dma((max(pair_count - 1, 1),)),
        ]
        + [pltpu.VMEM(table.shape, F32) for table in first_tables]
        + [dma((len(first_tables),))],
        compiler_params=pltpu.CompilerParams(
            collective_id=0, has_side_effects=True, vmem_limit_bytes=55 * 1024 * 1024
        ),
    )(offsets, image, gains, window, phases, coverage, jnp.asarray(twist), *map(jnp.asarray, first_tables))
    second_tables = [unit_t, pick, turn, outer_t]
    result = pl.pallas_call(
        inverse_kernel,
        out_shape=jax.ShapeDtypeStruct((rows, 2 * lines, width), F32),
        in_specs=[smem] + [vmem] * 3 + [pl.BlockSpec(memory_space=pl.ANY)] * len(second_tables),
        out_specs=far,
        scratch_shapes=[
            pltpu.VMEM((2 * lines, width), F32),
            pltpu.VMEM((4 * span, total), F32),
            pltpu.VMEM((rows, 2 * lines, width), F32),
        ]
        + [pltpu.VMEM(table.shape, F32) for table in second_tables]
        + [dma((len(second_tables),)), dma((facet_count,))],
        compiler_params=pltpu.CompilerParams(vmem_limit_bytes=48 * 1024 * 1024),
    )(offsets, returned, gains, window, *map(jnp.asarray, second_tables))
    result = jnp.transpose(result.reshape(rows, lines, 2, width), (0, 2, 1, 3))
    return result.reshape(1, rows, 2, length)


def solution(mesh):
    return jax.shard_map(
        on_device,
        mesh=mesh,
        in_specs=(
            P("facet", None, None, None),
            P("facet", None),
            P(),
            P(),
            P("wa", None),
            P("sub", "wa", None),
        ),
        out_specs=P("facet", ("sub", "wa"), None, None),
        check_vma=False,
    )
```

```python
import functools
import math

import jax
import jax.numpy as jnp
import numpy as np
from jax import lax
from jax.experimental import pallas as pl
from jax.experimental.pallas import tpu as pltpu
from jax.sharding import PartitionSpec as P

MESH = pl.DeviceIdType.MESH
F32 = jnp.float32
BF16 = jnp.bfloat16


def complex_rows(matrix):
    return np.block([[matrix.real, matrix.imag], [-matrix.imag, matrix.real]])


def tables(length, width, facet_count):
    low = length // width
    quads = width // low
    a = np.arange(width)
    b = np.arange(low)
    dft = np.exp(-2j * np.pi * np.outer(a, a) / width)
    order = (a.reshape(width // quads, quads).T).reshape(-1)
    picked = dft[:, order]
    spread = np.zeros((2, width, width, 2))
    spread[0, :, :, 0] = picked.real
    spread[0, :, :, 1] = -picked.imag
    spread[1, :, :, 0] = picked.imag
    spread[1, :, :, 1] = picked.real
    outer = spread.reshape(2 * width, 2 * width)
    turn = np.tile(np.exp(-2j * np.pi * np.outer(a, b) / length), (1, quads))
    turn = np.stack([turn.real, turn.imag]).astype(np.float32)
    fine = np.exp(-2j * np.pi * np.outer(b, b) / low) * length**-0.5
    pick = np.zeros((low, 2, quads, 2, quads, low))
    for quad in range(quads):
        pick[:, 0, quad, 0, quad] = fine.real
        pick[:, 0, quad, 1, quad] = -fine.imag
        pick[:, 1, quad, 0, quad] = fine.imag
        pick[:, 1, quad, 1, quad] = fine.real
    pick = pick.reshape(low, 2 * quads, 2 * width).astype(np.float32)
    unit = complex_rows(np.conj(dft) * width**-0.5)
    twist = np.exp(-2j * np.pi * np.outer(np.arange(facet_count), a) / (facet_count * width))
    twist = np.stack([twist.real, twist.imag]).astype(np.float32)
    outer, unit = outer.astype(np.float32), unit.astype(np.float32)
    return twist, outer, turn, pick, unit, unit.T, outer.T


def split(value):
    high = value.astype(BF16)
    return high, (value - high.astype(F32)).astype(BF16)


def mm(left, right, transposed=False):
    axis = 1 if transposed else 0
    one = jnp.concatenate([left[0], left[0], left[1]], axis=1)
    two = jnp.concatenate([right[0], right[1], right[0]], axis=axis)
    return lax.dot_general(one, two, (((1,), (axis,)), ((), ())), preferred_element_type=F32)


def cos_sin(value):
    turns = jnp.floor(value * (2.0 / math.pi) + 0.5)
    rest = (value - turns * 1.5703125) - turns * (math.pi / 2 - 1.5703125)
    square = rest * rest
    sine = rest + rest * square * (
        -1.0 / 6 + square * (1.0 / 120 + square * (-1.0 / 5040 + square * (1.0 / 362880)))
    )
    cosine = 1.0 + square * (
        -0.5 + square * (1.0 / 24 + square * (-1.0 / 720 + square * (1.0 / 40320)))
    )
    odd = jnp.abs(turns) == 1.0
    sign_cos = jnp.where(turns == 1.0, -1.0, jnp.where(jnp.abs(turns) == 2.0, -1.0, 1.0))
    sign_sin = jnp.where(turns == -1.0, -1.0, jnp.where(jnp.abs(turns) == 2.0, -1.0, 1.0))
    return jnp.where(odd, sine, cosine) * sign_cos, jnp.where(odd, cosine, sine) * sign_sin


def radix(parts, sign):
    count = len(parts)
    if count == 1:
        return parts
    if count % 2:
        raise ValueError("odd length")
    even = radix(parts[0::2], sign)
    odd = radix(parts[1::2], sign)
    first, second = [], []
    for k in range(count // 2):
        real, imag = odd[k]
        if 4 * k == count:
            real, imag = (-imag, real) if sign > 0 else (imag, -real)
        elif k:
            c = math.cos(2 * math.pi * k / count)
            s = sign * math.sin(2 * math.pi * k / count)
            real, imag = real * c - imag * s, real * s + imag * c
        first.append((even[k][0] + real, even[k][1] + imag))
        second.append((even[k][0] - real, even[k][1] - imag))
    return first + second


def swap_blocks(blocks, low):
    blocks = list(blocks)
    count = len(blocks)
    width = count * low
    lane = lax.broadcasted_iota(jnp.int32, blocks[0].shape, 1)
    step = count // 2
    while step:
        shift = step * low
        upper = (lane & shift) != 0
        for i in range(count):
            if i & step:
                continue
            one, two = blocks[i], blocks[i + step]
            blocks[i] = jnp.where(upper, pltpu.roll(two, shift, 1), one)
            blocks[i + step] = jnp.where(upper, two, pltpu.roll(one, width - shift, 1))
        step //= 2
    return blocks


def offset_tables(offsets_ref, window_ref, quads):
    width = window_ref.shape[1]
    subs = offsets_ref.shape[0]
    span = subs * quads
    starts = [offsets_ref[s] for s in range(subs)]
    first_q = [start // width for start in starts]
    rests = [start & (width - 1) for start in starts]
    row = lax.broadcasted_iota(jnp.int32, (span, width), 0)
    offset_rows = jnp.zeros((span, width), jnp.int32)
    window_full = jnp.broadcast_to(window_ref[...], (8, width))
    window_rows = jnp.zeros((span, width), F32)
    for s in range(subs):
        offset_rows = jnp.where(row >= s * quads, rests[s], offset_rows)
        moved = pltpu.roll(window_full, rests[s], 1)[0:1]
        window_rows = jnp.where(row >= s * quads, moved, window_rows)
    span_lane = lax.broadcasted_iota(jnp.int32, (span, width), 1)
    steps = ((offset_rows * span_lane + width // 2) & (width - 1)) - width // 2
    turn_cos, turn_sin = cos_sin(steps.astype(F32) * (2.0 * math.pi / width))
    return first_q, turn_cos, turn_sin, span_lane >= offset_rows, window_rows


def gather_pick(first_q, pick_ref):
    low = pick_ref.shape[0]
    picked = []
    for q in first_q:
        picked.append(pick_ref[q])
        picked.append(pick_ref[lax.rem(q + 1, low)])
    return split(jnp.concatenate(picked, axis=0))


def kernel(
    geometry,
    offsets_ref,
    facets_ref,
    correction_ref,
    window_ref,
    phases_ref,
    coverage_ref,
    twist_ref,
    outer_far,
    turn_far,
    pick_far,
    unit_far,
    unit_t_far,
    returned,
    image,
    gain,
    cut,
    sent,
    arrived,
    back,
    ordered,
    counts,
    expanded,
    screens,
    load_sem,
    fwd_send,
    fwd_recv,
    bwd_send,
    bwd_recv,
    cov_send,
    cov_recv,
    ph_send,
    ph_recv,
    outer_ref,
    turn_ref,
    pick_ref,
    unit_ref,
    unit_t_ref,
    table_sem,
):
    facet_count, sub_count, pair_count = geometry
    facet = lax.axis_index("facet")
    sub = lax.axis_index("sub")
    pair = lax.axis_index("wa")
    rows = image.shape[0]
    width = window_ref.shape[1]
    subs = offsets_ref.shape[0]
    low = pick_ref.shape[0]
    quads = width // low
    length = low * width
    span = subs * quads
    per_sub, per_wa = coverage_ref.shape[0], coverage_ref.shape[1]
    planes = per_wa * pair_count
    total = facet_count * width

    facet_mates = [lax.rem(facet + d, facet_count) for d in range(1, facet_count)]
    hops = [(ds, dw) for ds in range(sub_count) for dw in range(pair_count) if ds or dw]
    barrier = pltpu.get_barrier_semaphore()
    for mate in facet_mates:
        pl.semaphore_signal(barrier, inc=1, device_id={"facet": mate}, device_id_type=MESH)
    grid_mates = [(lax.rem(sub + ds, sub_count), lax.rem(pair + dw, pair_count)) for ds, dw in hops]
    for mate_sub, mate_pair in grid_mates:
        pl.semaphore_signal(
            barrier, inc=1, device_id={"sub": mate_sub, "wa": mate_pair}, device_id_type=MESH
        )
    pair_size = 2 if facet_count % 2 == 0 else 1
    pairs = facet_count // pair_size
    order = [lax.rem(facet // pair_size + 1 + step, pairs) for step in range(pairs)]
    slots = [
        order[step] * pair_size + lax.rem(facet + g, pair_size)
        for step in range(pairs - 1)
        for g in range(pair_size)
    ]
    near = order[-1] * pair_size
    far_first = slots + [near + lax.rem(facet + 1 + g, pair_size) for g in range(pair_size - 1)]
    batch = pair_size * quads
    first_row = (sub * pair_count + pair) * rows
    loads = []
    for step, which in enumerate(order):
        load = pltpu.make_async_copy(
            facets_ref.at[pl.ds(first_row + which * batch, batch)],
            image.at[pl.ds(step * batch, batch)],
            load_sem.at[step],
        )
        load.start()
        loads.append(load)
    fetches = {}
    for i, (name, far, near) in enumerate(
        (
            ("outer", outer_far, outer_ref),
            ("turn", turn_far, turn_ref),
            ("pick", pick_far, pick_ref),
            ("unit", unit_far, unit_ref),
            ("unit_t", unit_t_far, unit_t_ref),
        )
    ):
        fetches[name] = pltpu.make_async_copy(far, near, table_sem.at[i])
        fetches[name].start()

    def gathers():
        copies = []
        for i, (mate_sub, mate_pair) in enumerate(grid_mates):
            copies.append(
                pltpu.make_async_remote_copy(
                    src_ref=ordered,
                    dst_ref=counts.at[sub, pair],
                    send_sem=cov_send.at[i],
                    recv_sem=cov_recv.at[i],
                    device_id={"sub": mate_sub, "wa": mate_pair},
                    device_id_type=MESH,
                )
            )
        for d in range(1, pair_count):
            copies.append(
                pltpu.make_async_remote_copy(
                    src_ref=phases_ref,
                    dst_ref=screens.at[pair],
                    send_sem=ph_send.at[d - 1],
                    recv_sem=ph_recv.at[d - 1],
                    device_id={"wa": lax.rem(pair + d, pair_count)},
                    device_id_type=MESH,
                )
            )
        return copies

    def greet():
        pl.semaphore_wait(barrier, len(facet_mates) + len(hops))
        for copy in gathers():
            copy.start()

    source = lax.broadcasted_iota(jnp.int32, (total, total), 0)
    inner = lax.broadcasted_iota(jnp.int32, (1, width), 1) * facet_count
    wanted = jnp.concatenate([inner + k for k in range(facet_count)], axis=1)
    chooser = jnp.where(source == wanted, 1.0, 0.0).astype(BF16)
    own = [coverage_ref[i].astype(F32) for i in range(per_sub)]
    own = jnp.dot(
        jnp.concatenate(own, axis=0).astype(BF16), chooser, preferred_element_type=F32
    )
    ordered[...] = own * (1.0 / (facet_count * planes))
    counts[sub, pair] = ordered[...]
    screens[pair] = phases_ref[...]

    gain[pl.ds(0, low, stride=2), :] = correction_ref[...]
    gain[pl.ds(1, low, stride=2), :] = correction_ref[...]
    first_q, turn_cos, turn_sin, is_first, window_rows = offset_tables(
        offsets_ref, window_ref, quads
    )
    fetches["pick"].wait()
    picked = gather_pick(first_q, pick_ref)

    pl.when((sub != 0) & (sub == sub_count - 1))(greet)
    gains = gain[...]
    fetches["outer"].wait()
    outer = split(outer_ref[...])
    fetches["turn"].wait()
    table_cos, table_sin = turn_ref[0], turn_ref[1]
    fetches["unit"].wait()
    unit = split(unit_ref[...])
    forward = []
    for step in range(pairs):
        loads[step].wait()
        groups = []
        for g in range(pair_size):
            at = step * batch + g * quads
            blocks = [image[at + i] * gains for i in range(quads)]
            groups.append(jnp.concatenate(swap_blocks(blocks, low), axis=0))
        spread = jnp.concatenate(groups, axis=1)
        mixed = mm(outer, split(spread))
        turned = []
        for g in range(pair_size):
            real = mixed[:width, g * width : (g + 1) * width]
            imag = mixed[width:, g * width : (g + 1) * width]
            turned.append(
                jnp.concatenate(
                    [real * table_cos - imag * table_sin, real * table_sin + imag * table_cos],
                    axis=1,
                )
            )
        turned = jnp.concatenate(turned, axis=0)
        spectrum = mm(picked, split(turned), transposed=True)
        if step == 0:
            pl.when((sub != 0) & (sub != sub_count - 1))(greet)
        for s in range(subs):
            here = slice(s * quads, (s + 1) * quads)
            base = s * 4 * quads
            keep = is_first[here]
            win = window_rows[here]
            for g in range(pair_size):
                cols = slice(g * width, (g + 1) * width)
                for c in range(2):
                    one = spectrum[base + c * quads : base + (c + 1) * quads, cols]
                    two = spectrum[base + (2 + c) * quads : base + (3 + c) * quads, cols]
                    cut[step, g, here, c * width : (c + 1) * width] = (
                        jnp.where(keep, one, two) * win
                    )
        mixed = mm(split(cut[step].reshape(pair_size * span, 2 * width)), unit)
        for g in range(pair_size):
            real = mixed[g * span : (g + 1) * span, :width]
            imag = mixed[g * span : (g + 1) * span, width:]
            sent[step, g, :, :width] = real * turn_cos + imag * turn_sin
            sent[step, g, :, width:] = imag * turn_cos - real * turn_sin
        if step == 0:
            pl.when(sub == 0)(greet)
        for g in range(pair_size):
            if step < pairs - 1:
                slot = lax.rem(facet + g, pair_size)
                mate = order[step] * pair_size + slot
            elif g < pair_size - 1:
                slot = lax.rem(facet + 1 + g, pair_size)
                mate = order[step] * pair_size + slot
            else:
                continue
            copy = pltpu.make_async_remote_copy(
                src_ref=sent.at[step, slot],
                dst_ref=arrived.at[facet],
                send_sem=fwd_send.at[step * pair_size + g],
                recv_sem=fwd_recv.at[step * pair_size + g],
                device_id={"facet": mate},
                device_id_type=MESH,
            )
            copy.start()
            forward.append(copy)
    arrived[facet] = sent[pairs - 1, lax.rem(facet, pair_size)]
    fetches["unit_t"].wait()
    unit_t = split(unit_t_ref[...])

    for copy in gathers():
        copy.wait()
    for owner in range(sub_count):
        for p in range(pair_count):
            for i in range(per_sub):
                for j in range(per_wa):
                    at = (p * per_wa + j) * span + (owner * per_sub + i) * quads
                    row = counts[owner, p, i * per_wa + j : i * per_wa + j + 1]
                    expanded[at : at + quads, :] = jnp.broadcast_to(row, (quads, total))
    kernels = []
    for p in range(pair_count):
        screen = screens[p]
        cos_all, sin_all = cos_sin(screen)
        for j in range(per_wa):
            kernels.append((cos_all[j : j + 1], sin_all[j : j + 1]))
    twist = [(twist_ref[0, k : k + 1], twist_ref[1, k : k + 1]) for k in range(facet_count)]

    backward = []
    halves, part = back.shape[0], back.shape[2]
    for copy in forward:
        copy.wait()
    for h in range(halves):
        pieces = [[] for _ in range(facet_count)]
        for w in range(planes):
            parts = []
            for f in range(facet_count):
                cols = slice(f * width, (f + 1) * width)
                kc, ks = kernels[w][0][:, cols], kernels[w][1][:, cols]
                both = arrived[f, h * part : (h + 1) * part, :]
                real, imag = both[:, :width], both[:, width:]
                parts.append((real * kc - imag * ks, real * ks + imag * kc))
            for k, (real, imag) in enumerate(radix(parts, -1)):
                tc, ts = twist[k]
                pieces[k].append(
                    jnp.concatenate([real * tc - imag * ts, real * ts + imag * tc], axis=1)
                )
        stacked = jnp.concatenate([piece for group in pieces for piece in group], axis=0)
        grid = mm(split(stacked), unit_t)
        scale = jnp.concatenate(
            [
                expanded[w * span + h * part : w * span + (h + 1) * part, k * width : (k + 1) * width]
                for k in range(facet_count)
                for w in range(planes)
            ],
            axis=0,
        )
        weighted = grid * jnp.concatenate([scale, scale], axis=1)
        image_side = mm(split(weighted), unit)
        sums = [None] * facet_count
        for w in range(planes):
            parts = []
            for k in range(facet_count):
                at = (k * planes + w) * part
                real = image_side[at : at + part, :width]
                imag = image_side[at : at + part, width:]
                tc, ts = twist[k]
                parts.append((real * tc + imag * ts, imag * tc - real * ts))
            for f, (real, imag) in enumerate(radix(parts, 1)):
                cols = slice(f * width, (f + 1) * width)
                kc, ks = kernels[w][0][:, cols], kernels[w][1][:, cols]
                term = (real * kc + imag * ks, imag * kc - real * ks)
                sums[f] = term if w == 0 else (sums[f][0] + term[0], sums[f][1] + term[1])
        for f in range(facet_count):
            back[h, f, :, :width] = sums[f][0]
            back[h, f, :, width:] = sums[f][1]
        for i, mate in enumerate(far_first):
            copy = pltpu.make_async_remote_copy(
                src_ref=back.at[h, mate],
                dst_ref=returned.at[h, facet],
                send_sem=bwd_send.at[h, i],
                recv_sem=bwd_recv.at[h, i],
                device_id={"facet": mate},
                device_id_type=MESH,
            )
            copy.start()
            backward.append(copy)
        returned[h, facet] = back[h, facet]
    for copy in backward:
        copy.wait()


def inverse_kernel(
    offsets_ref,
    returned,
    correction_ref,
    window_ref,
    unit_t_ref,
    pick_ref,
    turn_ref,
    outer_t_ref,
    out_ref,
    gain,
    segments,
    image,
    out_sem,
):
    halves, facet_count, part, double = returned.shape
    span = halves * part
    width = double // 2
    subs = offsets_ref.shape[0]
    low = pick_ref.shape[0]
    quads = width // low
    gain[pl.ds(0, low, stride=2), :] = correction_ref[...]
    gain[pl.ds(1, low, stride=2), :] = correction_ref[...]
    gains = gain[...]
    first_q, turn_cos, turn_sin, is_first, window_rows = offset_tables(
        offsets_ref, window_ref, quads
    )
    unturned = []
    for g in range(facet_count):
        whole = jnp.concatenate([returned[h, g] for h in range(halves)], axis=0)
        real, imag = whole[:, :width], whole[:, width:]
        unturned.append(
            jnp.concatenate(
                [real * turn_cos - imag * turn_sin, real * turn_sin + imag * turn_cos], axis=1
            )
        )
    unturned = jnp.concatenate(unturned, axis=0)
    mixed = mm(split(unturned), split(unit_t_ref[...]))
    win_first = jnp.where(is_first, window_rows, 0.0)
    win_second = jnp.where(is_first, 0.0, window_rows)
    for g in range(facet_count):
        cols = slice(g * width, (g + 1) * width)
        for c in range(2):
            part = mixed[g * span : (g + 1) * span, c * width : (c + 1) * width]
            for h, win in enumerate((win_first, win_second)):
                masked = part * win
                for s in range(subs):
                    at = (4 * s + 2 * h + c) * quads
                    segments[at : at + quads, cols] = masked[s * quads : (s + 1) * quads]
    picked = gather_pick(first_q, pick_ref)
    table_cos, table_sin = turn_ref[0], turn_ref[1]
    outer_t = split(outer_t_ref[...])
    share = 2 * width // quads
    pair_size = 2 if facet_count % 2 == 0 else 1
    stores = []
    for first in range(0, facet_count, pair_size):
        here = range(first, first + pair_size)
        columns = jnp.concatenate(
            [segments[:, g * width : (g + 1) * width].T for g in here], axis=0
        )
        fine = mm(split(columns), picked)
        reals, imags = [], []
        for g in range(pair_size):
            real = fine[g * width : (g + 1) * width, :width]
            imag = fine[g * width : (g + 1) * width, width:]
            reals.append(real * table_cos + imag * table_sin)
            imags.append(imag * table_cos - real * table_sin)
        joined = jnp.concatenate(
            [jnp.concatenate(reals, axis=1), jnp.concatenate(imags, axis=1)], axis=0
        )
        spread = mm(outer_t, split(joined))
        for j, g in enumerate(here):
            cols = slice(j * width, (j + 1) * width)
            blocks = [spread[i * share : (i + 1) * share, cols] for i in range(quads)]
            for i, block in enumerate(swap_blocks(blocks, low)):
                image[g * quads + i] = block * gains
            store = pltpu.make_async_copy(
                image.at[pl.ds(g * quads, quads)],
                out_ref.at[pl.ds(g * quads, quads)],
                out_sem.at[g],
            )
            store.start()
            stores.append(store)
    for store in stores:
        store.wait()


def on_device(facets, correction, window, offsets, phases, coverage):
    facet_count = lax.axis_size("facet")
    sub_count = lax.axis_size("sub")
    pair_count = lax.axis_size("wa")
    row_count, length = facets.shape[1], facets.shape[3]
    width = window.shape[0]
    subs = offsets.shape[0]
    rows = row_count // (sub_count * pair_count)
    low = length // width
    quads = width // low
    if rows != facet_count * quads or low * quads != width:
        raise ValueError("unsupported sizes")
    span = subs * quads
    total = facet_count * width
    lines = length // width
    image = facets.reshape(row_count, 2, lines, width)
    image = jnp.transpose(image, (0, 2, 1, 3)).reshape(row_count, 2 * lines, width)
    twist, outer, turn, pick, unit, unit_t, outer_t = tables(length, width, facet_count)
    vmem = pl.BlockSpec(memory_space=pltpu.VMEM)
    smem = pl.BlockSpec(memory_space=pltpu.SMEM)
    far = pl.BlockSpec(memory_space=pltpu.HBM)
    others = sub_count * pair_count - 1
    dma = pltpu.SemaphoreType.DMA
    halves = 2 if subs % 2 == 0 and (span // 2) % 8 == 0 else 1
    block = (halves, facet_count, span // halves, 2 * width)
    gains = correction.reshape(lines, width)
    pair_size = 2 if facet_count % 2 == 0 else 1
    held = coverage.shape[0] * coverage.shape[1]
    window = window.reshape(1, width)
    first_tables = [outer, turn, pick, unit, unit_t]
    returned = pl.pallas_call(
        functools.partial(kernel, (facet_count, sub_count, pair_count)),
        out_shape=pltpu.VMEM(block, F32),
        in_specs=[smem, far] + [vmem] * 5 + [far] * len(first_tables),
        out_specs=vmem,
        scratch_shapes=[
            pltpu.VMEM((rows, 2 * lines, width), F32),
            pltpu.VMEM((2 * lines, width), F32),
            pltpu.VMEM((facet_count // pair_size, pair_size, span, 2 * width), F32),
            pltpu.VMEM((facet_count // pair_size, pair_size, span, 2 * width), F32),
            pltpu.VMEM((facet_count, span, 2 * width), F32),
            pltpu.VMEM(block, F32),
            pltpu.VMEM((held, total), F32),
            pltpu.VMEM((sub_count, pair_count, held, total), F32),
            pltpu.VMEM((coverage.shape[1] * pair_count * span, total), F32),
            pltpu.VMEM((pair_count,) + phases.shape, F32),
            dma((facet_count // pair_size,)),
            dma((facet_count - 1,)),
            dma((facet_count - 1,)),
            dma((halves, facet_count - 1)),
            dma((halves, facet_count - 1)),
            dma((others,)),
            dma((others,)),
            dma((max(pair_count - 1, 1),)),
            dma((max(pair_count - 1, 1),)),
        ]
        + [pltpu.VMEM(table.shape, F32) for table in first_tables]
        + [dma((len(first_tables),))],
        compiler_params=pltpu.CompilerParams(
            collective_id=0, has_side_effects=True, vmem_limit_bytes=55 * 1024 * 1024
        ),
    )(offsets, image, gains, window, phases, coverage, jnp.asarray(twist), *map(jnp.asarray, first_tables))
    second_tables = [unit_t, pick, turn, outer_t]
    result = pl.pallas_call(
        inverse_kernel,
        out_shape=jax.ShapeDtypeStruct((rows, 2 * lines, width), F32),
        in_specs=[smem] + [vmem] * (3 + len(second_tables)),
        out_specs=far,
        scratch_shapes=[
            pltpu.VMEM((2 * lines, width), F32),
            pltpu.VMEM((4 * span, total), F32),
            pltpu.VMEM((rows, 2 * lines, width), F32),
            dma((facet_count,)),
        ],
        compiler_params=pltpu.CompilerParams(vmem_limit_bytes=48 * 1024 * 1024),
    )(offsets, returned, gains, window, *map(jnp.asarray, second_tables))
    result = jnp.transpose(result.reshape(rows, lines, 2, width), (0, 2, 1, 3))
    return result.reshape(1, rows, 2, length)


def solution(mesh):
    return jax.shard_map(
        on_device,
        mesh=mesh,
        in_specs=(
            P("facet", None, None, None),
            P("facet", None),
            P(),
            P(),
            P("wa", None),
            P("sub", "wa", None),
        ),
        out_specs=P("facet", ("sub", "wa"), None, None),
        check_vma=False,
    )
```

```python
import functools
import math

import jax
import jax.numpy as jnp
import numpy as np
from jax import lax
from jax.experimental import pallas as pl
from jax.experimental.pallas import tpu as pltpu
from jax.sharding import PartitionSpec as P

MESH = pl.DeviceIdType.MESH
F32 = jnp.float32
BF16 = jnp.bfloat16


def complex_rows(matrix):
    return np.block([[matrix.real, matrix.imag], [-matrix.imag, matrix.real]])


def tables(length, width, facet_count):
    low = length // width
    quads = width // low
    a = np.arange(width)
    b = np.arange(low)
    dft = np.exp(-2j * np.pi * np.outer(a, a) / width)
    order = (a.reshape(width // quads, quads).T).reshape(-1)
    picked = dft[:, order]
    spread = np.zeros((2, width, width, 2))
    spread[0, :, :, 0] = picked.real
    spread[0, :, :, 1] = -picked.imag
    spread[1, :, :, 0] = picked.imag
    spread[1, :, :, 1] = picked.real
    outer = spread.reshape(2 * width, 2 * width)
    turn = np.tile(np.exp(-2j * np.pi * np.outer(a, b) / length), (1, quads))
    turn = np.stack([turn.real, turn.imag]).astype(np.float32)
    fine = np.exp(-2j * np.pi * np.outer(b, b) / low) * length**-0.5
    pick = np.zeros((low, 2, quads, 2, quads, low))
    for quad in range(quads):
        pick[:, 0, quad, 0, quad] = fine.real
        pick[:, 0, quad, 1, quad] = -fine.imag
        pick[:, 1, quad, 0, quad] = fine.imag
        pick[:, 1, quad, 1, quad] = fine.real
    pick = pick.reshape(low, 2 * quads, 2 * width).astype(np.float32)
    unit = complex_rows(np.conj(dft) * width**-0.5)
    twist = np.exp(-2j * np.pi * np.outer(np.arange(facet_count), a) / (facet_count * width))
    twist = np.stack([twist.real, twist.imag]).astype(np.float32)
    outer, unit = outer.astype(np.float32), unit.astype(np.float32)
    return twist, outer, turn, pick, unit, unit.T, outer.T


def split(value):
    high = value.astype(BF16)
    return high, (value - high.astype(F32)).astype(BF16)


def mm(left, right, transposed=False):
    axis = 1 if transposed else 0
    one = jnp.concatenate([left[0], left[0], left[1]], axis=1)
    two = jnp.concatenate([right[0], right[1], right[0]], axis=axis)
    return lax.dot_general(one, two, (((1,), (axis,)), ((), ())), preferred_element_type=F32)


def cos_sin(value):
    turns = jnp.floor(value * (2.0 / math.pi) + 0.5)
    rest = (value - turns * 1.5703125) - turns * (math.pi / 2 - 1.5703125)
    square = rest * rest
    sine = rest + rest * square * (
        -1.0 / 6 + square * (1.0 / 120 + square * (-1.0 / 5040 + square * (1.0 / 362880)))
    )
    cosine = 1.0 + square * (
        -0.5 + square * (1.0 / 24 + square * (-1.0 / 720 + square * (1.0 / 40320)))
    )
    odd = jnp.abs(turns) == 1.0
    sign_cos = jnp.where(turns == 1.0, -1.0, jnp.where(jnp.abs(turns) == 2.0, -1.0, 1.0))
    sign_sin = jnp.where(turns == -1.0, -1.0, jnp.where(jnp.abs(turns) == 2.0, -1.0, 1.0))
    return jnp.where(odd, sine, cosine) * sign_cos, jnp.where(odd, cosine, sine) * sign_sin


def radix(parts, sign):
    count = len(parts)
    if count == 1:
        return parts
    if count % 2:
        raise ValueError("odd length")
    even = radix(parts[0::2], sign)
    odd = radix(parts[1::2], sign)
    first, second = [], []
    for k in range(count // 2):
        real, imag = odd[k]
        if 4 * k == count:
            real, imag = (-imag, real) if sign > 0 else (imag, -real)
        elif k:
            c = math.cos(2 * math.pi * k / count)
            s = sign * math.sin(2 * math.pi * k / count)
            real, imag = real * c - imag * s, real * s + imag * c
        first.append((even[k][0] + real, even[k][1] + imag))
        second.append((even[k][0] - real, even[k][1] - imag))
    return first + second


def swap_blocks(blocks, low):
    blocks = list(blocks)
    count = len(blocks)
    width = count * low
    lane = lax.broadcasted_iota(jnp.int32, blocks[0].shape, 1)
    step = count // 2
    while step:
        shift = step * low
        upper = (lane & shift) != 0
        for i in range(count):
            if i & step:
                continue
            one, two = blocks[i], blocks[i + step]
            blocks[i] = jnp.where(upper, pltpu.roll(two, shift, 1), one)
            blocks[i + step] = jnp.where(upper, two, pltpu.roll(one, width - shift, 1))
        step //= 2
    return blocks


def offset_tables(offsets_ref, window_ref, quads):
    width = window_ref.shape[1]
    subs = offsets_ref.shape[0]
    span = subs * quads
    starts = [offsets_ref[s] for s in range(subs)]
    first_q = [start // width for start in starts]
    rests = [start & (width - 1) for start in starts]
    row = lax.broadcasted_iota(jnp.int32, (span, width), 0)
    offset_rows = jnp.zeros((span, width), jnp.int32)
    window_full = jnp.broadcast_to(window_ref[...], (8, width))
    window_rows = jnp.zeros((span, width), F32)
    for s in range(subs):
        offset_rows = jnp.where(row >= s * quads, rests[s], offset_rows)
        moved = pltpu.roll(window_full, rests[s], 1)[0:1]
        window_rows = jnp.where(row >= s * quads, moved, window_rows)
    span_lane = lax.broadcasted_iota(jnp.int32, (span, width), 1)
    steps = ((offset_rows * span_lane + width // 2) & (width - 1)) - width // 2
    turn_cos, turn_sin = cos_sin(steps.astype(F32) * (2.0 * math.pi / width))
    return first_q, turn_cos, turn_sin, span_lane >= offset_rows, window_rows


def gather_pick(first_q, pick_ref):
    low = pick_ref.shape[0]
    picked = []
    for q in first_q:
        picked.append(pick_ref[q])
        picked.append(pick_ref[lax.rem(q + 1, low)])
    return split(jnp.concatenate(picked, axis=0))


def kernel(
    geometry,
    offsets_ref,
    facets_ref,
    correction_ref,
    window_ref,
    phases_ref,
    coverage_ref,
    twist_ref,
    outer_far,
    turn_far,
    pick_far,
    unit_far,
    unit_t_far,
    returned,
    image,
    gain,
    cut,
    sent,
    arrived,
    back,
    ordered,
    counts,
    expanded,
    screens,
    load_sem,
    fwd_send,
    fwd_recv,
    bwd_send,
    bwd_recv,
    cov_send,
    cov_recv,
    ph_send,
    ph_recv,
    outer_ref,
    turn_ref,
    pick_ref,
    unit_ref,
    unit_t_ref,
    table_sem,
):
    facet_count, sub_count, pair_count = geometry
    facet = lax.axis_index("facet")
    sub = lax.axis_index("sub")
    pair = lax.axis_index("wa")
    rows = image.shape[0]
    width = window_ref.shape[1]
    subs = offsets_ref.shape[0]
    low = pick_ref.shape[0]
    quads = width // low
    length = low * width
    span = subs * quads
    per_sub, per_wa = coverage_ref.shape[0], coverage_ref.shape[1]
    planes = per_wa * pair_count
    total = facet_count * width

    facet_mates = [lax.rem(facet + d, facet_count) for d in range(1, facet_count)]
    hops = [(ds, dw) for ds in range(sub_count) for dw in range(pair_count) if ds or dw]
    barrier = pltpu.get_barrier_semaphore()
    for mate in facet_mates:
        pl.semaphore_signal(barrier, inc=1, device_id={"facet": mate}, device_id_type=MESH)
    grid_mates = [(lax.rem(sub + ds, sub_count), lax.rem(pair + dw, pair_count)) for ds, dw in hops]
    for mate_sub, mate_pair in grid_mates:
        pl.semaphore_signal(
            barrier, inc=1, device_id={"sub": mate_sub, "wa": mate_pair}, device_id_type=MESH
        )
    pair_size = 2 if facet_count % 2 == 0 else 1
    pairs = facet_count // pair_size
    order = [lax.rem(facet // pair_size + 1 + step, pairs) for step in range(pairs)]
    slots = [
        order[step] * pair_size + lax.rem(facet + g, pair_size)
        for step in range(pairs - 1)
        for g in range(pair_size)
    ]
    near = order[-1] * pair_size
    far_first = slots + [near + lax.rem(facet + 1 + g, pair_size) for g in range(pair_size - 1)]
    batch = pair_size * quads
    first_row = (sub * pair_count + pair) * rows
    loads = []
    for step, which in enumerate(order):
        load = pltpu.make_async_copy(
            facets_ref.at[pl.ds(first_row + which * batch, batch)],
            image.at[pl.ds(step * batch, batch)],
            load_sem.at[step],
        )
        load.start()
        loads.append(load)
    fetches = {}
    for i, (name, far, near) in enumerate(
        (
            ("outer", outer_far, outer_ref),
            ("turn", turn_far, turn_ref),
            ("pick", pick_far, pick_ref),
            ("unit", unit_far, unit_ref),
            ("unit_t", unit_t_far, unit_t_ref),
        )
    ):
        fetches[name] = pltpu.make_async_copy(far, near, table_sem.at[i])
        fetches[name].start()

    def gathers():
        copies = []
        for i, (mate_sub, mate_pair) in enumerate(grid_mates):
            copies.append(
                pltpu.make_async_remote_copy(
                    src_ref=ordered,
                    dst_ref=counts.at[sub, pair],
                    send_sem=cov_send.at[i],
                    recv_sem=cov_recv.at[i],
                    device_id={"sub": mate_sub, "wa": mate_pair},
                    device_id_type=MESH,
                )
            )
        for d in range(1, pair_count):
            copies.append(
                pltpu.make_async_remote_copy(
                    src_ref=phases_ref,
                    dst_ref=screens.at[pair],
                    send_sem=ph_send.at[d - 1],
                    recv_sem=ph_recv.at[d - 1],
                    device_id={"wa": lax.rem(pair + d, pair_count)},
                    device_id_type=MESH,
                )
            )
        return copies

    def greet():
        pl.semaphore_wait(barrier, len(facet_mates) + len(hops))
        for copy in gathers():
            copy.start()

    source = lax.broadcasted_iota(jnp.int32, (width, width), 0)
    target = lax.broadcasted_iota(jnp.int32, (1, width), 1)
    fold = width // facet_count
    wanted = (target & (fold - 1)) * facet_count + target // fold
    chooser = jnp.where(source == wanted, 1.0, 0.0).astype(BF16)
    own = jnp.concatenate([coverage_ref[i].astype(F32) for i in range(per_sub)], axis=0)
    held = per_sub * per_wa
    own = jnp.concatenate([own[:, k * width : (k + 1) * width] for k in range(facet_count)], axis=0)
    own = jnp.dot(own.astype(BF16), chooser, preferred_element_type=F32)
    own = own * (1.0 / (facet_count * planes))
    own = [own[k * held : (k + 1) * held] for k in range(facet_count)]
    for k, block in enumerate(swap_blocks(own, fold)):
        ordered[:, k * width : (k + 1) * width] = block
    counts[sub, pair] = ordered[...]
    screens[pair] = phases_ref[...]
    pl.when((sub != 0) & (sub == sub_count - 1))(greet)

    gain[pl.ds(0, low, stride=2), :] = correction_ref[...]
    gain[pl.ds(1, low, stride=2), :] = correction_ref[...]
    first_q, turn_cos, turn_sin, is_first, window_rows = offset_tables(
        offsets_ref, window_ref, quads
    )
    fetches["pick"].wait()
    picked = gather_pick(first_q, pick_ref)

    gains = gain[...]
    fetches["outer"].wait()
    outer = split(outer_ref[...])
    fetches["turn"].wait()
    table_cos, table_sin = turn_ref[0], turn_ref[1]
    fetches["unit"].wait()
    unit = split(unit_ref[...])
    forward = []
    for step in range(pairs):
        loads[step].wait()
        groups = []
        for g in range(pair_size):
            at = step * batch + g * quads
            blocks = [image[at + i] * gains for i in range(quads)]
            groups.append(jnp.concatenate(swap_blocks(blocks, low), axis=0))
        spread = jnp.concatenate(groups, axis=1)
        mixed = mm(outer, split(spread))
        if step == 0:
            pl.when((sub != 0) & (sub != sub_count - 1))(greet)
        turned = []
        for g in range(pair_size):
            real = mixed[:width, g * width : (g + 1) * width]
            imag = mixed[width:, g * width : (g + 1) * width]
            turned.append(
                jnp.concatenate(
                    [real * table_cos - imag * table_sin, real * table_sin + imag * table_cos],
                    axis=1,
                )
            )
        turned = jnp.concatenate(turned, axis=0)
        spectrum = mm(picked, split(turned), transposed=True)
        for s in range(subs):
            here = slice(s * quads, (s + 1) * quads)
            base = s * 4 * quads
            keep = is_first[here]
            win = window_rows[here]
            for g in range(pair_size):
                cols = slice(g * width, (g + 1) * width)
                for c in range(2):
                    one = spectrum[base + c * quads : base + (c + 1) * quads, cols]
                    two = spectrum[base + (2 + c) * quads : base + (3 + c) * quads, cols]
                    cut[step, g, here, c * width : (c + 1) * width] = (
                        jnp.where(keep, one, two) * win
                    )
        mixed = mm(split(cut[step].reshape(pair_size * span, 2 * width)), unit)
        for g in range(pair_size):
            real = mixed[g * span : (g + 1) * span, :width]
            imag = mixed[g * span : (g + 1) * span, width:]
            sent[step, g, :, :width] = real * turn_cos + imag * turn_sin
            sent[step, g, :, width:] = imag * turn_cos - real * turn_sin
        if step == 0:
            pl.when(sub == 0)(greet)
        for g in range(pair_size):
            if step < pairs - 1:
                slot = lax.rem(facet + g, pair_size)
                mate = order[step] * pair_size + slot
            elif g < pair_size - 1:
                slot = lax.rem(facet + 1 + g, pair_size)
                mate = order[step] * pair_size + slot
            else:
                continue
            copy = pltpu.make_async_remote_copy(
                src_ref=sent.at[step, slot],
                dst_ref=arrived.at[facet],
                send_sem=fwd_send.at[step * pair_size + g],
                recv_sem=fwd_recv.at[step * pair_size + g],
                device_id={"facet": mate},
                device_id_type=MESH,
            )
            copy.start()
            forward.append(copy)
    arrived[facet] = sent[pairs - 1, lax.rem(facet, pair_size)]
    fetches["unit_t"].wait()
    unit_t = split(unit_t_ref[...])

    arrivals = gathers()
    for copy in arrivals[len(hops) :]:
        copy.wait()
    kernels = []
    for p in range(pair_count):
        screen = screens[p]
        cos_all, sin_all = cos_sin(screen)
        for j in range(per_wa):
            kernels.append((cos_all[j : j + 1], sin_all[j : j + 1]))
    twist = [(twist_ref[0, k : k + 1], twist_ref[1, k : k + 1]) for k in range(facet_count)]

    backward = []
    halves, part = back.shape[0], back.shape[2]
    for copy in forward:
        copy.wait()
    for h in range(halves):
        pieces = [[] for _ in range(facet_count)]
        for w in range(planes):
            parts = []
            for f in range(facet_count):
                cols = slice(f * width, (f + 1) * width)
                kc, ks = kernels[w][0][:, cols], kernels[w][1][:, cols]
                both = arrived[f, h * part : (h + 1) * part, :]
                real, imag = both[:, :width], both[:, width:]
                parts.append((real * kc - imag * ks, real * ks + imag * kc))
            for k, (real, imag) in enumerate(radix(parts, -1)):
                tc, ts = twist[k]
                pieces[k].append(
                    jnp.concatenate([real * tc - imag * ts, real * ts + imag * tc], axis=1)
                )
        stacked = jnp.concatenate([piece for group in pieces for piece in group], axis=0)
        grid = mm(split(stacked), unit_t)
        if h == 0:
            for copy in arrivals[: len(hops)]:
                copy.wait()
            for owner in range(sub_count):
                for p in range(pair_count):
                    for i in range(per_sub):
                        for j in range(per_wa):
                            at = (p * per_wa + j) * span + (owner * per_sub + i) * quads
                            row = counts[owner, p, i * per_wa + j : i * per_wa + j + 1]
                            expanded[at : at + quads, :] = jnp.broadcast_to(row, (quads, total))
        scale = jnp.concatenate(
            [
                expanded[w * span + h * part : w * span + (h + 1) * part, k * width : (k + 1) * width]
                for k in range(facet_count)
                for w in range(planes)
            ],
            axis=0,
        )
        weighted = grid * jnp.concatenate([scale, scale], axis=1)
        image_side = mm(split(weighted), unit)
        sums = [None] * facet_count
        for w in range(planes):
            parts = []
            for k in range(facet_count):
                at = (k * planes + w) * part
                real = image_side[at : at + part, :width]
                imag = image_side[at : at + part, width:]
                tc, ts = twist[k]
                parts.append((real * tc + imag * ts, imag * tc - real * ts))
            for f, (real, imag) in enumerate(radix(parts, 1)):
                cols = slice(f * width, (f + 1) * width)
                kc, ks = kernels[w][0][:, cols], kernels[w][1][:, cols]
                term = (real * kc + imag * ks, imag * kc - real * ks)
                sums[f] = term if w == 0 else (sums[f][0] + term[0], sums[f][1] + term[1])
        for f in range(facet_count):
            back[h, f, :, :width] = sums[f][0]
            back[h, f, :, width:] = sums[f][1]
        for i, mate in enumerate(far_first):
            copy = pltpu.make_async_remote_copy(
                src_ref=back.at[h, mate],
                dst_ref=returned.at[h, facet],
                send_sem=bwd_send.at[h, i],
                recv_sem=bwd_recv.at[h, i],
                device_id={"facet": mate},
                device_id_type=MESH,
            )
            copy.start()
            backward.append(copy)
        returned[h, facet] = back[h, facet]
    for copy in backward:
        copy.wait()


def inverse_kernel(
    offsets_ref,
    returned,
    correction_ref,
    window_ref,
    unit_t_ref,
    pick_ref,
    turn_ref,
    outer_t_ref,
    out_ref,
    gain,
    segments,
    image,
    out_sem,
):
    halves, facet_count, part, double = returned.shape
    span = halves * part
    width = double // 2
    subs = offsets_ref.shape[0]
    low = pick_ref.shape[0]
    quads = width // low
    gain[pl.ds(0, low, stride=2), :] = correction_ref[...]
    gain[pl.ds(1, low, stride=2), :] = correction_ref[...]
    gains = gain[...]
    first_q, turn_cos, turn_sin, is_first, window_rows = offset_tables(
        offsets_ref, window_ref, quads
    )
    unturned = []
    for g in range(facet_count):
        whole = jnp.concatenate([returned[h, g] for h in range(halves)], axis=0)
        real, imag = whole[:, :width], whole[:, width:]
        unturned.append(
            jnp.concatenate(
                [real * turn_cos - imag * turn_sin, real * turn_sin + imag * turn_cos], axis=1
            )
        )
    unturned = jnp.concatenate(unturned, axis=0)
    mixed = mm(split(unturned), split(unit_t_ref[...]))
    win_first = jnp.where(is_first, window_rows, 0.0)
    win_second = jnp.where(is_first, 0.0, window_rows)
    for g in range(facet_count):
        cols = slice(g * width, (g + 1) * width)
        for c in range(2):
            part = mixed[g * span : (g + 1) * span, c * width : (c + 1) * width]
            for h, win in enumerate((win_first, win_second)):
                masked = part * win
                for s in range(subs):
                    at = (4 * s + 2 * h + c) * quads
                    segments[at : at + quads, cols] = masked[s * quads : (s + 1) * quads]
    picked = gather_pick(first_q, pick_ref)
    table_cos, table_sin = turn_ref[0], turn_ref[1]
    outer_t = split(outer_t_ref[...])
    share = 2 * width // quads
    pair_size = 2 if facet_count % 2 == 0 else 1
    stores = []
    for first in range(0, facet_count, pair_size):
        here = range(first, first + pair_size)
        columns = jnp.concatenate(
            [segments[:, g * width : (g + 1) * width].T for g in here], axis=0
        )
        fine = mm(split(columns), picked)
        reals, imags = [], []
        for g in range(pair_size):
            real = fine[g * width : (g + 1) * width, :width]
            imag = fine[g * width : (g + 1) * width, width:]
            reals.append(real * table_cos + imag * table_sin)
            imags.append(imag * table_cos - real * table_sin)
        joined = jnp.concatenate(
            [jnp.concatenate(reals, axis=1), jnp.concatenate(imags, axis=1)], axis=0
        )
        spread = mm(outer_t, split(joined))
        for j, g in enumerate(here):
            cols = slice(j * width, (j + 1) * width)
            blocks = [spread[i * share : (i + 1) * share, cols] for i in range(quads)]
            for i, block in enumerate(swap_blocks(blocks, low)):
                image[g * quads + i] = block * gains
            store = pltpu.make_async_copy(
                image.at[pl.ds(g * quads, quads)],
                out_ref.at[pl.ds(g * quads, quads)],
                out_sem.at[g],
            )
            store.start()
            stores.append(store)
    for store in stores:
        store.wait()


def on_device(facets, correction, window, offsets, phases, coverage):
    facet_count = lax.axis_size("facet")
    sub_count = lax.axis_size("sub")
    pair_count = lax.axis_size("wa")
    row_count, length = facets.shape[1], facets.shape[3]
    width = window.shape[0]
    subs = offsets.shape[0]
    rows = row_count // (sub_count * pair_count)
    low = length // width
    quads = width // low
    if rows != facet_count * quads or low * quads != width:
        raise ValueError("unsupported sizes")
    span = subs * quads
    total = facet_count * width
    lines = length // width
    image = facets.reshape(row_count, 2, lines, width)
    image = jnp.transpose(image, (0, 2, 1, 3)).reshape(row_count, 2 * lines, width)
    twist, outer, turn, pick, unit, unit_t, outer_t = tables(length, width, facet_count)
    vmem = pl.BlockSpec(memory_space=pltpu.VMEM)
    smem = pl.BlockSpec(memory_space=pltpu.SMEM)
    far = pl.BlockSpec(memory_space=pltpu.HBM)
    others = sub_count * pair_count - 1
    dma = pltpu.SemaphoreType.DMA
    halves = 2 if subs % 2 == 0 and (span // 2) % 8 == 0 else 1
    block = (halves, facet_count, span // halves, 2 * width)
    gains = correction.reshape(lines, width)
    pair_size = 2 if facet_count % 2 == 0 else 1
    held = coverage.shape[0] * coverage.shape[1]
    window = window.reshape(1, width)
    first_tables = [outer, turn, pick, unit, unit_t]
    returned = pl.pallas_call(
        functools.partial(kernel, (facet_count, sub_count, pair_count)),
        out_shape=pltpu.VMEM(block, F32),
        in_specs=[smem, far] + [vmem] * 5 + [far] * len(first_tables),
        out_specs=vmem,
        scratch_shapes=[
            pltpu.VMEM((rows, 2 * lines, width), F32),
            pltpu.VMEM((2 * lines, width), F32),
            pltpu.VMEM((facet_count // pair_size, pair_size, span, 2 * width), F32),
            pltpu.VMEM((facet_count // pair_size, pair_size, span, 2 * width), F32),
            pltpu.VMEM((facet_count, span, 2 * width), F32),
            pltpu.VMEM(block, F32),
            pltpu.VMEM((held, total), F32),
            pltpu.VMEM((sub_count, pair_count, held, total), F32),
            pltpu.VMEM((coverage.shape[1] * pair_count * span, total), F32),
            pltpu.VMEM((pair_count,) + phases.shape, F32),
            dma((facet_count // pair_size,)),
            dma((facet_count - 1,)),
            dma((facet_count - 1,)),
            dma((halves, facet_count - 1)),
            dma((halves, facet_count - 1)),
            dma((others,)),
            dma((others,)),
            dma((max(pair_count - 1, 1),)),
            dma((max(pair_count - 1, 1),)),
        ]
        + [pltpu.VMEM(table.shape, F32) for table in first_tables]
        + [dma((len(first_tables),))],
        compiler_params=pltpu.CompilerParams(
            collective_id=0, has_side_effects=True, vmem_limit_bytes=55 * 1024 * 1024
        ),
    )(offsets, image, gains, window, phases, coverage, jnp.asarray(twist), *map(jnp.asarray, first_tables))
    second_tables = [unit_t, pick, turn, outer_t]
    result = pl.pallas_call(
        inverse_kernel,
        out_shape=jax.ShapeDtypeStruct((rows, 2 * lines, width), F32),
        in_specs=[smem] + [vmem] * (3 + len(second_tables)),
        out_specs=far,
        scratch_shapes=[
            pltpu.VMEM((2 * lines, width), F32),
            pltpu.VMEM((4 * span, total), F32),
            pltpu.VMEM((rows, 2 * lines, width), F32),
            dma((facet_count,)),
        ],
        compiler_params=pltpu.CompilerParams(vmem_limit_bytes=48 * 1024 * 1024),
    )(offsets, returned, gains, window, *map(jnp.asarray, second_tables))
    result = jnp.transpose(result.reshape(rows, lines, 2, width), (0, 2, 1, 3))
    return result.reshape(1, rows, 2, length)


def solution(mesh):
    return jax.shard_map(
        on_device,
        mesh=mesh,
        in_specs=(
            P("facet", None, None, None),
            P("facet", None),
            P(),
            P(),
            P("wa", None),
            P("sub", "wa", None),
        ),
        out_specs=P("facet", ("sub", "wa"), None, None),
        check_vma=False,
    )
```

```python
import functools
import math

import jax
import jax.numpy as jnp
import numpy as np
from jax import lax
from jax.experimental import pallas as pl
from jax.experimental.pallas import tpu as pltpu
from jax.sharding import PartitionSpec as P

MESH = pl.DeviceIdType.MESH
F32 = jnp.float32
BF16 = jnp.bfloat16


def complex_rows(matrix):
    return np.block([[matrix.real, matrix.imag], [-matrix.imag, matrix.real]])


def tables(length, width, facet_count):
    low = length // width
    quads = width // low
    a = np.arange(width)
    b = np.arange(low)
    dft = np.exp(-2j * np.pi * np.outer(a, a) / width)
    order = (a.reshape(width // quads, quads).T).reshape(-1)
    picked = dft[:, order]
    spread = np.zeros((2, width, width, 2))
    spread[0, :, :, 0] = picked.real
    spread[0, :, :, 1] = -picked.imag
    spread[1, :, :, 0] = picked.imag
    spread[1, :, :, 1] = picked.real
    outer = spread.reshape(2 * width, 2 * width)
    turn = np.tile(np.exp(-2j * np.pi * np.outer(a, b) / length), (1, quads))
    turn = np.stack([turn.real, turn.imag]).astype(np.float32)
    fine = np.exp(-2j * np.pi * np.outer(b, b) / low) * length**-0.5
    pick = np.zeros((low, 2, quads, 2, quads, low))
    for quad in range(quads):
        pick[:, 0, quad, 0, quad] = fine.real
        pick[:, 0, quad, 1, quad] = -fine.imag
        pick[:, 1, quad, 0, quad] = fine.imag
        pick[:, 1, quad, 1, quad] = fine.real
    pick = pick.reshape(low, 2 * quads, 2 * width).astype(np.float32)
    unit = complex_rows(np.conj(dft) * width**-0.5)
    twist = np.exp(-2j * np.pi * np.outer(np.arange(facet_count), a) / (facet_count * width))
    twist = np.stack([twist.real, twist.imag]).astype(np.float32)
    outer, unit = outer.astype(np.float32), unit.astype(np.float32)
    return twist, outer, turn, pick, unit, unit.T, outer.T


def split(value):
    high = value.astype(BF16)
    return high, (value - high.astype(F32)).astype(BF16)


def mm(left, right, transposed=False):
    axis = 1 if transposed else 0
    one = jnp.concatenate([left[0], left[0], left[1]], axis=1)
    two = jnp.concatenate([right[0], right[1], right[0]], axis=axis)
    return lax.dot_general(one, two, (((1,), (axis,)), ((), ())), preferred_element_type=F32)


def cos_sin(value):
    turns = jnp.floor(value * (2.0 / math.pi) + 0.5)
    rest = (value - turns * 1.5703125) - turns * (math.pi / 2 - 1.5703125)
    square = rest * rest
    sine = rest + rest * square * (
        -1.0 / 6 + square * (1.0 / 120 + square * (-1.0 / 5040 + square * (1.0 / 362880)))
    )
    cosine = 1.0 + square * (
        -0.5 + square * (1.0 / 24 + square * (-1.0 / 720 + square * (1.0 / 40320)))
    )
    odd = jnp.abs(turns) == 1.0
    sign_cos = jnp.where(turns == 1.0, -1.0, jnp.where(jnp.abs(turns) == 2.0, -1.0, 1.0))
    sign_sin = jnp.where(turns == -1.0, -1.0, jnp.where(jnp.abs(turns) == 2.0, -1.0, 1.0))
    return jnp.where(odd, sine, cosine) * sign_cos, jnp.where(odd, cosine, sine) * sign_sin


def radix(parts, sign):
    count = len(parts)
    if count == 1:
        return parts
    if count % 2:
        raise ValueError("odd length")
    even = radix(parts[0::2], sign)
    odd = radix(parts[1::2], sign)
    first, second = [], []
    for k in range(count // 2):
        real, imag = odd[k]
        if 4 * k == count:
            real, imag = (-imag, real) if sign > 0 else (imag, -real)
        elif k:
            c = math.cos(2 * math.pi * k / count)
            s = sign * math.sin(2 * math.pi * k / count)
            real, imag = real * c - imag * s, real * s + imag * c
        first.append((even[k][0] + real, even[k][1] + imag))
        second.append((even[k][0] - real, even[k][1] - imag))
    return first + second


def swap_blocks(blocks, low):
    blocks = list(blocks)
    count = len(blocks)
    width = count * low
    lane = lax.broadcasted_iota(jnp.int32, blocks[0].shape, 1)
    step = count // 2
    while step:
        shift = step * low
        upper = (lane & shift) != 0
        for i in range(count):
            if i & step:
                continue
            one, two = blocks[i], blocks[i + step]
            blocks[i] = jnp.where(upper, pltpu.roll(two, shift, 1), one)
            blocks[i + step] = jnp.where(upper, two, pltpu.roll(one, width - shift, 1))
        step //= 2
    return blocks


def offset_tables(offsets_ref, window_ref, quads):
    width = window_ref.shape[1]
    subs = offsets_ref.shape[0]
    span = subs * quads
    starts = [offsets_ref[s] for s in range(subs)]
    first_q = [start // width for start in starts]
    rests = [start & (width - 1) for start in starts]
    row = lax.broadcasted_iota(jnp.int32, (span, width), 0)
    offset_rows = jnp.zeros((span, width), jnp.int32)
    window_full = jnp.broadcast_to(window_ref[...], (8, width))
    window_rows = jnp.zeros((span, width), F32)
    for s in range(subs):
        offset_rows = jnp.where(row >= s * quads, rests[s], offset_rows)
        moved = pltpu.roll(window_full, rests[s], 1)[0:1]
        window_rows = jnp.where(row >= s * quads, moved, window_rows)
    span_lane = lax.broadcasted_iota(jnp.int32, (span, width), 1)
    steps = ((offset_rows * span_lane + width // 2) & (width - 1)) - width // 2
    turn_cos, turn_sin = cos_sin(steps.astype(F32) * (2.0 * math.pi / width))
    return first_q, turn_cos, turn_sin, span_lane >= offset_rows, window_rows


def gather_pick(first_q, pick_ref):
    low = pick_ref.shape[0]
    picked = []
    for q in first_q:
        picked.append(pick_ref[q])
        picked.append(pick_ref[lax.rem(q + 1, low)])
    return split(jnp.concatenate(picked, axis=0))


def kernel(
    geometry,
    offsets_ref,
    facets_ref,
    correction_far,
    window_far,
    phases_far,
    coverage_far,
    twist_far,
    outer_far,
    turn_far,
    pick_far,
    unit_far,
    unit_t_far,
    returned,
    image,
    gain,
    cut,
    sent,
    arrived,
    back,
    ordered,
    counts,
    expanded,
    screens,
    load_sem,
    fwd_send,
    fwd_recv,
    bwd_send,
    bwd_recv,
    cov_send,
    cov_recv,
    ph_send,
    ph_recv,
    outer_ref,
    turn_ref,
    pick_ref,
    unit_ref,
    unit_t_ref,
    table_sem,
    correction_ref,
    window_ref,
    phases_ref,
    coverage_ref,
    twist_ref,
    small_sem,
):
    facet_count, sub_count, pair_count = geometry
    facet = lax.axis_index("facet")
    sub = lax.axis_index("sub")
    pair = lax.axis_index("wa")
    rows = image.shape[0]
    width = window_ref.shape[1]
    subs = offsets_ref.shape[0]
    low = pick_ref.shape[0]
    quads = width // low
    length = low * width
    span = subs * quads
    per_sub, per_wa = coverage_ref.shape[0], coverage_ref.shape[1]
    planes = per_wa * pair_count
    total = facet_count * width

    facet_mates = [lax.rem(facet + d, facet_count) for d in range(1, facet_count)]
    hops = [(ds, dw) for ds in range(sub_count) for dw in range(pair_count) if ds or dw]
    barrier = pltpu.get_barrier_semaphore()
    for mate in facet_mates:
        pl.semaphore_signal(barrier, inc=1, device_id={"facet": mate}, device_id_type=MESH)
    grid_mates = [(lax.rem(sub + ds, sub_count), lax.rem(pair + dw, pair_count)) for ds, dw in hops]
    for mate_sub, mate_pair in grid_mates:
        pl.semaphore_signal(
            barrier, inc=1, device_id={"sub": mate_sub, "wa": mate_pair}, device_id_type=MESH
        )
    fetches = {}
    for i, (name, far, near) in enumerate(
        (
            ("coverage", coverage_far, coverage_ref),
            ("phases", phases_far, phases_ref),
            ("correction", correction_far, correction_ref),
            ("window", window_far, window_ref),
            ("twist", twist_far, twist_ref),
        )
    ):
        fetches[name] = pltpu.make_async_copy(far, near, small_sem.at[i])
        fetches[name].start()
    pair_size = 2 if facet_count % 2 == 0 else 1
    pairs = facet_count // pair_size
    order = [lax.rem(facet // pair_size + 1 + step, pairs) for step in range(pairs)]
    slots = [
        order[step] * pair_size + lax.rem(facet + g, pair_size)
        for step in range(pairs - 1)
        for g in range(pair_size)
    ]
    near = order[-1] * pair_size
    far_first = slots + [near + lax.rem(facet + 1 + g, pair_size) for g in range(pair_size - 1)]
    batch = pair_size * quads
    first_row = (sub * pair_count + pair) * rows
    loads = []
    for step, which in enumerate(order):
        load = pltpu.make_async_copy(
            facets_ref.at[pl.ds(first_row + which * batch, batch)],
            image.at[pl.ds(step * batch, batch)],
            load_sem.at[step],
        )
        load.start()
        loads.append(load)
    for i, (name, far, near) in enumerate(
        (
            ("outer", outer_far, outer_ref),
            ("turn", turn_far, turn_ref),
            ("pick", pick_far, pick_ref),
            ("unit", unit_far, unit_ref),
            ("unit_t", unit_t_far, unit_t_ref),
        )
    ):
        fetches[name] = pltpu.make_async_copy(far, near, table_sem.at[i])
        fetches[name].start()

    def gathers():
        copies = []
        for i, (mate_sub, mate_pair) in enumerate(grid_mates):
            copies.append(
                pltpu.make_async_remote_copy(
                    src_ref=ordered,
                    dst_ref=counts.at[sub, pair],
                    send_sem=cov_send.at[i],
                    recv_sem=cov_recv.at[i],
                    device_id={"sub": mate_sub, "wa": mate_pair},
                    device_id_type=MESH,
                )
            )
        for d in range(1, pair_count):
            copies.append(
                pltpu.make_async_remote_copy(
                    src_ref=phases_ref,
                    dst_ref=screens.at[pair],
                    send_sem=ph_send.at[d - 1],
                    recv_sem=ph_recv.at[d - 1],
                    device_id={"wa": lax.rem(pair + d, pair_count)},
                    device_id_type=MESH,
                )
            )
        return copies

    def greet():
        pl.semaphore_wait(barrier, len(facet_mates) + len(hops))
        for copy in gathers():
            copy.start()

    source = lax.broadcasted_iota(jnp.int32, (width, width), 0)
    target = lax.broadcasted_iota(jnp.int32, (1, width), 1)
    fold = width // facet_count
    wanted = (target & (fold - 1)) * facet_count + target // fold
    chooser = jnp.where(source == wanted, 1.0, 0.0).astype(BF16)
    fetches["coverage"].wait()
    own = jnp.concatenate([coverage_ref[i].astype(F32) for i in range(per_sub)], axis=0)
    held = per_sub * per_wa
    own = jnp.concatenate([own[:, k * width : (k + 1) * width] for k in range(facet_count)], axis=0)
    own = jnp.dot(own.astype(BF16), chooser, preferred_element_type=F32)
    own = own * (1.0 / (facet_count * planes))
    own = [own[k * held : (k + 1) * held] for k in range(facet_count)]
    for k, block in enumerate(swap_blocks(own, fold)):
        ordered[:, k * width : (k + 1) * width] = block
    counts[sub, pair] = ordered[...]
    fetches["phases"].wait()
    screens[pair] = phases_ref[...]
    pl.when((sub != 0) & (sub == sub_count - 1))(greet)

    fetches["window"].wait()
    first_q, turn_cos, turn_sin, is_first, window_rows = offset_tables(
        offsets_ref, window_ref, quads
    )
    fetches["pick"].wait()
    picked = gather_pick(first_q, pick_ref)

    fetches["correction"].wait()
    gain[pl.ds(0, low, stride=2), :] = correction_ref[...]
    gain[pl.ds(1, low, stride=2), :] = correction_ref[...]
    gains = gain[...]
    fetches["outer"].wait()
    outer = split(outer_ref[...])
    fetches["turn"].wait()
    table_cos, table_sin = turn_ref[0], turn_ref[1]
    fetches["unit"].wait()
    unit = split(unit_ref[...])
    forward = []
    for step in range(pairs):
        loads[step].wait()
        groups = []
        for g in range(pair_size):
            at = step * batch + g * quads
            blocks = [image[at + i] * gains for i in range(quads)]
            groups.append(jnp.concatenate(swap_blocks(blocks, low), axis=0))
        spread = jnp.concatenate(groups, axis=1)
        mixed = mm(outer, split(spread))
        if step == 0:
            pl.when((sub != 0) & (sub != sub_count - 1))(greet)
        turned = []
        for g in range(pair_size):
            real = mixed[:width, g * width : (g + 1) * width]
            imag = mixed[width:, g * width : (g + 1) * width]
            turned.append(
                jnp.concatenate(
                    [real * table_cos - imag * table_sin, real * table_sin + imag * table_cos],
                    axis=1,
                )
            )
        turned = jnp.concatenate(turned, axis=0)
        spectrum = mm(picked, split(turned), transposed=True)
        for s in range(subs):
            here = slice(s * quads, (s + 1) * quads)
            base = s * 4 * quads
            keep = is_first[here]
            win = window_rows[here]
            for g in range(pair_size):
                cols = slice(g * width, (g + 1) * width)
                for c in range(2):
                    one = spectrum[base + c * quads : base + (c + 1) * quads, cols]
                    two = spectrum[base + (2 + c) * quads : base + (3 + c) * quads, cols]
                    cut[step, g, here, c * width : (c + 1) * width] = (
                        jnp.where(keep, one, two) * win
                    )
        mixed = mm(split(cut[step].reshape(pair_size * span, 2 * width)), unit)
        for g in range(pair_size):
            real = mixed[g * span : (g + 1) * span, :width]
            imag = mixed[g * span : (g + 1) * span, width:]
            sent[step, g, :, :width] = real * turn_cos + imag * turn_sin
            sent[step, g, :, width:] = imag * turn_cos - real * turn_sin
        if step == 0:
            pl.when(sub == 0)(greet)
        for g in range(pair_size):
            if step < pairs - 1:
                slot = lax.rem(facet + g, pair_size)
                mate = order[step] * pair_size + slot
            elif g < pair_size - 1:
                slot = lax.rem(facet + 1 + g, pair_size)
                mate = order[step] * pair_size + slot
            else:
                continue
            copy = pltpu.make_async_remote_copy(
                src_ref=sent.at[step, slot],
                dst_ref=arrived.at[facet],
                send_sem=fwd_send.at[step * pair_size + g],
                recv_sem=fwd_recv.at[step * pair_size + g],
                device_id={"facet": mate},
                device_id_type=MESH,
            )
            copy.start()
            forward.append(copy)
    arrived[facet] = sent[pairs - 1, lax.rem(facet, pair_size)]
    fetches["unit_t"].wait()
    unit_t = split(unit_t_ref[...])

    arrivals = gathers()
    for copy in arrivals[len(hops) :]:
        copy.wait()
    kernels = []
    for p in range(pair_count):
        screen = screens[p]
        cos_all, sin_all = cos_sin(screen)
        for j in range(per_wa):
            kernels.append((cos_all[j : j + 1], sin_all[j : j + 1]))
    fetches["twist"].wait()
    twist = [(twist_ref[0, k : k + 1], twist_ref[1, k : k + 1]) for k in range(facet_count)]

    backward = []
    halves, part = back.shape[0], back.shape[2]
    for copy in forward:
        copy.wait()
    for h in range(halves):
        pieces = [[] for _ in range(facet_count)]
        for w in range(planes):
            parts = []
            for f in range(facet_count):
                cols = slice(f * width, (f + 1) * width)
                kc, ks = kernels[w][0][:, cols], kernels[w][1][:, cols]
                both = arrived[f, h * part : (h + 1) * part, :]
                real, imag = both[:, :width], both[:, width:]
                parts.append((real * kc - imag * ks, real * ks + imag * kc))
            for k, (real, imag) in enumerate(radix(parts, -1)):
                tc, ts = twist[k]
                pieces[k].append(
                    jnp.concatenate([real * tc - imag * ts, real * ts + imag * tc], axis=1)
                )
        stacked = jnp.concatenate([piece for group in pieces for piece in group], axis=0)
        grid = mm(split(stacked), unit_t)
        if h == 0:
            for copy in arrivals[: len(hops)]:
                copy.wait()
            for owner in range(sub_count):
                for p in range(pair_count):
                    for i in range(per_sub):
                        for j in range(per_wa):
                            at = (p * per_wa + j) * span + (owner * per_sub + i) * quads
                            row = counts[owner, p, i * per_wa + j : i * per_wa + j + 1]
                            expanded[at : at + quads, :] = jnp.broadcast_to(row, (quads, total))
        scale = jnp.concatenate(
            [
                expanded[w * span + h * part : w * span + (h + 1) * part, k * width : (k + 1) * width]
                for k in range(facet_count)
                for w in range(planes)
            ],
            axis=0,
        )
        weighted = grid * jnp.concatenate([scale, scale], axis=1)
        image_side = mm(split(weighted), unit)
        sums = [None] * facet_count
        for w in range(planes):
            parts = []
            for k in range(facet_count):
                at = (k * planes + w) * part
                real = image_side[at : at + part, :width]
                imag = image_side[at : at + part, width:]
                tc, ts = twist[k]
                parts.append((real * tc + imag * ts, imag * tc - real * ts))
            for f, (real, imag) in enumerate(radix(parts, 1)):
                cols = slice(f * width, (f + 1) * width)
                kc, ks = kernels[w][0][:, cols], kernels[w][1][:, cols]
                term = (real * kc + imag * ks, imag * kc - real * ks)
                sums[f] = term if w == 0 else (sums[f][0] + term[0], sums[f][1] + term[1])
        for f in range(facet_count):
            back[h, f, :, :width] = sums[f][0]
            back[h, f, :, width:] = sums[f][1]
        for i, mate in enumerate(far_first):
            copy = pltpu.make_async_remote_copy(
                src_ref=back.at[h, mate],
                dst_ref=returned.at[h, facet],
                send_sem=bwd_send.at[h, i],
                recv_sem=bwd_recv.at[h, i],
                device_id={"facet": mate},
                device_id_type=MESH,
            )
            copy.start()
            backward.append(copy)
        returned[h, facet] = back[h, facet]
    for copy in backward:
        copy.wait()


def inverse_kernel(
    offsets_ref,
    returned,
    correction_ref,
    window_ref,
    unit_t_ref,
    pick_ref,
    turn_ref,
    outer_t_ref,
    out_ref,
    gain,
    segments,
    image,
    out_sem,
):
    halves, facet_count, part, double = returned.shape
    span = halves * part
    width = double // 2
    subs = offsets_ref.shape[0]
    low = pick_ref.shape[0]
    quads = width // low
    gain[pl.ds(0, low, stride=2), :] = correction_ref[...]
    gain[pl.ds(1, low, stride=2), :] = correction_ref[...]
    gains = gain[...]
    first_q, turn_cos, turn_sin, is_first, window_rows = offset_tables(
        offsets_ref, window_ref, quads
    )
    unturned = []
    for g in range(facet_count):
        whole = jnp.concatenate([returned[h, g] for h in range(halves)], axis=0)
        real, imag = whole[:, :width], whole[:, width:]
        unturned.append(
            jnp.concatenate(
                [real * turn_cos - imag * turn_sin, real * turn_sin + imag * turn_cos], axis=1
            )
        )
    unturned = jnp.concatenate(unturned, axis=0)
    mixed = mm(split(unturned), split(unit_t_ref[...]))
    win_first = jnp.where(is_first, window_rows, 0.0)
    win_second = jnp.where(is_first, 0.0, window_rows)
    for g in range(facet_count):
        cols = slice(g * width, (g + 1) * width)
        for c in range(2):
            part = mixed[g * span : (g + 1) * span, c * width : (c + 1) * width]
            for h, win in enumerate((win_first, win_second)):
                masked = part * win
                for s in range(subs):
                    at = (4 * s + 2 * h + c) * quads
                    segments[at : at + quads, cols] = masked[s * quads : (s + 1) * quads]
    picked = gather_pick(first_q, pick_ref)
    table_cos, table_sin = turn_ref[0], turn_ref[1]
    outer_t = split(outer_t_ref[...])
    share = 2 * width // quads
    pair_size = 2 if facet_count % 2 == 0 else 1
    stores = []
    for first in range(0, facet_count, pair_size):
        here = range(first, first + pair_size)
        columns = jnp.concatenate(
            [segments[:, g * width : (g + 1) * width].T for g in here], axis=0
        )
        fine = mm(split(columns), picked)
        reals, imags = [], []
        for g in range(pair_size):
            real = fine[g * width : (g + 1) * width, :width]
            imag = fine[g * width : (g + 1) * width, width:]
            reals.append(real * table_cos + imag * table_sin)
            imags.append(imag * table_cos - real * table_sin)
        joined = jnp.concatenate(
            [jnp.concatenate(reals, axis=1), jnp.concatenate(imags, axis=1)], axis=0
        )
        spread = mm(outer_t, split(joined))
        for j, g in enumerate(here):
            cols = slice(j * width, (j + 1) * width)
            blocks = [spread[i * share : (i + 1) * share, cols] for i in range(quads)]
            for i, block in enumerate(swap_blocks(blocks, low)):
                image[g * quads + i] = block * gains
            store = pltpu.make_async_copy(
                image.at[pl.ds(g * quads, quads)],
                out_ref.at[pl.ds(g * quads, quads)],
                out_sem.at[g],
            )
            store.start()
            stores.append(store)
    for store in stores:
        store.wait()


def on_device(facets, correction, window, offsets, phases, coverage):
    facet_count = lax.axis_size("facet")
    sub_count = lax.axis_size("sub")
    pair_count = lax.axis_size("wa")
    row_count, length = facets.shape[1], facets.shape[3]
    width = window.shape[0]
    subs = offsets.shape[0]
    rows = row_count // (sub_count * pair_count)
    low = length // width
    quads = width // low
    if rows != facet_count * quads or low * quads != width:
        raise ValueError("unsupported sizes")
    span = subs * quads
    total = facet_count * width
    lines = length // width
    image = facets.reshape(row_count, 2, lines, width)
    image = jnp.transpose(image, (0, 2, 1, 3)).reshape(row_count, 2 * lines, width)
    twist, outer, turn, pick, unit, unit_t, outer_t = tables(length, width, facet_count)
    vmem = pl.BlockSpec(memory_space=pltpu.VMEM)
    smem = pl.BlockSpec(memory_space=pltpu.SMEM)
    far = pl.BlockSpec(memory_space=pltpu.HBM)
    others = sub_count * pair_count - 1
    dma = pltpu.SemaphoreType.DMA
    halves = 2 if subs % 2 == 0 and (span // 2) % 8 == 0 else 1
    block = (halves, facet_count, span // halves, 2 * width)
    gains = correction.reshape(lines, width)
    pair_size = 2 if facet_count % 2 == 0 else 1
    held = coverage.shape[0] * coverage.shape[1]
    window = window.reshape(1, width)
    first_tables = [outer, turn, pick, unit, unit_t]
    returned = pl.pallas_call(
        functools.partial(kernel, (facet_count, sub_count, pair_count)),
        out_shape=pltpu.VMEM(block, F32),
        in_specs=[smem] + [far] * (6 + len(first_tables)),
        out_specs=vmem,
        scratch_shapes=[
            pltpu.VMEM((rows, 2 * lines, width), F32),
            pltpu.VMEM((2 * lines, width), F32),
            pltpu.VMEM((facet_count // pair_size, pair_size, span, 2 * width), F32),
            pltpu.VMEM((facet_count // pair_size, pair_size, span, 2 * width), F32),
            pltpu.VMEM((facet_count, span, 2 * width), F32),
            pltpu.VMEM(block, F32),
            pltpu.VMEM((held, total), F32),
            pltpu.VMEM((sub_count, pair_count, held, total), F32),
            pltpu.VMEM((coverage.shape[1] * pair_count * span, total), F32),
            pltpu.VMEM((pair_count,) + phases.shape, F32),
            dma((facet_count // pair_size,)),
            dma((facet_count - 1,)),
            dma((facet_count - 1,)),
            dma((halves, facet_count - 1)),
            dma((halves, facet_count - 1)),
            dma((others,)),
            dma((others,)),
            dma((max(pair_count - 1, 1),)),
            dma((max(pair_count - 1, 1),)),
        ]
        + [pltpu.VMEM(table.shape, F32) for table in first_tables]
        + [dma((len(first_tables),))]
        + [
            pltpu.VMEM(gains.shape, F32),
            pltpu.VMEM(window.shape, F32),
            pltpu.VMEM(phases.shape, F32),
            pltpu.VMEM(coverage.shape, jnp.int32),
            pltpu.VMEM(twist.shape, F32),
            dma((5,)),
        ],
        compiler_params=pltpu.CompilerParams(
            collective_id=0, has_side_effects=True, vmem_limit_bytes=55 * 1024 * 1024
        ),
    )(offsets, image, gains, window, phases, coverage, jnp.asarray(twist), *map(jnp.asarray, first_tables))
    second_tables = [unit_t, pick, turn, outer_t]
    result = pl.pallas_call(
        inverse_kernel,
        out_shape=jax.ShapeDtypeStruct((rows, 2 * lines, width), F32),
        in_specs=[smem] + [vmem] * (3 + len(second_tables)),
        out_specs=far,
        scratch_shapes=[
            pltpu.VMEM((2 * lines, width), F32),
            pltpu.VMEM((4 * span, total), F32),
            pltpu.VMEM((rows, 2 * lines, width), F32),
            dma((facet_count,)),
        ],
        compiler_params=pltpu.CompilerParams(vmem_limit_bytes=48 * 1024 * 1024),
    )(offsets, returned, gains, window, *map(jnp.asarray, second_tables))
    result = jnp.transpose(result.reshape(rows, lines, 2, width), (0, 2, 1, 3))
    return result.reshape(1, rows, 2, length)


def solution(mesh):
    return jax.shard_map(
        on_device,
        mesh=mesh,
        in_specs=(
            P("facet", None, None, None),
            P("facet", None),
            P(),
            P(),
            P("wa", None),
            P("sub", "wa", None),
        ),
        out_specs=P("facet", ("sub", "wa"), None, None),
        check_vma=False,
    )
```

```python
import functools
import math

import jax
import jax.numpy as jnp
import numpy as np
from jax import lax
from jax.experimental import pallas as pl
from jax.experimental.pallas import tpu as pltpu
from jax.sharding import PartitionSpec as P

MESH = pl.DeviceIdType.MESH
F32 = jnp.float32
BF16 = jnp.bfloat16


def complex_rows(matrix):
    return np.block([[matrix.real, matrix.imag], [-matrix.imag, matrix.real]])


def tables(length, width, facet_count):
    low = length // width
    quads = width // low
    a = np.arange(width)
    b = np.arange(low)
    dft = np.exp(-2j * np.pi * np.outer(a, a) / width)
    order = (a.reshape(width // quads, quads).T).reshape(-1)
    picked = dft[:, order]
    spread = np.zeros((2, width, width, 2))
    spread[0, :, :, 0] = picked.real
    spread[0, :, :, 1] = -picked.imag
    spread[1, :, :, 0] = picked.imag
    spread[1, :, :, 1] = picked.real
    outer = spread.reshape(2 * width, 2 * width)
    turn = np.tile(np.exp(-2j * np.pi * np.outer(a, b) / length), (1, quads))
    turn = np.stack([turn.real, turn.imag]).astype(np.float32)
    fine = np.exp(-2j * np.pi * np.outer(b, b) / low) * length**-0.5
    pick = np.zeros((low, 2, quads, 2, quads, low))
    for quad in range(quads):
        pick[:, 0, quad, 0, quad] = fine.real
        pick[:, 0, quad, 1, quad] = -fine.imag
        pick[:, 1, quad, 0, quad] = fine.imag
        pick[:, 1, quad, 1, quad] = fine.real
    pick = pick.reshape(low, 2 * quads, 2 * width).astype(np.float32)
    unit = complex_rows(np.conj(dft) * width**-0.5)
    twist = np.exp(-2j * np.pi * np.outer(np.arange(facet_count), a) / (facet_count * width))
    twist = np.stack([twist.real, twist.imag]).astype(np.float32)
    outer, unit = outer.astype(np.float32), unit.astype(np.float32)
    return twist, outer, turn, pick, unit, unit.T, outer.T


def split(value):
    high = value.astype(BF16)
    return high, (value - high.astype(F32)).astype(BF16)


def mm(left, right, transposed=False):
    axis = 1 if transposed else 0
    one = jnp.concatenate([left[0], left[0], left[1]], axis=1)
    two = jnp.concatenate([right[0], right[1], right[0]], axis=axis)
    return lax.dot_general(one, two, (((1,), (axis,)), ((), ())), preferred_element_type=F32)


def cos_sin(value):
    turns = jnp.floor(value * (2.0 / math.pi) + 0.5)
    rest = (value - turns * 1.5703125) - turns * (math.pi / 2 - 1.5703125)
    square = rest * rest
    sine = rest + rest * square * (
        -1.0 / 6 + square * (1.0 / 120 + square * (-1.0 / 5040 + square * (1.0 / 362880)))
    )
    cosine = 1.0 + square * (
        -0.5 + square * (1.0 / 24 + square * (-1.0 / 720 + square * (1.0 / 40320)))
    )
    odd = jnp.abs(turns) == 1.0
    sign_cos = jnp.where(turns == 1.0, -1.0, jnp.where(jnp.abs(turns) == 2.0, -1.0, 1.0))
    sign_sin = jnp.where(turns == -1.0, -1.0, jnp.where(jnp.abs(turns) == 2.0, -1.0, 1.0))
    return jnp.where(odd, sine, cosine) * sign_cos, jnp.where(odd, cosine, sine) * sign_sin


def radix(parts, sign):
    count = len(parts)
    if count == 1:
        return parts
    if count % 2:
        raise ValueError("odd length")
    even = radix(parts[0::2], sign)
    odd = radix(parts[1::2], sign)
    first, second = [], []
    for k in range(count // 2):
        real, imag = odd[k]
        if 4 * k == count:
            real, imag = (-imag, real) if sign > 0 else (imag, -real)
        elif k:
            c = math.cos(2 * math.pi * k / count)
            s = sign * math.sin(2 * math.pi * k / count)
            real, imag = real * c - imag * s, real * s + imag * c
        first.append((even[k][0] + real, even[k][1] + imag))
        second.append((even[k][0] - real, even[k][1] - imag))
    return first + second


def swap_blocks(blocks, low):
    blocks = list(blocks)
    count = len(blocks)
    width = count * low
    lane = lax.broadcasted_iota(jnp.int32, blocks[0].shape, 1)
    step = count // 2
    while step:
        shift = step * low
        upper = (lane & shift) != 0
        for i in range(count):
            if i & step:
                continue
            one, two = blocks[i], blocks[i + step]
            blocks[i] = jnp.where(upper, pltpu.roll(two, shift, 1), one)
            blocks[i + step] = jnp.where(upper, two, pltpu.roll(one, width - shift, 1))
        step //= 2
    return blocks


def offset_tables(offsets_ref, window_ref, quads):
    width = window_ref.shape[1]
    subs = offsets_ref.shape[0]
    span = subs * quads
    starts = [offsets_ref[s] for s in range(subs)]
    first_q = [start // width for start in starts]
    rests = [start & (width - 1) for start in starts]
    row = lax.broadcasted_iota(jnp.int32, (span, width), 0)
    offset_rows = jnp.zeros((span, width), jnp.int32)
    window_full = jnp.broadcast_to(window_ref[...], (8, width))
    window_rows = jnp.zeros((span, width), F32)
    for s in range(subs):
        offset_rows = jnp.where(row >= s * quads, rests[s], offset_rows)
        moved = pltpu.roll(window_full, rests[s], 1)[0:1]
        window_rows = jnp.where(row >= s * quads, moved, window_rows)
    span_lane = lax.broadcasted_iota(jnp.int32, (span, width), 1)
    steps = ((offset_rows * span_lane + width // 2) & (width - 1)) - width // 2
    turn_cos, turn_sin = cos_sin(steps.astype(F32) * (2.0 * math.pi / width))
    return first_q, turn_cos, turn_sin, span_lane >= offset_rows, window_rows


def gather_pick(first_q, pick_ref):
    low = pick_ref.shape[0]
    picked = []
    for q in first_q:
        picked.append(pick_ref[q])
        picked.append(pick_ref[lax.rem(q + 1, low)])
    return split(jnp.concatenate(picked, axis=0))


def kernel(
    geometry,
    offsets_ref,
    facets_ref,
    correction_ref,
    window_ref,
    phases_ref,
    coverage_ref,
    twist_ref,
    outer_far,
    turn_far,
    pick_far,
    unit_far,
    unit_t_far,
    segments,
    image,
    gain,
    cut,
    sent,
    arrived,
    back,
    returned,
    ordered,
    counts,
    expanded,
    screens,
    load_sem,
    fwd_send,
    fwd_recv,
    bwd_send,
    bwd_recv,
    cov_send,
    cov_recv,
    ph_send,
    ph_recv,
    outer_ref,
    turn_ref,
    pick_ref,
    unit_ref,
    unit_t_ref,
    table_sem,
):
    facet_count, sub_count, pair_count = geometry
    facet = lax.axis_index("facet")
    sub = lax.axis_index("sub")
    pair = lax.axis_index("wa")
    rows = image.shape[0]
    width = window_ref.shape[1]
    subs = offsets_ref.shape[0]
    low = pick_ref.shape[0]
    quads = width // low
    length = low * width
    span = subs * quads
    per_sub, per_wa = coverage_ref.shape[0], coverage_ref.shape[1]
    planes = per_wa * pair_count
    total = facet_count * width

    facet_mates = [lax.rem(facet + d, facet_count) for d in range(1, facet_count)]
    hops = [(ds, dw) for ds in range(sub_count) for dw in range(pair_count) if ds or dw]
    barrier = pltpu.get_barrier_semaphore()
    for mate in facet_mates:
        pl.semaphore_signal(barrier, inc=1, device_id={"facet": mate}, device_id_type=MESH)
    grid_mates = [(lax.rem(sub + ds, sub_count), lax.rem(pair + dw, pair_count)) for ds, dw in hops]
    for mate_sub, mate_pair in grid_mates:
        pl.semaphore_signal(
            barrier, inc=1, device_id={"sub": mate_sub, "wa": mate_pair}, device_id_type=MESH
        )
    pair_size = 2 if facet_count % 2 == 0 else 1
    pairs = facet_count // pair_size
    order = [lax.rem(facet // pair_size + 1 + step, pairs) for step in range(pairs)]
    slots = [
        order[step] * pair_size + lax.rem(facet + g, pair_size)
        for step in range(pairs - 1)
        for g in range(pair_size)
    ]
    near = order[-1] * pair_size
    far_first = slots + [near + lax.rem(facet + 1 + g, pair_size) for g in range(pair_size - 1)]
    batch = pair_size * quads
    first_row = (sub * pair_count + pair) * rows
    loads = []
    for step, which in enumerate(order):
        load = pltpu.make_async_copy(
            facets_ref.at[pl.ds(first_row + which * batch, batch)],
            image.at[pl.ds(step * batch, batch)],
            load_sem.at[step],
        )
        load.start()
        loads.append(load)
    fetches = {}
    for i, (name, far, near) in enumerate(
        (
            ("outer", outer_far, outer_ref),
            ("turn", turn_far, turn_ref),
            ("pick", pick_far, pick_ref),
            ("unit", unit_far, unit_ref),
            ("unit_t", unit_t_far, unit_t_ref),
        )
    ):
        fetches[name] = pltpu.make_async_copy(far, near, table_sem.at[i])
        fetches[name].start()

    def gathers():
        copies = []
        for i, (mate_sub, mate_pair) in enumerate(grid_mates):
            copies.append(
                pltpu.make_async_remote_copy(
                    src_ref=ordered,
                    dst_ref=counts.at[sub, pair],
                    send_sem=cov_send.at[i],
                    recv_sem=cov_recv.at[i],
                    device_id={"sub": mate_sub, "wa": mate_pair},
                    device_id_type=MESH,
                )
            )
        for d in range(1, pair_count):
            copies.append(
                pltpu.make_async_remote_copy(
                    src_ref=phases_ref,
                    dst_ref=screens.at[pair],
                    send_sem=ph_send.at[d - 1],
                    recv_sem=ph_recv.at[d - 1],
                    device_id={"wa": lax.rem(pair + d, pair_count)},
                    device_id_type=MESH,
                )
            )
        return copies

    def greet():
        pl.semaphore_wait(barrier, len(facet_mates) + len(hops))
        for copy in gathers():
            copy.start()

    source = lax.broadcasted_iota(jnp.int32, (width, width), 0)
    target = lax.broadcasted_iota(jnp.int32, (1, width), 1)
    fold = width // facet_count
    wanted = (target & (fold - 1)) * facet_count + target // fold
    chooser = jnp.where(source == wanted, 1.0, 0.0).astype(BF16)
    own = jnp.concatenate([coverage_ref[i].astype(F32) for i in range(per_sub)], axis=0)
    held = per_sub * per_wa
    own = jnp.concatenate([own[:, k * width : (k + 1) * width] for k in range(facet_count)], axis=0)
    own = jnp.dot(own.astype(BF16), chooser, preferred_element_type=F32)
    own = own * (1.0 / (facet_count * planes))
    own = [own[k * held : (k + 1) * held] for k in range(facet_count)]
    for k, block in enumerate(swap_blocks(own, fold)):
        ordered[:, k * width : (k + 1) * width] = block
    counts[sub, pair] = ordered[...]
    screens[pair] = phases_ref[...]
    pl.when((sub != 0) & (sub == sub_count - 1))(greet)

    gain[pl.ds(0, low, stride=2), :] = correction_ref[...]
    gain[pl.ds(1, low, stride=2), :] = correction_ref[...]
    first_q, turn_cos, turn_sin, is_first, window_rows = offset_tables(
        offsets_ref, window_ref, quads
    )
    fetches["pick"].wait()
    picked = gather_pick(first_q, pick_ref)

    gains = gain[...]
    fetches["outer"].wait()
    outer = split(outer_ref[...])
    fetches["turn"].wait()
    table_cos, table_sin = turn_ref[0], turn_ref[1]
    fetches["unit"].wait()
    unit = split(unit_ref[...])
    forward = []
    for step in range(pairs):
        loads[step].wait()
        groups = []
        for g in range(pair_size):
            at = step * batch + g * quads
            blocks = [image[at + i] * gains for i in range(quads)]
            groups.append(jnp.concatenate(swap_blocks(blocks, low), axis=0))
        spread = jnp.concatenate(groups, axis=1)
        mixed = mm(outer, split(spread))
        if step == 0:
            pl.when((sub != 0) & (sub != sub_count - 1))(greet)
        turned = []
        for g in range(pair_size):
            real = mixed[:width, g * width : (g + 1) * width]
            imag = mixed[width:, g * width : (g + 1) * width]
            turned.append(
                jnp.concatenate(
                    [real * table_cos - imag * table_sin, real * table_sin + imag * table_cos],
                    axis=1,
                )
            )
        turned = jnp.concatenate(turned, axis=0)
        spectrum = mm(picked, split(turned), transposed=True)
        for s in range(subs):
            here = slice(s * quads, (s + 1) * quads)
            base = s * 4 * quads
            keep = is_first[here]
            win = window_rows[here]
            for g in range(pair_size):
                cols = slice(g * width, (g + 1) * width)
                for c in range(2):
                    one = spectrum[base + c * quads : base + (c + 1) * quads, cols]
                    two = spectrum[base + (2 + c) * quads : base + (3 + c) * quads, cols]
                    cut[step, g, here, c * width : (c + 1) * width] = (
                        jnp.where(keep, one, two) * win
                    )
        mixed = mm(split(cut[step].reshape(pair_size * span, 2 * width)), unit)
        for g in range(pair_size):
            real = mixed[g * span : (g + 1) * span, :width]
            imag = mixed[g * span : (g + 1) * span, width:]
            sent[step, g, :, :width] = real * turn_cos + imag * turn_sin
            sent[step, g, :, width:] = imag * turn_cos - real * turn_sin
        if step == 0:
            pl.when(sub == 0)(greet)
        for g in range(pair_size):
            if step < pairs - 1:
                slot = lax.rem(facet + g, pair_size)
                mate = order[step] * pair_size + slot
            elif g < pair_size - 1:
                slot = lax.rem(facet + 1 + g, pair_size)
                mate = order[step] * pair_size + slot
            else:
                continue
            copy = pltpu.make_async_remote_copy(
                src_ref=sent.at[step, slot],
                dst_ref=arrived.at[facet],
                send_sem=fwd_send.at[step * pair_size + g],
                recv_sem=fwd_recv.at[step * pair_size + g],
                device_id={"facet": mate},
                device_id_type=MESH,
            )
            copy.start()
            forward.append(copy)
    arrived[facet] = sent[pairs - 1, lax.rem(facet, pair_size)]
    fetches["unit_t"].wait()
    unit_t = split(unit_t_ref[...])

    arrivals = gathers()
    for copy in arrivals[len(hops) :]:
        copy.wait()
    kernels = []
    for p in range(pair_count):
        screen = screens[p]
        cos_all, sin_all = cos_sin(screen)
        for j in range(per_wa):
            kernels.append((cos_all[j : j + 1], sin_all[j : j + 1]))
    twist = [(twist_ref[0, k : k + 1], twist_ref[1, k : k + 1]) for k in range(facet_count)]

    backward = []
    halves, part = back.shape[0], back.shape[2]
    for copy in forward:
        copy.wait()
    for h in range(halves):
        pieces = [[] for _ in range(facet_count)]
        for w in range(planes):
            parts = []
            for f in range(facet_count):
                cols = slice(f * width, (f + 1) * width)
                kc, ks = kernels[w][0][:, cols], kernels[w][1][:, cols]
                both = arrived[f, h * part : (h + 1) * part, :]
                real, imag = both[:, :width], both[:, width:]
                parts.append((real * kc - imag * ks, real * ks + imag * kc))
            for k, (real, imag) in enumerate(radix(parts, -1)):
                tc, ts = twist[k]
                pieces[k].append(
                    jnp.concatenate([real * tc - imag * ts, real * ts + imag * tc], axis=1)
                )
        stacked = jnp.concatenate([piece for group in pieces for piece in group], axis=0)
        grid = mm(split(stacked), unit_t)
        if h == 0:
            for copy in arrivals[: len(hops)]:
                copy.wait()
            for owner in range(sub_count):
                for p in range(pair_count):
                    for i in range(per_sub):
                        for j in range(per_wa):
                            at = (p * per_wa + j) * span + (owner * per_sub + i) * quads
                            row = counts[owner, p, i * per_wa + j : i * per_wa + j + 1]
                            expanded[at : at + quads, :] = jnp.broadcast_to(row, (quads, total))
        scale = jnp.concatenate(
            [
                expanded[w * span + h * part : w * span + (h + 1) * part, k * width : (k + 1) * width]
                for k in range(facet_count)
                for w in range(planes)
            ],
            axis=0,
        )
        weighted = grid * jnp.concatenate([scale, scale], axis=1)
        image_side = mm(split(weighted), unit)
        sums = [None] * facet_count
        for w in range(planes):
            parts = []
            for k in range(facet_count):
                at = (k * planes + w) * part
                real = image_side[at : at + part, :width]
                imag = image_side[at : at + part, width:]
                tc, ts = twist[k]
                parts.append((real * tc + imag * ts, imag * tc - real * ts))
            for f, (real, imag) in enumerate(radix(parts, 1)):
                cols = slice(f * width, (f + 1) * width)
                kc, ks = kernels[w][0][:, cols], kernels[w][1][:, cols]
                term = (real * kc + imag * ks, imag * kc - real * ks)
                sums[f] = term if w == 0 else (sums[f][0] + term[0], sums[f][1] + term[1])
        for f in range(facet_count):
            back[h, f, :, :width] = sums[f][0]
            back[h, f, :, width:] = sums[f][1]
        copies = []
        for i, mate in enumerate(far_first):
            copy = pltpu.make_async_remote_copy(
                src_ref=back.at[h, mate],
                dst_ref=returned.at[h, facet],
                send_sem=bwd_send.at[h, i],
                recv_sem=bwd_recv.at[h, i],
                device_id={"facet": mate},
                device_id_type=MESH,
            )
            copy.start()
            copies.append(copy)
        backward.append(copies)
        returned[h, facet] = back[h, facet]
    win_first = jnp.where(is_first, window_rows, 0.0)
    win_second = jnp.where(is_first, 0.0, window_rows)
    for h in range(halves):
        for copy in backward[h]:
            copy.wait()
        rows_h = slice(h * part, (h + 1) * part)
        tc, ts = turn_cos[rows_h], turn_sin[rows_h]
        unturned = []
        for g in range(facet_count):
            real, imag = returned[h, g, :, :width], returned[h, g, :, width:]
            unturned.append(
                jnp.concatenate([real * tc - imag * ts, real * ts + imag * tc], axis=1)
            )
        mixed = mm(split(jnp.concatenate(unturned, axis=0)), unit_t)
        for g in range(facet_count):
            cols = slice(g * width, (g + 1) * width)
            for c in range(2):
                piece = mixed[g * part : (g + 1) * part, c * width : (c + 1) * width]
                for band, win in enumerate((win_first, win_second)):
                    masked = piece * win[rows_h]
                    for s in range(part // quads):
                        at = (4 * (h * (part // quads) + s) + 2 * band + c) * quads
                        segments[at : at + quads, cols] = masked[s * quads : (s + 1) * quads]


def inverse_kernel(
    offsets_ref,
    segments,
    correction_ref,
    pick_ref,
    turn_ref,
    outer_t_ref,
    out_ref,
    gain,
    image,
    out_sem,
):
    width = correction_ref.shape[1]
    facet_count = segments.shape[1] // width
    low = pick_ref.shape[0]
    quads = width // low
    gain[pl.ds(0, low, stride=2), :] = correction_ref[...]
    gain[pl.ds(1, low, stride=2), :] = correction_ref[...]
    gains = gain[...]
    first_q = [offsets_ref[s] // width for s in range(offsets_ref.shape[0])]
    picked = gather_pick(first_q, pick_ref)
    table_cos, table_sin = turn_ref[0], turn_ref[1]
    outer_t = split(outer_t_ref[...])
    share = 2 * width // quads
    pair_size = 2 if facet_count % 2 == 0 else 1
    stores = []
    for first in range(0, facet_count, pair_size):
        here = range(first, first + pair_size)
        columns = jnp.concatenate(
            [segments[:, g * width : (g + 1) * width].T for g in here], axis=0
        )
        fine = mm(split(columns), picked)
        reals, imags = [], []
        for g in range(pair_size):
            real = fine[g * width : (g + 1) * width, :width]
            imag = fine[g * width : (g + 1) * width, width:]
            reals.append(real * table_cos + imag * table_sin)
            imags.append(imag * table_cos - real * table_sin)
        joined = jnp.concatenate(
            [jnp.concatenate(reals, axis=1), jnp.concatenate(imags, axis=1)], axis=0
        )
        spread = mm(outer_t, split(joined))
        for j, g in enumerate(here):
            cols = slice(j * width, (j + 1) * width)
            blocks = [spread[i * share : (i + 1) * share, cols] for i in range(quads)]
            for i, block in enumerate(swap_blocks(blocks, low)):
                image[g * quads + i] = block * gains
            store = pltpu.make_async_copy(
                image.at[pl.ds(g * quads, quads)],
                out_ref.at[pl.ds(g * quads, quads)],
                out_sem.at[g],
            )
            store.start()
            stores.append(store)
    for store in stores:
        store.wait()


def on_device(facets, correction, window, offsets, phases, coverage):
    facet_count = lax.axis_size("facet")
    sub_count = lax.axis_size("sub")
    pair_count = lax.axis_size("wa")
    row_count, length = facets.shape[1], facets.shape[3]
    width = window.shape[0]
    subs = offsets.shape[0]
    rows = row_count // (sub_count * pair_count)
    low = length // width
    quads = width // low
    if rows != facet_count * quads or low * quads != width:
        raise ValueError("unsupported sizes")
    span = subs * quads
    total = facet_count * width
    lines = length // width
    image = facets.reshape(row_count, 2, lines, width)
    image = jnp.transpose(image, (0, 2, 1, 3)).reshape(row_count, 2 * lines, width)
    twist, outer, turn, pick, unit, unit_t, outer_t = tables(length, width, facet_count)
    vmem = pl.BlockSpec(memory_space=pltpu.VMEM)
    smem = pl.BlockSpec(memory_space=pltpu.SMEM)
    far = pl.BlockSpec(memory_space=pltpu.HBM)
    others = sub_count * pair_count - 1
    dma = pltpu.SemaphoreType.DMA
    halves = 2 if subs % 2 == 0 and (span // 2) % 8 == 0 else 1
    block = (halves, facet_count, span // halves, 2 * width)
    gains = correction.reshape(lines, width)
    pair_size = 2 if facet_count % 2 == 0 else 1
    held = coverage.shape[0] * coverage.shape[1]
    window = window.reshape(1, width)
    first_tables = [outer, turn, pick, unit, unit_t]
    segments = pl.pallas_call(
        functools.partial(kernel, (facet_count, sub_count, pair_count)),
        out_shape=pltpu.VMEM((4 * span, total), F32),
        in_specs=[smem, far] + [vmem] * 5 + [far] * len(first_tables),
        out_specs=vmem,
        scratch_shapes=[
            pltpu.VMEM((rows, 2 * lines, width), F32),
            pltpu.VMEM((2 * lines, width), F32),
            pltpu.VMEM((facet_count // pair_size, pair_size, span, 2 * width), F32),
            pltpu.VMEM((facet_count // pair_size, pair_size, span, 2 * width), F32),
            pltpu.VMEM((facet_count, span, 2 * width), F32),
            pltpu.VMEM(block, F32),
            pltpu.VMEM(block, F32),
            pltpu.VMEM((held, total), F32),
            pltpu.VMEM((sub_count, pair_count, held, total), F32),
            pltpu.VMEM((coverage.shape[1] * pair_count * span, total), F32),
            pltpu.VMEM((pair_count,) + phases.shape, F32),
            dma((facet_count // pair_size,)),
            dma((facet_count - 1,)),
            dma((facet_count - 1,)),
            dma((halves, facet_count - 1)),
            dma((halves, facet_count - 1)),
            dma((others,)),
            dma((others,)),
            dma((max(pair_count - 1, 1),)),
            dma((max(pair_count - 1, 1),)),
        ]
        + [pltpu.VMEM(table.shape, F32) for table in first_tables]
        + [dma((len(first_tables),))],
        compiler_params=pltpu.CompilerParams(
            collective_id=0, has_side_effects=True, vmem_limit_bytes=55 * 1024 * 1024
        ),
    )(offsets, image, gains, window, phases, coverage, jnp.asarray(twist), *map(jnp.asarray, first_tables))
    second_tables = [pick, turn, outer_t]
    result = pl.pallas_call(
        inverse_kernel,
        out_shape=jax.ShapeDtypeStruct((rows, 2 * lines, width), F32),
        in_specs=[smem] + [vmem] * (2 + len(second_tables)),
        out_specs=far,
        scratch_shapes=[
            pltpu.VMEM((2 * lines, width), F32),
            pltpu.VMEM((rows, 2 * lines, width), F32),
            dma((facet_count,)),
        ],
        compiler_params=pltpu.CompilerParams(vmem_limit_bytes=48 * 1024 * 1024),
    )(offsets, segments, gains, *map(jnp.asarray, second_tables))
    result = jnp.transpose(result.reshape(rows, lines, 2, width), (0, 2, 1, 3))
    return result.reshape(1, rows, 2, length)


def solution(mesh):
    return jax.shard_map(
        on_device,
        mesh=mesh,
        in_specs=(
            P("facet", None, None, None),
            P("facet", None),
            P(),
            P(),
            P("wa", None),
            P("sub", "wa", None),
        ),
        out_specs=P("facet", ("sub", "wa"), None, None),
        check_vma=False,
    )
```
